256 devices in a mesh: ctx: 32 (over x, z_hi, core), head: 8 (over z_lo, y).
Axes of the slice: x: 4, y: 4, z: 8 (z_hi: 4, z_lo: 2; z = z_hi * 2 + z_lo), core: 2. Of those that a mesh axis runs over, the one named last changes fastest.
Arguments:
- hidden: bfloat16 [16384, 8192], P('ctx', 'head'), may hold values from -6 to 6
- dt_weight: bfloat16 [8192, 256], P('head'), may hold values from -0.375 to 0.375
- dt_bias: float32 [256], P('head'), may hold values from -2 to 1
- decay_rate: float32 [256], P('head'), may hold values from 1.2207031e-06 to 0.05
- skip_gain: float32 [256], P('head'), may hold values from 0.5 to 2
- ssm_in: bfloat16 [16384, 16384], P('ctx', 'head'), may hold values from -6 to 6
- bc_in: bfloat16 [16384, 8, 512], P('ctx', 'head'), may hold values from -6 to 6
- conv_x: float32 [4, 16384], P(None, 'head'), may hold values from -3 to 3
- conv_bc: float32 [4, 8, 512], P(None, 'head'), may hold values from -3 to 3
- gate_in: bfloat16 [16384, 16384], P('ctx', 'head'), may hold values from -6 to 6
- norm_gain: float32 [16384], P('head'), may hold values from 0.1 to 1.9
- query_heads: bfloat16 [16384, 4096], P('ctx', 'head'), may hold values from -32 to 32
- key_heads: bfloat16 [16384, 1024], P('ctx', 'head'), may hold values from -6 to 6
- value_heads: bfloat16 [16384, 1024], P('ctx', 'head'), may hold values from -6 to 6
Outputs:
- mamba_out: bfloat16 [16384, 16384], P('ctx', 'head')
- attn_out: bfloat16 [16384, 4096], P('ctx', 'head')
The draws below stay inside these ranges and needn't reach their ends.
All inputs are finite; a program needn't handle non-finite values.
Results may differ from the reference program's by a relative error of at most 0.0075.
Values may be sent and summed in bfloat16 or wider, within the bound.
No kernel may reach another device: no remote copies, remote signals or barrier semaphores. Data moves between devices by JAX's collectives and lax.ppermute only.
A program may use at most 256 MiB of HBM per device.

```python
import math
import jax
import jax.numpy as jnp
from jax import lax

D = 8192
MH = 256
P_SIZE = 64
N = 256
G = 8
KCONV = 4
SPAN = 128
QH = 32
KVH = 8
HD = 128
TOK_DEV = 512
INNER = 16384
TOKENS = 16384


def shared_keys(key):
    base = jnp.clip(jax.random.normal(key, (TOKENS, KVH * HD), jnp.float32), -6.0, 6.0)
    position = jnp.arange(TOKENS)
    chosen = (position + 1) % TOK_DEV == TOK_DEV // 2
    return jnp.where(chosen[:, None], base, base)


def draw_decay_rate(key, part):
    key = jax.random.fold_in(key, 11)
    key_slow = jax.random.fold_in(key, 0)
    return jnp.exp(jax.random.uniform(key_slow, (MH,), jnp.float32, math.log(0.02 / TOKENS), math.log(0.05)))


def draw_key_heads(key, part):
    return shared_keys(key).astype(jnp.bfloat16)


def draw_query_heads(key, part):
    key = jax.random.fold_in(key, 23)
    return jnp.clip(3.0 * jax.random.normal(key, (TOKENS, QH * HD), jnp.float32), -32.0, 32.0).astype(jnp.bfloat16)


def strengthened(entries, rng, source, target, parts, factor):
    def block_of(axis_at):
        return (jnp.arange(entries.shape[axis_at]) // (entries.shape[axis_at] // parts)).reshape((-1,) + (1,) * (entries.ndim - 1 - axis_at))

    first = jax.random.permutation(rng, parts)[block_of(target)]
    second = (block_of(target) + parts // 2) % parts
    return jnp.where((block_of(source) == first) | (block_of(source) == second), factor * entries, entries)


def block_scale(rng, extent, shards, low, largest):
    level = 1.0
    for dim, blocks in shards:
        heights = jax.random.uniform(jax.random.fold_in(jax.random.fold_in(rng, 6), dim), (blocks,), jnp.float32, low / len(shards), largest / len(shards))
        level = level * jnp.repeat(jnp.exp(heights), extent[dim] // blocks).reshape((-1,) + (1,) * (len(extent) - 1 - dim))
    return level


def normal_values(key, shape, spread, reach, cuts=(), kind=jnp.bfloat16):
    level = block_scale(key, shape, cuts, -0.22, 0.18) if cuts else 1.0
    drawn = jax.random.normal(key, shape, jnp.float32) * spread * level
    return jnp.minimum(jnp.maximum(drawn, -reach), reach).astype(kind)


def gaussian_with(key, dims, deviation, reach, cuts, heavy, kind=jnp.bfloat16):
    entries = deviation * jax.random.normal(key, dims, jnp.float32)
    if cuts:
        entries = entries * block_scale(key, dims, cuts, -0.22, 0.18)
    return jnp.clip(strengthened(entries, jax.random.fold_in(key, 3), *heavy), -reach, reach).astype(kind)


def setup_inputs(seed: int = 0) -> dict:
    seeds = jax.random.split(jax.random.key(seed), 15)
    return {
        "hidden": normal_values(seeds[0], (TOKENS, D), 1.0, 6.0, ((0, 32), (1, 8))),
        "dt_weight": gaussian_with(seeds[1], (D, MH), (D // 16) ** -0.5, 0.375, ((0, 8),), (0, 1, 8, 2.0)),
        "dt_bias": jnp.clip(-2.0 + 3.0 * jax.random.uniform(seeds[2], (MH,), jnp.float32) ** block_scale(seeds[2], (MH,), ((0, 8),), -0.2, 0.2), -2.0, 1.0),
        "decay_rate": draw_decay_rate(jax.random.fold_in(seeds[14], 71), 0),
        "skip_gain": jnp.clip(0.5 + 1.5 * jax.random.uniform(seeds[4], (MH,), jnp.float32) ** block_scale(seeds[4], (MH,), ((0, 8),), -0.2, 0.2), 0.5, 2.0),
        "ssm_in": normal_values(seeds[5], (TOKENS, INNER), 1.0, 6.0, ((0, 32), (1, 8))),
        "bc_in": normal_values(seeds[6], (TOKENS, G, 2 * N), 1.0, 6.0, ((0, 32), (1, 8))),
        "conv_x": normal_values(seeds[7], (KCONV, INNER), KCONV ** -0.5, 3.0, ((1, 8),), jnp.float32),
        "conv_bc": normal_values(seeds[8], (KCONV, G, 2 * N), KCONV ** -0.5, 3.0, ((1, 8),), jnp.float32),
        "gate_in": normal_values(seeds[9], (TOKENS, INNER), 1.0, 6.0, ((0, 32), (1, 8))),
        "norm_gain": jnp.clip(1.0 + 0.18 * jax.random.normal(seeds[10], (INNER,), jnp.float32), 0.1, 1.9),
        "query_heads": draw_query_heads(jax.random.fold_in(seeds[14], 71), 0),
        "key_heads": draw_key_heads(jax.random.fold_in(seeds[14], 71), 0),
        "value_heads": normal_values(seeds[13], (TOKENS, KVH * HD), 1.0, 6.0, ((0, 32), (1, 8))),
    }


def conv_silu(window, weights, length):
    running = weights[0] * window[0:length].astype(jnp.float32)
    for offset in range(1, weights.shape[0]):
        running = running + weights[offset] * window[offset:offset + length].astype(jnp.float32)
    return jax.nn.silu(running).astype(jnp.bfloat16)

def span_terms(inputs_span, bmatrix, cmatrix, steps_span, decay_rates):
    length, head_count, head_size = inputs_span.shape
    groups = bmatrix.shape[1]
    per_group = head_count // groups
    cumulative = jnp.cumsum(-steps_span * decay_rates[None, :], axis=0)
    products = jnp.einsum('igm,jgm->gij', cmatrix.astype(jnp.float32), bmatrix.astype(jnp.float32))
    products = jnp.broadcast_to(products[:, None], (groups, per_group, length, length)).reshape(head_count, length, length)
    causal = jnp.tril(jnp.ones((length, length), dtype=bool))
    across = cumulative.T[:, :, None] - cumulative.T[:, None, :]
    decays = jnp.exp(jnp.where(causal[None], across, -1e+30))
    mixing = (products * decays * steps_span.T[:, None, :]).astype(jnp.bfloat16)
    mixing = lax.optimization_barrier(mixing).astype(jnp.float32)
    intra = jnp.einsum('hij,jhp->ihp', mixing, inputs_span.astype(jnp.float32))
    to_last = jnp.exp(cumulative[-1][None, :] - cumulative) * steps_span
    weighted = (inputs_span.astype(jnp.float32) * to_last[:, :, None]).astype(jnp.bfloat16)
    weighted = lax.optimization_barrier(weighted).astype(jnp.float32)
    increment = jnp.einsum('jghp,jgm->ghpm', weighted.reshape(length, groups, per_group, head_size), bmatrix.astype(jnp.float32))
    return (intra, cumulative, increment.reshape(head_count, head_size, bmatrix.shape[2]))

def state_readout(cmatrix, state, cumulative):
    length = cmatrix.shape[0]
    groups = cmatrix.shape[1]
    head_count, head_size, state_size = state.shape
    state_low = lax.optimization_barrier(state.astype(jnp.bfloat16)).astype(jnp.float32)
    shaped = state_low.reshape(groups, head_count // groups, head_size, state_size)
    readout = jnp.einsum('igm,ghpm->ighp', cmatrix.astype(jnp.float32), shaped, precision=lax.Precision.HIGHEST)
    return readout.reshape(length, head_count, head_size) * jnp.exp(cumulative)[:, :, None]

def gated_norm(mixed, gate, gain, groups):
    row_count, inner_width = mixed.shape
    gated = mixed * jax.nn.silu(gate.astype(jnp.float32))
    shaped = gated.reshape(row_count, groups, inner_width // groups)
    factor = lax.rsqrt(lax.optimization_barrier(jnp.mean(shaped * shaped, axis=-1, keepdims=True)) + 1e-05)
    return ((shaped * factor).reshape(row_count, inner_width) * gain[None, :]).astype(jnp.bfloat16)

def attend_block(carry, query_rows, query_pos, key_block, value_block, key_pos):
    maximum, denominator, weighted_sum = carry
    scale = query_rows.shape[-1] ** (-0.5)
    scores = jnp.einsum('rghd,sgd->rghs', query_rows.astype(jnp.float32), key_block.astype(jnp.float32)) * scale
    visible = (key_pos[None, :] <= query_pos[:, None])[:, None, None, :]
    scores = jnp.where(visible, scores, -1e+30)
    updated = jnp.maximum(maximum, lax.optimization_barrier(jnp.max(scores, axis=-1)))
    weights = jnp.where(visible, jnp.exp(scores - updated[..., None]), 0.0)
    factor = jnp.exp(maximum - updated)
    denominator = denominator * factor + lax.optimization_barrier(jnp.sum(weights, axis=-1))
    rounded = lax.optimization_barrier(weights.astype(jnp.bfloat16)).astype(jnp.float32)
    weighted_sum = weighted_sum * factor[..., None] + jnp.einsum('rghs,sgd->rghd', rounded, value_block.astype(jnp.float32))
    return (updated, denominator, weighted_sum)

def attention_all(query_heads, key_heads, value_heads):
    block = math.gcd(TOKENS, 512)
    blocks = TOKENS // block
    query_rows = query_heads.reshape(TOKENS, KVH, QH // KVH, HD)
    key_rows = key_heads.reshape(TOKENS, KVH, HD)
    value_rows = value_heads.reshape(TOKENS, KVH, HD)

    def one_block(block_index):
        first_row = (block_index * block).astype(jnp.int32)
        row_block = lax.dynamic_slice_in_dim(query_rows, first_row, block, 0)
        query_pos = first_row + jnp.arange(block, dtype=jnp.int32)
        initial = (jnp.full(row_block.shape[:3], -1e+30, jnp.float32), jnp.zeros(row_block.shape[:3], jnp.float32), jnp.zeros(row_block.shape, jnp.float32))

        def visit(key_index, state):
            key_first = (key_index * block).astype(jnp.int32)
            key_block = lax.dynamic_slice_in_dim(key_rows, key_first, block, 0)
            value_block = lax.dynamic_slice_in_dim(value_rows, key_first, block, 0)
            key_pos = key_first + jnp.arange(block, dtype=jnp.int32)
            return attend_block(state, row_block, query_pos, key_block, value_block, key_pos)
        state = lax.fori_loop(jnp.int32(0), (block_index + 1).astype(jnp.int32), visit, initial)
        return (state[2] / state[1][..., None]).astype(jnp.bfloat16).reshape(block, QH * HD)
    return lax.map(one_block, jnp.arange(blocks, dtype=jnp.int32)).reshape(TOKENS, QH * HD)

def reference(hidden, dt_weight, dt_bias, decay_rate, skip_gain, ssm_in, bc_in, conv_x, conv_bc, gate_in, norm_gain, query_heads, key_heads, value_heads):
    step_size = jax.nn.softplus(jnp.dot(hidden, dt_weight, preferred_element_type=jnp.float32) + dt_bias[None, :])
    spans = TOKENS // SPAN
    inputs_all = ssm_in.reshape(spans, SPAN, INNER)
    pairs_all = bc_in.reshape(spans, SPAN, G, 2 * N)
    gates_all = gate_in.reshape(spans, SPAN, INNER)
    steps_all = step_size.reshape(spans, SPAN, MH)

    def advance(carry, items):
        state, inner_tail, pair_tail = carry
        inputs_block, pairs_block, gate_block, steps_block = items
        inner_window = jnp.concatenate([inner_tail, inputs_block], axis=0)
        pair_window = jnp.concatenate([pair_tail, pairs_block], axis=0)
        conv_inner = conv_silu(inner_window, conv_x, SPAN)
        conv_pair = conv_silu(pair_window, conv_bc, SPAN)
        bmatrix = conv_pair[:, :, :N]
        cmatrix = conv_pair[:, :, N:]
        heads_in = conv_inner.reshape(SPAN, MH, P_SIZE)
        intra, cumulative, increment = span_terms(heads_in, bmatrix, cmatrix, steps_block, decay_rate)
        readout = state_readout(cmatrix, state, cumulative)
        mixed = intra + readout + skip_gain[None, :, None] * heads_in.astype(jnp.float32)
        output_block = gated_norm(mixed.reshape(SPAN, INNER), gate_block, norm_gain, G)
        state = jnp.exp(cumulative[-1])[:, None, None] * state + increment
        return ((state, inner_window[SPAN:], pair_window[SPAN:]), output_block)
    initial = (jnp.zeros((MH, P_SIZE, N), jnp.float32), jnp.zeros((KCONV - 1, INNER), jnp.bfloat16), jnp.zeros((KCONV - 1, G, 2 * N), jnp.bfloat16))
    final_carry, mamba_blocks = lax.scan(advance, initial, (inputs_all, pairs_all, gates_all, steps_all))
    mamba_out = mamba_blocks.reshape(TOKENS, INNER)
    attn_out = attention_all(query_heads, key_heads, value_heads)
    return (mamba_out, attn_out)
```

```python
import functools
import math

import jax
import jax.numpy as jnp
import numpy as np
from jax import lax
from jax.experimental import pallas as pl
from jax.experimental.pallas import tpu as pltpu
from jax.sharding import PartitionSpec as P

SPAN = 128
HD = 128
BF = jnp.bfloat16
F32 = jnp.float32
NX, NZ, NC = 4, 4, 2
HEADS, PSIZE, STATE = 32, 64, 256
CHAN = HEADS * PSIZE
TOK = 512
HB = 8
HBC = HB * PSIZE
CHUNK = 1024
VMEM_LIMIT = 58 << 20


def pairs_of(move):
    found = []
    for x in range(NX):
        for z in range(NZ):
            for c in range(NC):
                target = move(x, z, c)
                if target is not None:
                    tx, tz, tc = target
                    found.append(((x * NZ + z) * NC + c, (tx * NZ + tz) * NC + tc))
    return found


def send(value, move):
    return lax.ppermute(value, "ctx", pairs_of(move))


def swap_core(value):
    return send(value, lambda x, z, c: (x, z, 1 - c))


def along_z(value, steps):
    return send(value, lambda x, z, c: (x, (z + steps) % NZ, c))


def along_x(value, steps, wrap=False):
    def move(x, z, c):
        if wrap or 0 <= x + steps < NX:
            return ((x + steps) % NX, z, c)
        return None

    return send(value, move)


def shifted_rows(rows, tail, steps):
    if steps == 0:
        return rows
    rolled = pltpu.roll(rows, steps, 0)
    before = pltpu.roll(tail, steps, 0)
    at = lax.broadcasted_iota(jnp.int32, before.shape, 0)
    top = jnp.where(at < steps, before, rolled[:8])
    return jnp.concatenate([top, rolled[8:]], axis=0)


def conv_silu(rows, tail, taps):
    taps_count = taps.shape[0]
    total = None
    for k in range(taps_count):
        term = taps[k : k + 1] * shifted_rows(rows, tail, taps_count - 1 - k)
        total = term if total is None else total + term
    return (total * jax.nn.sigmoid(total)).astype(BF)


def two_parts(value):
    high = value.astype(BF).astype(F32)
    return [high, (value - high).astype(BF).astype(F32)]


def three_parts(value):
    high = value.astype(BF).astype(F32)
    return [high] + two_parts(value - high)


def span_kernel(
    x_ref,
    before_ref,
    xtail_ref,
    pair_ref,
    pbefore_ref,
    ptail_ref,
    steps_ref,
    rate_ref,
    skip_ref,
    taps_ref,
    ptaps_ref,
    spread_ref,
    column_ref,
    rows_ref,
    y_ref,
    c_ref,
    log_ref,
    end_ref,
    b_s,
    g_s,
    cum_s,
    ci_s,
    ex_s,
    dec_s,
    start_s,
    state_s,
):
    span, block = pl.program_id(0), pl.program_id(1)

    @pl.when(block == 0)
    def _():
        @pl.when(span == 0)
        def _():
            start_s[...] = jnp.zeros_like(start_s)

        before = jnp.where(span == 0, ptail_ref[...], pbefore_ref[...]).astype(F32)[8:]
        pair = conv_silu(pair_ref[...].astype(F32), before, ptaps_ref[...])
        bmat, cmat = pair[:, :STATE], pair[:, STATE:]
        b_s[...] = bmat
        c_ref[...] = cmat
        product = lax.dot_general(
            cmat, bmat, (((1,), (1,)), ((), ())), preferred_element_type=F32
        )
        at_i = lax.broadcasted_iota(jnp.int32, (SPAN, SPAN), 0)
        at_j = lax.broadcasted_iota(jnp.int32, (SPAN, SPAN), 1)
        g_s[...] = jnp.where(at_j <= at_i, product, 0.0)
        steps = steps_ref[...]
        upper = jnp.where(at_i <= at_j, 1.0, 0.0)
        cum = jnp.dot(
            -steps * rate_ref[...], upper, precision=lax.Precision.HIGHEST, preferred_element_type=F32
        )
        cum_s[...] = cum
        last = cum[:, SPAN - 1 : SPAN]
        ci_s[...] = jnp.concatenate(three_parts(cum) + [jnp.zeros_like(cum)], axis=0).T.astype(BF)
        ex_s[...] = jnp.concatenate(
            two_parts(jnp.exp(last - cum) * steps) + two_parts(jnp.exp(cum)), axis=0
        ).T.astype(BF)
        dec_s[...] = jnp.broadcast_to(
            jnp.concatenate(two_parts(jnp.exp(last)), axis=0), dec_s.shape
        ).astype(BF)
        log_ref[...] = start_s[:, :SPAN] + cum
        start_s[...] = start_s[...] + last

    x_rows = x_ref[...].astype(F32)
    before = jnp.where(span == 0, xtail_ref[...], before_ref[...]).astype(F32)[8:]
    xin = conv_silu(x_rows, before, taps_ref[...])
    xf = xin.astype(F32)
    spread = spread_ref[...]
    zero = jnp.zeros_like(spread)
    weight = jnp.dot(ex_s[...], jnp.concatenate([spread, zero], axis=0), preferred_element_type=F32)
    grown = jnp.dot(ex_s[...], jnp.concatenate([zero, spread], axis=0), preferred_element_type=F32)
    rows_i = jnp.dot(ci_s[...], column_ref[...], preferred_element_type=F32)
    first = span == 0
    state = jnp.where(first, 0.0, state_s[block])
    read = lax.dot_general(
        c_ref[...], state.astype(BF), (((1,), (1,)), ((), ())), preferred_element_type=F32
    )
    base = read * grown + skip_ref[...] * xf
    cum_rows = cum_s[pl.ds(block * HB, HB), :]
    step_rows = steps_ref[pl.ds(block * HB, HB), :]
    masked = g_s[...]
    lane = lax.broadcasted_iota(jnp.int32, (SPAN, 2 * PSIZE), 1)
    for pair in range(HB // 2):
        mixes = []
        for h in (2 * pair, 2 * pair + 1):
            gap = rows_i[:, h * SPAN : (h + 1) * SPAN] - cum_rows[h : h + 1]
            mixes.append(
                (masked * jnp.exp(jnp.minimum(gap, 0.0)) * step_rows[h : h + 1]).astype(BF)
            )
        two = xf[:, pair * 128 : (pair + 1) * 128]
        left = jnp.where(lane < PSIZE, two, 0.0).astype(BF)
        right = jnp.where(lane < PSIZE, 0.0, two).astype(BF)
        intra = jnp.dot(
            jnp.concatenate(mixes, axis=1),
            jnp.concatenate([left, right], axis=0),
            preferred_element_type=F32,
        )
        y_ref[:, pair * 128 : (pair + 1) * 128] = base[:, pair * 128 : (pair + 1) * 128] + intra
    weighted = (xf * weight).astype(BF)
    gain = lax.dot_general(
        weighted, b_s[...], (((0,), (0,)), ((), ())), preferred_element_type=F32
    )
    decay = jnp.dot(rows_ref[...], dec_s[...], preferred_element_type=F32)
    state = state * decay + gain
    state_s[block] = state
    end_ref[...] = state.astype(BF)


def own_tokens(ssm_in, tail, bc_in, steps, rate, skip, conv_x, conv_bc):
    spread = np.zeros((2 * HEADS, CHAN), np.float32)
    column = np.zeros((4 * HEADS, HEADS * SPAN), np.float32)
    for h in range(HEADS):
        for part in range(2):
            spread[part * HEADS + h, h * PSIZE : (h + 1) * PSIZE] = 1
        for part in range(3):
            column[part * HEADS + h, h * SPAN : (h + 1) * SPAN] = 1
    grid = (TOK // SPAN, HEADS // HB)
    prior = lambda s, b: (jnp.maximum(s * (SPAN // 16) - 1, 0), b)
    prior0 = lambda s, b: (jnp.maximum(s * (SPAN // 16) - 1, 0), 0)
    return pl.pallas_call(
        span_kernel,
        grid=grid,
        in_specs=[
            pl.BlockSpec((SPAN, HBC), lambda s, b: (s, b)),
            pl.BlockSpec((16, HBC), prior),
            pl.BlockSpec((16, HBC), lambda s, b: (0, b)),
            pl.BlockSpec((SPAN, 2 * STATE), lambda s, b: (s, 0)),
            pl.BlockSpec((16, 2 * STATE), prior0),
            pl.BlockSpec((16, 2 * STATE), lambda s, b: (0, CHAN // (2 * STATE))),
            pl.BlockSpec((HEADS, SPAN), lambda s, b: (0, s)),
            pl.BlockSpec((HEADS, 1), lambda s, b: (0, 0)),
            pl.BlockSpec((1, HBC), lambda s, b: (0, b)),
            pl.BlockSpec((4, HBC), lambda s, b: (0, b)),
            pl.BlockSpec((4, 2 * STATE), lambda s, b: (0, 0)),
            pl.BlockSpec((2 * HEADS, HBC), lambda s, b: (0, b)),
            pl.BlockSpec((4 * HEADS, HB * SPAN), lambda s, b: (0, b)),
            pl.BlockSpec((HBC, 2 * HEADS), lambda s, b: (b, 0)),
        ],
        out_specs=[
            pl.BlockSpec((SPAN, HBC), lambda s, b: (s, b)),
            pl.BlockSpec((SPAN, STATE), lambda s, b: (s, 0)),
            pl.BlockSpec((HEADS, SPAN), lambda s, b: (0, s)),
            pl.BlockSpec((HBC, STATE), lambda s, b: (b, 0)),
        ],
        out_shape=[
            jax.ShapeDtypeStruct((TOK, CHAN), F32),
            jax.ShapeDtypeStruct((TOK, STATE), BF),
            jax.ShapeDtypeStruct((HEADS, TOK), F32),
            jax.ShapeDtypeStruct((CHAN, STATE), BF),
        ],
        scratch_shapes=[
            pltpu.VMEM((SPAN, STATE), BF),
            pltpu.VMEM((SPAN, SPAN), F32),
            pltpu.VMEM((HEADS, SPAN), F32),
            pltpu.VMEM((SPAN, 4 * HEADS), BF),
            pltpu.VMEM((SPAN, 4 * HEADS), BF),
            pltpu.VMEM((2 * HEADS, STATE), BF),
            pltpu.VMEM((HEADS, SPAN), F32),
            pltpu.VMEM((HEADS // HB, HBC, STATE), F32),
        ],
        compiler_params=pltpu.CompilerParams(vmem_limit_bytes=VMEM_LIMIT),
        cost_estimate=pl.CostEstimate(flops=8 << 30, bytes_accessed=12 << 20, transcendentals=4 << 20),
    )(
        ssm_in,
        ssm_in,
        tail,
        bc_in,
        bc_in,
        tail,
        steps,
        rate,
        skip,
        conv_x,
        conv_bc,
        jnp.asarray(spread, BF),
        jnp.asarray(column, BF),
        jnp.asarray(spread.T, BF),
    )


def entering_state(end, logs, c, z, x):
    half = end.reshape(2, 16, PSIZE, STATE)
    keep = lax.dynamic_index_in_dim(half, c, 0, False)
    give = lax.dynamic_index_in_dim(half, 1 - c, 0, False)
    other = swap_core(give)
    by_half = logs.reshape(NX, NZ, NC, 2, 16)
    mine = lax.dynamic_index_in_dim(by_half, c, 3, False)
    here = lax.dynamic_index_in_dim(lax.dynamic_index_in_dim(mine, x, 0, False), z, 0, False)
    early = jnp.where(c == 0, keep, other).astype(F32)
    late = jnp.where(c == 0, other, keep).astype(F32)
    total = (late + jnp.exp(here[1])[:, None, None] * early).astype(BF).reshape(NZ, 4, PSIZE, STATE)
    quarters = [lax.dynamic_index_in_dim(total, (z + s) % NZ, 0, False) for s in range(NZ)]
    got = [quarters[0]] + [along_z(quarters[s], s) for s in range(1, NZ)]
    chip = jnp.sum(mine, axis=2).reshape(NX, NZ, NZ, 4)
    chip = lax.dynamic_index_in_dim(chip, z, 2, False)
    plane = lax.dynamic_index_in_dim(chip, x, 0, False)
    upto = jnp.concatenate([jnp.zeros((1, 4), F32), jnp.cumsum(plane, axis=0)], axis=0)
    sources = (z - jnp.arange(NZ)) % NZ
    first = jnp.take(upto, sources + 1, axis=0)
    reach = upto[:, None, :] - first[None]
    weights = jnp.where(
        sources[None, :, None] < jnp.arange(NZ + 1)[:, None, None], jnp.exp(jnp.minimum(reach, 0.0)), 0.0
    )

    def joined(to):
        return sum(weights[to, s][:, None, None] * got[s].astype(F32) for s in range(NZ))

    whole = joined(NZ).astype(BF)
    planes = jnp.sum(chip, axis=1)
    passed = jnp.concatenate([jnp.zeros((1, 4), F32), jnp.cumsum(planes, axis=0)], axis=0)
    into = lax.dynamic_index_in_dim(passed, x, 0, False)
    carried = jnp.zeros((4, PSIZE, STATE), F32)
    for s in range(1, NX):
        after = lax.dynamic_index_in_dim(passed, jnp.maximum(x - s, 0) + 1, 0, False)
        factor = jnp.where(x >= s, jnp.exp(jnp.minimum(into - after, 0.0)), 0.0)
        carried = carried + factor[:, None, None] * along_x(whole, s).astype(F32)
    prefix = [joined(to) for to in range(NZ)]
    outs = jnp.stack(
        [
            (prefix[to] + jnp.exp(upto[to])[:, None, None] * carried).astype(BF)
            for to in range(NZ)
        ]
    )
    back = [lax.dynamic_index_in_dim(outs, z, 0, False)]
    for s in range(1, NZ):
        back.append(along_z(lax.dynamic_index_in_dim(outs, (z + s) % NZ, 0, False), s))
    back = jnp.stack(back)
    chip_in = jnp.stack(
        [lax.dynamic_index_in_dim(back, (z - q) % NZ, 0, False) for q in range(NZ)]
    ).reshape(16, PSIZE, STATE)
    second = (early + jnp.exp(here[0])[:, None, None] * chip_in.astype(F32)).astype(BF)
    for_me = jnp.where(c == 0, chip_in, second)
    for_other = swap_core(jnp.where(c == 0, second, chip_in))
    return jnp.stack(
        [jnp.where(c == 0, for_me, for_other), jnp.where(c == 0, for_other, for_me)]
    ).reshape(CHAN, STATE)


def finish_kernel(y_ref, c_ref, log_ref, in_ref, gate_ref, gain_ref, spread_ref, out_ref):
    grown = jnp.concatenate(
        two_parts(jnp.exp(log_ref[...])) + [jnp.zeros((2 * HEADS, SPAN), F32)], axis=0
    ).T.astype(BF)
    spread = spread_ref[...]
    scale = jnp.dot(
        grown, jnp.concatenate([spread, jnp.zeros_like(spread)], axis=0), preferred_element_type=F32
    )
    read = lax.dot_general(
        c_ref[...], in_ref[...], (((1,), (1,)), ((), ())), preferred_element_type=F32
    )
    mixed = y_ref[...] + read * scale
    gate = gate_ref[...].astype(F32)
    gated = mixed * (gate * jax.nn.sigmoid(gate))
    mean = jnp.mean(gated * gated, axis=1, keepdims=True)
    out_ref[...] = (gated * lax.rsqrt(mean + 1e-05) * gain_ref[...]).astype(BF)


def finish(y, cmat, logs, entering, gate, gain):
    spread = np.zeros((2 * HEADS, CHAN), np.float32)
    for h in range(HEADS):
        for part in range(2):
            spread[part * HEADS + h, h * PSIZE : (h + 1) * PSIZE] = 1
    return pl.pallas_call(
        finish_kernel,
        grid=(TOK // SPAN,),
        in_specs=[
            pl.BlockSpec((SPAN, CHAN), lambda s: (s, 0)),
            pl.BlockSpec((SPAN, STATE), lambda s: (s, 0)),
            pl.BlockSpec((HEADS, SPAN), lambda s: (0, s)),
            pl.BlockSpec((CHAN, STATE), lambda s: (0, 0)),
            pl.BlockSpec((SPAN, CHAN), lambda s: (s, 0)),
            pl.BlockSpec((1, CHAN), lambda s: (0, 0)),
            pl.BlockSpec((2 * HEADS, CHAN), lambda s: (0, 0)),
        ],
        out_specs=pl.BlockSpec((SPAN, CHAN), lambda s: (s, 0)),
        out_shape=jax.ShapeDtypeStruct((TOK, CHAN), BF),
        compiler_params=pltpu.CompilerParams(vmem_limit_bytes=VMEM_LIMIT),
        cost_estimate=pl.CostEstimate(flops=2 << 30, bytes_accessed=10 << 20, transcendentals=1 << 20),
    )(y, cmat, logs, entering, gate, gain, jnp.asarray(spread, BF))


def attend_kernel(
    list_ref,
    q_ref,
    *refs,
    planes,
):
    pieces = refs[: 2 * planes]
    out_ref, kv, sums, top, qq, sa, sb, ma, mb, sems = refs[2 * planes :]
    sub = 256

    def copies():
        found = []
        for p in range(planes):
            for side in range(2):
                for slot in range(NZ):
                    found.append(
                        pltpu.make_async_copy(
                            pieces[2 * p + side].at[slot],
                            kv.at[p * NZ + slot, pl.ds(side * TOK, TOK)],
                            sems.at[(p * 2 + side) * NZ + slot],
                        )
                    )
        return found

    @pl.when(pl.program_id(0) == 0)
    def _():
        for copy in copies():
            copy.start()

    scaled = q_ref[...].astype(F32) * (HD**-0.5 * math.log2(math.e))
    high = scaled.astype(BF)
    low = (scaled - high.astype(F32)).astype(BF)
    qq[...] = jnp.concatenate([high, low], axis=1)
    sums[...] = jnp.zeros_like(sums)
    top[...] = jnp.full_like(top, -1e30)

    @pl.when(pl.program_id(0) == 0)
    def _():
        for copy in copies():
            copy.wait()

    count = list_ref[0]
    core = list_ref[1]
    ones = jnp.ones((CHUNK, HD), BF)

    def score(at, s_ref, m_ref, masked=False):
        keys = kv[at, :, :HD]
        twice = jnp.concatenate([keys, keys], axis=1)
        for r in range(TOK // sub):
            rows = slice(r * sub, (r + 1) * sub)
            s = lax.dot_general(
                qq[rows, :], twice, (((1,), (1,)), ((), ())), preferred_element_type=F32
            )
            if masked:
                row = lax.broadcasted_iota(jnp.int32, s.shape, 0) + r * sub
                key = lax.broadcasted_iota(jnp.int32, s.shape, 1)
                limit = jnp.where(core == 1, 2 * TOK, TOK)
                seen = ((key < TOK) & (key <= row)) | ((key >= TOK) & (key < limit))
                s = jnp.where(seen, s, -1e30)
            s_ref[rows, :] = s
            m_ref[rows, :] = jnp.broadcast_to(jnp.max(s, axis=1, keepdims=True), (sub, HD))

    def gather(at, s_ref, m_ref):
        values = jnp.concatenate([kv[at, :, HD:], ones], axis=1)
        for r in range(TOK // sub):
            rows = slice(r * sub, (r + 1) * sub)
            old = top[rows, :]
            new = jnp.maximum(old, m_ref[rows, :])
            weights = jnp.exp2(s_ref[rows, :] - new[:, :1]).astype(BF)
            factor = jnp.exp2(old - new)
            part = jnp.dot(weights, values, preferred_element_type=F32)
            sums[rows, :] = sums[rows, :] * jnp.concatenate([factor, factor], axis=1) + part
            top[rows, :] = new

    def chunk(i):
        return list_ref[2 + jnp.minimum(i, count - 1)]

    score(chunk(0), sa, ma, masked=True)

    def body(j, _):
        i = 2 * j
        score(chunk(i + 1), sb, mb)
        gather(chunk(i), sa, ma)
        score(chunk(i + 2), sa, ma)
        gather(chunk(i + 1), sb, mb)
        return 0

    lax.fori_loop(0, count // 2, body, 0)

    @pl.when(count % 2 == 1)
    def _():
        gather(chunk(count - 1), sa, ma)

    out_ref[...] = (sums[:, :HD] / sums[:, HD:]).astype(BF)


def attend(order, query, pieces):
    planes = len(pieces) // 2
    return pl.pallas_call(
        functools.partial(attend_kernel, planes=planes),
        grid=(4,),
        in_specs=[
            pl.BlockSpec(memory_space=pltpu.SMEM),
            pl.BlockSpec((TOK, HD), lambda h: (0, h)),
        ]
        + [pl.BlockSpec(memory_space=pl.ANY)] * len(pieces),
        out_specs=pl.BlockSpec((TOK, HD), lambda h: (0, h)),
        out_shape=jax.ShapeDtypeStruct((TOK, 4 * HD), BF),
        scratch_shapes=[
            pltpu.VMEM((planes * NZ, CHUNK, 2 * HD), BF),
            pltpu.VMEM((TOK, 2 * HD), F32),
            pltpu.VMEM((TOK, HD), F32),
            pltpu.VMEM((TOK, 2 * HD), BF),
            pltpu.VMEM((TOK, CHUNK), F32),
            pltpu.VMEM((TOK, CHUNK), F32),
            pltpu.VMEM((TOK, HD), F32),
            pltpu.VMEM((TOK, HD), F32),
            pltpu.SemaphoreType.DMA((planes * 2 * NZ,)),
        ],
        compiler_params=pltpu.CompilerParams(vmem_limit_bytes=VMEM_LIMIT),
        cost_estimate=pl.CostEstimate(flops=50 << 30, bytes_accessed=10 << 20, transcendentals=32 << 20),
    )(order, query, *pieces)


def gathered_keys(key_heads, value_heads):
    own = jnp.concatenate([key_heads, value_heads], axis=1)
    up = along_z(own, 1)
    down = along_z(own, -1)
    two = along_z(up, 1)
    plane = jnp.stack([own, up, down, two])
    left = along_x(plane, 1, wrap=True)
    right = along_x(plane, -1, wrap=True)
    far = jnp.concatenate(
        [along_x(left[:2], 1, wrap=True), along_x(right[2:], -1, wrap=True)], axis=0
    )
    pieces = []
    for part in (plane, left, right, far):
        pieces += [part, swap_core(part)]
    return pieces


def visible_chunks(c, z, x):
    px = (x + jnp.array([0, -1, 1, -2])) % NX
    pz = (z + jnp.array([0, -1, 1, -2])) % NZ
    chip = (px[:, None] * NZ + pz[None, :]).reshape(-1)
    mine = x * NZ + z
    ids = jnp.arange(NX * NZ)
    rank = jnp.where(chip == mine, -1, jnp.where(chip < mine, ids, 99))
    place = jnp.sum(rank[None, :] < rank[:, None], axis=1)
    listed = jnp.sum(
        jnp.where((place[:, None] == ids[None, :]) & (rank[:, None] < 99), ids[:, None], 0), axis=0
    )
    return jnp.concatenate([jnp.stack([mine + 1, c]), listed]).astype(jnp.int32)


def local(
    hidden,
    dt_weight,
    dt_bias,
    decay_rate,
    skip_gain,
    ssm_in,
    bc_in,
    conv_x,
    conv_bc,
    gate_in,
    norm_gain,
    query_heads,
    key_heads,
    value_heads,
):
    mine = lax.axis_index("ctx")
    x, z, c = mine // (NZ * NC), (mine // NC) % NZ, mine % NC
    bc = bc_in.reshape(TOK, 2 * STATE)
    ends = jnp.concatenate([ssm_in[TOK - 16 :], bc[TOK - 16 :]], axis=1)
    tail = lax.ppermute(ends, "ctx", [(i, i + 1) for i in range(31)])
    partial = lax.dot_general(
        dt_weight, hidden, (((0,), (1,)), ((), ())), preferred_element_type=F32
    )
    parts = lax.all_to_all(partial.reshape(8, HEADS, TOK), "head", 0, 0, tiled=True)
    steps = jax.nn.softplus(jnp.sum(parts, axis=0) + dt_bias[:, None])
    total = -jnp.sum(steps, axis=1) * decay_rate
    logs = lax.all_gather(total, "ctx")
    y, cmat, grown, end = own_tokens(
        ssm_in,
        tail,
        bc,
        steps,
        decay_rate[:, None],
        jnp.repeat(skip_gain, PSIZE)[None],
        conv_x,
        conv_bc.reshape(4, 2 * STATE),
    )
    pieces = gathered_keys(key_heads, value_heads)
    entering = entering_state(end, logs, c, z, x)
    attn_out = attend(visible_chunks(c, z, x), query_heads, pieces)
    mamba_out = finish(y, cmat, grown, entering, gate_in, norm_gain[None])
    return (mamba_out, attn_out)


def solution(mesh):
    in_specs = (
        P("ctx", "head"),
        P("head", None),
        P("head"),
        P("head"),
        P("head"),
        P("ctx", "head"),
        P("ctx", "head", None),
        P(None, "head"),
        P(None, "head", None),
        P("ctx", "head"),
        P("head"),
        P("ctx", "head"),
        P("ctx", "head"),
        P("ctx", "head"),
    )
    out_specs = (P("ctx", "head"), P("ctx", "head"))
    return jax.shard_map(local, mesh=mesh, in_specs=in_specs, out_specs=out_specs, check_vma=False)
```

```python
import functools
import math

import jax
import jax.numpy as jnp
import numpy as np
from jax import lax
from jax.experimental import pallas as pl
from jax.experimental.pallas import tpu as pltpu
from jax.sharding import PartitionSpec as P

SPAN = 128
HD = 128
BF = jnp.bfloat16
F32 = jnp.float32
NX, NZ, NC = 4, 4, 2
HEADS, PSIZE, STATE = 32, 64, 256
CHAN = HEADS * PSIZE
TOK = 512
HB = 32
HBC = HB * PSIZE
CHUNK = 1024
VMEM_LIMIT = 58 << 20


def pairs_of(move):
    found = []
    for x in range(NX):
        for z in range(NZ):
            for c in range(NC):
                target = move(x, z, c)
                if target is not None:
                    tx, tz, tc = target
                    found.append(((x * NZ + z) * NC + c, (tx * NZ + tz) * NC + tc))
    return found


def send(value, move):
    return lax.ppermute(value, "ctx", pairs_of(move))


def swap_core(value):
    return send(value, lambda x, z, c: (x, z, 1 - c))


def along_z(value, steps):
    return send(value, lambda x, z, c: (x, (z + steps) % NZ, c))


def along_x(value, steps, wrap=False):
    def move(x, z, c):
        if wrap or 0 <= x + steps < NX:
            return ((x + steps) % NX, z, c)
        return None

    return send(value, move)


def shifted_rows(rows, tail, steps):
    if steps == 0:
        return rows
    rolled = pltpu.roll(rows, steps, 0)
    before = pltpu.roll(tail, steps, 0)
    at = lax.broadcasted_iota(jnp.int32, before.shape, 0)
    top = jnp.where(at < steps, before, rolled[:8])
    return jnp.concatenate([top, rolled[8:]], axis=0)


def conv_silu(rows, tail, taps):
    taps_count = taps.shape[0]
    total = None
    for k in range(taps_count):
        term = taps[k : k + 1] * shifted_rows(rows, tail, taps_count - 1 - k)
        total = term if total is None else total + term
    return (total * jax.nn.sigmoid(total)).astype(BF)


def two_parts(value):
    high = value.astype(BF).astype(F32)
    return [high, (value - high).astype(BF).astype(F32)]


def three_parts(value):
    high = value.astype(BF).astype(F32)
    return [high] + two_parts(value - high)


def states_kernel(
    core_ref,
    x_ref,
    before_ref,
    xtail_ref,
    pair_ref,
    pbefore_ref,
    ptail_ref,
    steps_ref,
    drop_ref,
    taps_ref,
    ptaps_ref,
    spread_ref,
    rows_ref,
    xin_ref,
    conv_ref,
    cum_ref,
    log_ref,
    start_ref,
    mine_ref,
    give_ref,
    b_s,
    ex_s,
    dec_s,
    log_s,
    state_s,
):
    span, block = pl.program_id(0), pl.program_id(1)

    @pl.when(block == 0)
    def _():
        @pl.when(span == 0)
        def _():
            log_s[...] = jnp.zeros_like(log_s)

        before = jnp.where(span == 0, ptail_ref[...], pbefore_ref[...]).astype(F32)[8:]
        pair = conv_silu(pair_ref[...].astype(F32), before, ptaps_ref[...])
        conv_ref[...] = pair
        b_s[...] = pair[:, :STATE]
        at_i = lax.broadcasted_iota(jnp.int32, (SPAN, SPAN), 0)
        at_j = lax.broadcasted_iota(jnp.int32, (SPAN, SPAN), 1)
        steps = steps_ref[...]
        upper = jnp.where(at_i <= at_j, 1.0, 0.0)
        cum = jnp.dot(
            drop_ref[...], upper, precision=lax.Precision.HIGHEST, preferred_element_type=F32
        )
        cum_ref[...] = cum
        last = cum[:, SPAN - 1 : SPAN]
        ex_s[...] = jnp.concatenate(
            two_parts(jnp.exp(last - cum) * steps) + [jnp.zeros((2 * HEADS, SPAN), F32)], axis=0
        ).T.astype(BF)
        dec_s[...] = jnp.broadcast_to(
            jnp.concatenate(two_parts(jnp.exp(last)), axis=0), dec_s.shape
        ).astype(BF)
        log_ref[...] = log_s[...] + cum
        log_s[...] = log_s[...] + last

    before = jnp.where(span == 0, xtail_ref[...], before_ref[...]).astype(F32)[8:]
    xin = conv_silu(x_ref[...].astype(F32), before, taps_ref[...])
    xin_ref[...] = xin
    spread = spread_ref[...]
    weight = jnp.dot(
        ex_s[...], jnp.concatenate([spread, jnp.zeros_like(spread)], axis=0), preferred_element_type=F32
    )
    weighted = (xin.astype(F32) * weight).astype(BF)
    gain = lax.dot_general(
        weighted, b_s[...], (((0,), (0,)), ((), ())), preferred_element_type=F32
    )
    decay = jnp.dot(rows_ref[...], dec_s[...], preferred_element_type=F32)
    state = jnp.where(span == 0, 0.0, state_s[block])
    start_ref[...] = state.astype(BF)
    state = state * decay + gain
    state_s[block] = state

    @pl.when(span == TOK // SPAN - 1)
    def _():
        low = state.astype(BF)
        first = core_ref[0] == 0
        mine_ref[...] = jnp.where(first, low[: CHAN // 2], low[CHAN // 2 :])
        give_ref[...] = jnp.where(first, low[CHAN // 2 :], low[: CHAN // 2])


def spread_rows():
    spread = np.zeros((2 * HEADS, CHAN), np.float32)
    for h in range(HEADS):
        for part in range(2):
            spread[part * HEADS + h, h * PSIZE : (h + 1) * PSIZE] = 1
    return spread


def own_states(core, ssm_in, tail, bc_in, steps, drop, conv_x, conv_bc):
    spread = spread_rows()
    blocks = HEADS // HB
    prior = lambda s, b: (jnp.maximum(s * (SPAN // 16) - 1, 0), b)
    prior0 = lambda s, b: (jnp.maximum(s * (SPAN // 16) - 1, 0), 0)
    return pl.pallas_call(
        states_kernel,
        grid=(TOK // SPAN, blocks),
        in_specs=[
            pl.BlockSpec(memory_space=pltpu.SMEM),
            pl.BlockSpec((SPAN, HBC), lambda s, b: (s, b)),
            pl.BlockSpec((16, HBC), prior),
            pl.BlockSpec((16, HBC), lambda s, b: (0, b)),
            pl.BlockSpec((SPAN, 2 * STATE), lambda s, b: (s, 0)),
            pl.BlockSpec((16, 2 * STATE), prior0),
            pl.BlockSpec((16, 2 * STATE), lambda s, b: (0, CHAN // (2 * STATE))),
            pl.BlockSpec((HEADS, SPAN), lambda s, b: (0, s)),
            pl.BlockSpec((HEADS, SPAN), lambda s, b: (0, s)),
            pl.BlockSpec((4, HBC), lambda s, b: (0, b)),
            pl.BlockSpec((4, 2 * STATE), lambda s, b: (0, 0)),
            pl.BlockSpec((2 * HEADS, HBC), lambda s, b: (0, b)),
            pl.BlockSpec((HBC, 2 * HEADS), lambda s, b: (b, 0)),
        ],
        out_specs=[
            pl.BlockSpec((SPAN, HBC), lambda s, b: (s, b)),
            pl.BlockSpec((SPAN, 2 * STATE), lambda s, b: (s, 0)),
            pl.BlockSpec((HEADS, SPAN), lambda s, b: (0, s)),
            pl.BlockSpec((HEADS, SPAN), lambda s, b: (0, s)),
            pl.BlockSpec((HBC, STATE), lambda s, b: (s * blocks + b, 0)),
            pl.BlockSpec((CHAN // 2, STATE), lambda s, b: (0, 0)),
            pl.BlockSpec((CHAN // 2, STATE), lambda s, b: (0, 0)),
        ],
        out_shape=[
            jax.ShapeDtypeStruct((TOK, CHAN), BF),
            jax.ShapeDtypeStruct((TOK, 2 * STATE), BF),
            jax.ShapeDtypeStruct((HEADS, TOK), F32),
            jax.ShapeDtypeStruct((HEADS, TOK), F32),
            jax.ShapeDtypeStruct((TOK // SPAN * CHAN, STATE), BF),
            jax.ShapeDtypeStruct((CHAN // 2, STATE), BF),
            jax.ShapeDtypeStruct((CHAN // 2, STATE), BF),
        ],
        scratch_shapes=[
            pltpu.VMEM((SPAN, STATE), BF),
            pltpu.VMEM((SPAN, 4 * HEADS), BF),
            pltpu.VMEM((2 * HEADS, STATE), BF),
            pltpu.VMEM((HEADS, SPAN), F32),
            pltpu.VMEM((blocks, HBC, STATE), F32),
        ],
        compiler_params=pltpu.CompilerParams(vmem_limit_bytes=VMEM_LIMIT),
        cost_estimate=pl.CostEstimate(flops=4 << 30, bytes_accessed=12 << 20, transcendentals=2 << 20),
    )(
        core,
        ssm_in,
        ssm_in,
        tail,
        bc_in,
        bc_in,
        tail,
        steps,
        drop,
        conv_x,
        conv_bc,
        jnp.asarray(spread, BF),
        jnp.asarray(spread.T, BF),
    )


def inside_kernel(
    xin_ref,
    pair_ref,
    cum_ref,
    steps_ref,
    start_ref,
    skip_ref,
    spread_ref,
    column_ref,
    y_ref,
    g_s,
    ci_s,
    ex_s,
):
    block = pl.program_id(1)
    cmat = pair_ref[:, STATE:]

    @pl.when(block == 0)
    def _():
        product = lax.dot_general(
            cmat, pair_ref[:, :STATE], (((1,), (1,)), ((), ())), preferred_element_type=F32
        )
        at_i = lax.broadcasted_iota(jnp.int32, (SPAN, SPAN), 0)
        at_j = lax.broadcasted_iota(jnp.int32, (SPAN, SPAN), 1)
        g_s[...] = jnp.where(at_j <= at_i, product, 0.0)
        cum = cum_ref[...]
        ci_s[...] = jnp.concatenate(three_parts(cum) + [jnp.zeros_like(cum)], axis=0).T.astype(BF)
        ex_s[...] = jnp.concatenate(
            two_parts(jnp.exp(cum)) + [jnp.zeros((2 * HEADS, SPAN), F32)], axis=0
        ).T.astype(BF)

    xf = xin_ref[...].astype(F32)
    spread = spread_ref[...]
    grown = jnp.dot(
        ex_s[...], jnp.concatenate([spread, jnp.zeros_like(spread)], axis=0), preferred_element_type=F32
    )
    rows_i = jnp.dot(ci_s[...], column_ref[...], preferred_element_type=F32)
    read = lax.dot_general(
        cmat, start_ref[...], (((1,), (1,)), ((), ())), preferred_element_type=F32
    )
    base = read * grown + skip_ref[...] * xf
    cum_rows = cum_ref[pl.ds(pl.multiple_of(block * HB, HB), HB), :]
    step_rows = steps_ref[pl.ds(pl.multiple_of(block * HB, HB), HB), :]
    masked = g_s[...]
    lane = lax.broadcasted_iota(jnp.int32, (SPAN, 2 * PSIZE), 1)
    for pair in range(HB // 2):
        mixes = []
        for h in (2 * pair, 2 * pair + 1):
            gap = rows_i[:, h * SPAN : (h + 1) * SPAN] - cum_rows[h : h + 1]
            mixes.append(
                (masked * jnp.exp(jnp.minimum(gap, 0.0)) * step_rows[h : h + 1]).astype(BF)
            )
        two = xf[:, pair * 128 : (pair + 1) * 128]
        left = jnp.where(lane < PSIZE, two, 0.0).astype(BF)
        right = jnp.where(lane < PSIZE, 0.0, two).astype(BF)
        intra = jnp.dot(
            jnp.concatenate(mixes, axis=1),
            jnp.concatenate([left, right], axis=0),
            preferred_element_type=F32,
        )
        y_ref[:, pair * 128 : (pair + 1) * 128] = base[:, pair * 128 : (pair + 1) * 128] + intra


def inside_blocks(xin, pair, cum, steps, starts, skip):
    column = np.zeros((4 * HEADS, HEADS * SPAN), np.float32)
    for h in range(HEADS):
        for part in range(3):
            column[part * HEADS + h, h * SPAN : (h + 1) * SPAN] = 1
    blocks = HEADS // HB
    return pl.pallas_call(
        inside_kernel,
        grid=(TOK // SPAN, blocks),
        in_specs=[
            pl.BlockSpec((SPAN, HBC), lambda s, b: (s, b)),
            pl.BlockSpec((SPAN, 2 * STATE), lambda s, b: (s, 0)),
            pl.BlockSpec((HEADS, SPAN), lambda s, b: (0, s)),
            pl.BlockSpec((HEADS, SPAN), lambda s, b: (0, s)),
            pl.BlockSpec((HBC, STATE), lambda s, b: (s * blocks + b, 0)),
            pl.BlockSpec((1, HBC), lambda s, b: (0, b)),
            pl.BlockSpec((2 * HEADS, HBC), lambda s, b: (0, b)),
            pl.BlockSpec((4 * HEADS, HB * SPAN), lambda s, b: (0, b)),
        ],
        out_specs=pl.BlockSpec((SPAN, HBC), lambda s, b: (s, b)),
        out_shape=jax.ShapeDtypeStruct((TOK, CHAN), F32),
        scratch_shapes=[
            pltpu.VMEM((SPAN, SPAN), F32),
            pltpu.VMEM((SPAN, 4 * HEADS), BF),
            pltpu.VMEM((SPAN, 4 * HEADS), BF),
        ],
        compiler_params=pltpu.CompilerParams(vmem_limit_bytes=VMEM_LIMIT),
        cost_estimate=pl.CostEstimate(flops=8 << 30, bytes_accessed=12 << 20, transcendentals=4 << 20),
    )(xin, pair, cum, steps, starts, skip, jnp.asarray(spread_rows(), BF), jnp.asarray(column, BF))


CHIPS = NX * NZ
SAME_CORE = [[2 * chip + core for chip in range(CHIPS)] for core in range(NC)]


def chain_kernel(decay_ref, from_ref, into_ref):
    carried = jnp.zeros(from_ref.shape[1:], F32)
    for chip in range(CHIPS):
        into_ref[chip] = carried.astype(BF)
        if chip < CHIPS - 1:
            carried = decay_ref[chip] * carried + from_ref[chip].astype(F32)


def chain(decays, states):
    return pl.pallas_call(
        chain_kernel,
        in_specs=[
            pl.BlockSpec(memory_space=pltpu.SMEM),
            pl.BlockSpec(memory_space=pltpu.VMEM),
        ],
        out_specs=pl.BlockSpec(memory_space=pltpu.VMEM),
        out_shape=jax.ShapeDtypeStruct(states.shape, BF),
        cost_estimate=pl.CostEstimate(flops=1 << 20, bytes_accessed=1 << 20, transcendentals=0),
    )(decays, states)


def exchanged(value):
    return lax.all_to_all(value, "ctx", 0, 0, tiled=True, axis_index_groups=SAME_CORE)


def decay_logs(total, mine):
    lead = total.reshape(2, 16).T.reshape(32, 1)
    rows = jnp.concatenate(
        [lead, jnp.broadcast_to(total[None], (32, HEADS)), jnp.zeros((32, 95), F32)], axis=1
    )
    got = lax.all_to_all(rows, "ctx", 0, 0, tiled=True)
    partner = lax.dynamic_index_in_dim(got, mine + 1 - 2 * (mine % NC), 0, False)[1 : 1 + HEADS]
    chip_decay = jnp.exp(jnp.sum(got[:, 0].reshape(CHIPS, NC), axis=1))
    return partner, chip_decay


def finish_kernel(
    core_ref, y_ref, c_ref, log_ref, in_ref, other_ref, gate_ref, gain_ref, spread_ref, out_ref
):
    grown = jnp.concatenate(
        two_parts(jnp.exp(log_ref[...])) + [jnp.zeros((2 * HEADS, SPAN), F32)], axis=0
    ).T.astype(BF)
    spread = spread_ref[...]
    scale = jnp.dot(
        grown, jnp.concatenate([spread, jnp.zeros_like(spread)], axis=0), preferred_element_type=F32
    )
    contract = (((1,), (1,)), ((), ()))
    kept = lax.dot_general(c_ref[...], in_ref[...], contract, preferred_element_type=F32)
    given = lax.dot_general(c_ref[...], other_ref[...], contract, preferred_element_type=F32)
    first = core_ref[0] == 0
    read = jnp.concatenate(
        [jnp.where(first, kept, given), jnp.where(first, given, kept)], axis=1
    )
    mixed = y_ref[...] + read * scale
    gate = gate_ref[...].astype(F32)
    gated = mixed * (gate * jax.nn.sigmoid(gate))
    mean = jnp.mean(gated * gated, axis=1, keepdims=True)
    out_ref[...] = (gated * lax.rsqrt(mean + 1e-05) * gain_ref[...]).astype(BF)


def finish(core, y, pair, logs, entering, other, gate, gain):
    return pl.pallas_call(
        finish_kernel,
        grid=(TOK // SPAN,),
        in_specs=[
            pl.BlockSpec(memory_space=pltpu.SMEM),
            pl.BlockSpec((SPAN, CHAN), lambda s: (s, 0)),
            pl.BlockSpec((SPAN, STATE), lambda s: (s, 1)),
            pl.BlockSpec((HEADS, SPAN), lambda s: (0, s)),
            pl.BlockSpec((CHAN // 2, STATE), lambda s: (0, 0)),
            pl.BlockSpec((CHAN // 2, STATE), lambda s: (0, 0)),
            pl.BlockSpec((SPAN, CHAN), lambda s: (s, 0)),
            pl.BlockSpec((1, CHAN), lambda s: (0, 0)),
            pl.BlockSpec((2 * HEADS, CHAN), lambda s: (0, 0)),
        ],
        out_specs=pl.BlockSpec((SPAN, CHAN), lambda s: (s, 0)),
        out_shape=jax.ShapeDtypeStruct((TOK, CHAN), BF),
        compiler_params=pltpu.CompilerParams(vmem_limit_bytes=VMEM_LIMIT),
        cost_estimate=pl.CostEstimate(flops=2 << 30, bytes_accessed=10 << 20, transcendentals=1 << 20),
    )(core, y, pair, logs, entering, other, gate, gain, jnp.asarray(spread_rows(), BF))


QHEADS = 4
SUB = 256


def attend_kernel(flag_ref, q_ref, near_ref, pair_ref, *refs, first, last):
    if first:
        carry_ref = None
        out_ref, kv, sums, top, qq, sa, sb, ma, mb, sems = refs
    else:
        carry_ref, out_ref, kv, sums, top, qq, sa, sb, ma, mb, sems = refs
    count = flag_ref[0]
    core = flag_ref[1]

    def copies():
        found = []
        for side, piece in enumerate((near_ref, pair_ref)):
            for slot in range(NZ):
                found.append(
                    pltpu.make_async_copy(
                        piece.at[slot], kv.at[slot, pl.ds(side * TOK, TOK)], sems.at[side * NZ + slot]
                    )
                )
        return found

    def score(head, at, s_ref, m_ref, masked=False):
        keys = kv[at, :, :HD]
        twice = jnp.concatenate([keys, keys], axis=1)
        for r in range(TOK // SUB):
            rows = slice(r * SUB, (r + 1) * SUB)
            s = lax.dot_general(
                qq[head, rows, :], twice, (((1,), (1,)), ((), ())), preferred_element_type=F32
            )
            if masked:
                row = lax.broadcasted_iota(jnp.int32, s.shape, 0) + r * SUB
                key = lax.broadcasted_iota(jnp.int32, s.shape, 1)
                limit = jnp.where(core == 1, 2 * TOK, TOK)
                seen = ((key < TOK) & (key <= row)) | ((key >= TOK) & (key < limit))
                s = jnp.where(seen, s, -1e30)
            s_ref[rows, :] = s
            m_ref[rows, :] = jnp.broadcast_to(jnp.max(s, axis=1, keepdims=True), (SUB, HD))

    def gather(head, at, s_ref, m_ref):
        values = jnp.concatenate([kv[at, :, HD:], jnp.ones((CHUNK, HD), BF)], axis=1)
        for r in range(TOK // SUB):
            rows = slice(r * SUB, (r + 1) * SUB)
            old = top[head, rows, :]
            new = jnp.maximum(old, m_ref[rows, :])
            weights = jnp.exp2(s_ref[rows, :] - new[:, :1]).astype(BF)
            factor = jnp.exp2(old - new)
            part = jnp.dot(weights, values, preferred_element_type=F32)
            sums[head, rows, :] = (
                sums[head, rows, :] * jnp.concatenate([factor, factor], axis=1) + part
            )
            top[head, rows, :] = new

    @pl.when(count > 0)
    def _():
        for copy in copies():
            copy.start()
        for head in range(QHEADS):
            scaled = q_ref[:, head * HD : (head + 1) * HD].astype(F32) * (HD**-0.5 * math.log2(math.e))
            high = scaled.astype(BF)
            low = (scaled - high.astype(F32)).astype(BF)
            qq[head] = jnp.concatenate([high, low], axis=1)
            if first:
                sums[head] = jnp.zeros((TOK, 2 * HD), F32)
                top[head] = jnp.full((TOK, HD), -1e30, F32)
            else:
                block = carry_ref[:, 2 * head * HD : 2 * (head + 1) * HD]
                sums[head] = jnp.concatenate(
                    [block[:, :HD], jnp.broadcast_to(block[:, HD : HD + 1], (TOK, HD))], axis=1
                )
                top[head] = jnp.broadcast_to(block[:, 2 * HD - 1 :], (TOK, HD))
        for copy in copies():
            copy.wait()

        if first:
            def chunk(i):
                return flag_ref[2 + jnp.minimum(i, count - 1)]

            def one_head(head, _):
                score(head, 0, sa, ma, masked=True)

                def body(j, _):
                    i = 2 * j
                    score(head, chunk(i + 1), sb, mb)
                    gather(head, chunk(i), sa, ma)
                    score(head, chunk(i + 2), sa, ma)
                    gather(head, chunk(i + 1), sb, mb)
                    return 0

                lax.fori_loop(0, count // 2, body, 0)

                @pl.when(count % 2 == 1)
                def _():
                    gather(head, chunk(count - 1), sa, ma)

                return 0

            lax.fori_loop(0, QHEADS, one_head, 0)
        else:
            score(0, 0, sa, ma)

            def one_head(head, _):
                score(head, 1, sb, mb)
                gather(head, 0, sa, ma)
                score(head, 2, sa, ma)
                gather(head, 1, sb, mb)
                score(head, 3, sb, mb)
                gather(head, 2, sa, ma)
                score(jnp.minimum(head + 1, QHEADS - 1), 0, sa, ma)
                gather(head, 3, sb, mb)
                return 0

            lax.fori_loop(0, QHEADS, one_head, 0)

        lane = lax.broadcasted_iota(jnp.int32, (TOK, HD), 1)
        for head in range(QHEADS):
            if last:
                out_ref[:, head * HD : (head + 1) * HD] = (
                    sums[head, :, :HD] / sums[head, :, HD:]
                ).astype(BF)
            else:
                out_ref[:, 2 * head * HD : (2 * head + 1) * HD] = sums[head, :, :HD]
                out_ref[:, (2 * head + 1) * HD : 2 * (head + 1) * HD] = jnp.where(
                    lane < HD // 2, sums[head, :, HD:], top[head]
                )

    if not first:

        @pl.when(count == 0)
        def _():
            if last:
                for head in range(QHEADS):
                    block = carry_ref[:, 2 * head * HD : 2 * (head + 1) * HD]
                    out_ref[:, head * HD : (head + 1) * HD] = (
                        block[:, :HD] / block[:, HD : HD + 1]
                    ).astype(BF)
            else:
                out_ref[...] = carry_ref[...]


def attend(flags, query, near, pair, carry=None, last=False):
    first = carry is None
    vmem = pl.BlockSpec(memory_space=pltpu.VMEM)
    hbm = pl.BlockSpec(memory_space=pl.ANY)
    out = (
        jax.ShapeDtypeStruct((TOK, QHEADS * HD), BF)
        if last
        else jax.ShapeDtypeStruct((TOK, 2 * QHEADS * HD), F32)
    )
    return pl.pallas_call(
        functools.partial(attend_kernel, first=first, last=last),
        in_specs=[pl.BlockSpec(memory_space=pltpu.SMEM), vmem, hbm, hbm] + ([] if first else [vmem]),
        out_specs=vmem,
        out_shape=out,
        scratch_shapes=[
            pltpu.VMEM((NZ, CHUNK, 2 * HD), BF),
            pltpu.VMEM((QHEADS, TOK, 2 * HD), F32),
            pltpu.VMEM((QHEADS, TOK, HD), F32),
            pltpu.VMEM((QHEADS, TOK, 2 * HD), BF),
            pltpu.VMEM((TOK, CHUNK), F32),
            pltpu.VMEM((TOK, CHUNK), F32),
            pltpu.VMEM((TOK, HD), F32),
            pltpu.VMEM((TOK, HD), F32),
            pltpu.SemaphoreType.DMA((2 * NZ,)),
        ],
        compiler_params=pltpu.CompilerParams(vmem_limit_bytes=40 << 20),
        cost_estimate=pl.CostEstimate(flops=14 << 30, bytes_accessed=8 << 20, transcendentals=8 << 20),
    )(flags, query, near, pair, *([] if first else [carry]))


def gathered_keys(key_heads, value_heads):
    own = jnp.concatenate([key_heads, value_heads], axis=1)
    up = along_z(own, 1)
    down = along_z(own, -1)
    two = along_z(up, 1)
    plane = jnp.stack([own, up, down, two])
    left = along_x(plane, 1, wrap=True)
    right = along_x(plane, -1, wrap=True)
    far = jnp.concatenate(
        [along_x(left[:2], 1, wrap=True), along_x(right[2:], -1, wrap=True)], axis=0
    )
    return [(part, swap_core(part)) for part in (plane, left, right, far)]


def plane_list(c, z):
    third = jnp.where(z == 3, 2, 3)
    return jnp.stack([z + 1, c, 0 * z, 0 * z + 1, third, 0 * z + 3]).astype(jnp.int32)


def local(
    hidden,
    dt_weight,
    dt_bias,
    decay_rate,
    skip_gain,
    ssm_in,
    bc_in,
    conv_x,
    conv_bc,
    gate_in,
    norm_gain,
    query_heads,
    key_heads,
    value_heads,
):
    mine = lax.axis_index("ctx")
    x, z, c = mine // (NZ * NC), (mine // NC) % NZ, mine % NC
    core = c.astype(jnp.int32)[None]
    bc = bc_in.reshape(TOK, 2 * STATE)
    ends = jnp.concatenate([ssm_in[TOK - 16 :], bc[TOK - 16 :]], axis=1)
    tail = lax.ppermute(ends, "ctx", [(i, i + 1) for i in range(31)])
    partial = lax.dot_general(
        dt_weight, hidden, (((0,), (1,)), ((), ())), preferred_element_type=F32
    )
    parts = lax.all_to_all(partial.reshape(8, HEADS, TOK), "head", 0, 0, tiled=True)
    steps = jax.nn.softplus(jnp.sum(parts, axis=0) + dt_bias[:, None])
    drop = -steps * decay_rate[:, None]
    total = jnp.sum(drop, axis=1)
    partner, chip_decay = decay_logs(total, mine)
    xin, pair, cum, logs, starts, keep, give = own_states(
        core, ssm_in, tail, bc, steps, drop, conv_x, conv_bc.reshape(4, 2 * STATE)
    )
    planes = gathered_keys(key_heads, value_heads)
    flags = [plane_list(c, z)] + [
        jnp.stack([4 * seen.astype(jnp.int32), c.astype(jnp.int32)])
        for seen in (x >= 1, x == 3, x >= 2)
    ]

    other = swap_core(give)
    by_half = lambda value: lax.dynamic_index_in_dim(value.reshape(2, 16), c, 0, False)
    shape = (16, PSIZE, STATE)
    log_first = by_half(jnp.where(c == 0, total, partner))
    log_second = by_half(jnp.where(c == 0, partner, total))
    early = jnp.where(c == 0, keep, other).reshape(shape).astype(F32)
    late = jnp.where(c == 0, other, keep).reshape(shape).astype(F32)
    both = (late + jnp.exp(log_second)[:, None, None] * early).astype(BF)
    collected = exchanged(both)
    both, xin, query = lax.optimization_barrier((both, xin, query_heads))
    y = inside_blocks(xin, pair, cum, steps, starts, jnp.repeat(skip_gain, PSIZE)[None])
    seen = attend(flags[0], query, *planes[0])
    collected, y, seen = lax.optimization_barrier((collected, y, seen))
    carried = chain(chip_decay, collected)
    chip_in = exchanged(carried)
    carried, seen = lax.optimization_barrier((carried, seen))
    seen = attend(flags[1], query, *planes[1], carry=seen)
    seen = attend(flags[2], query, *planes[2], carry=seen)
    chip_in, seen = lax.optimization_barrier((chip_in, seen))
    after = (early + jnp.exp(log_first)[:, None, None] * chip_in.astype(F32)).astype(BF)
    entering = jnp.where(c == 0, chip_in, after).reshape(CHAN // 2, STATE)
    sent = jnp.where(c == 0, after, chip_in).reshape(CHAN // 2, STATE)
    received = swap_core(sent)
    sent, seen = lax.optimization_barrier((sent, seen))
    attn_out = attend(flags[3], query, *planes[3], carry=seen, last=True)
    received, attn_out = lax.optimization_barrier((received, attn_out))
    mamba_out = finish(core, y, pair, logs, entering, received, gate_in, norm_gain[None])
    return (mamba_out, attn_out)


def solution(mesh):
    in_specs = (
        P("ctx", "head"),
        P("head", None),
        P("head"),
        P("head"),
        P("head"),
        P("ctx", "head"),
        P("ctx", "head", None),
        P(None, "head"),
        P(None, "head", None),
        P("ctx", "head"),
        P("head"),
        P("ctx", "head"),
        P("ctx", "head"),
        P("ctx", "head"),
    )
    out_specs = (P("ctx", "head"), P("ctx", "head"))
    return jax.shard_map(local, mesh=mesh, in_specs=in_specs, out_specs=out_specs, check_vma=False)
```

```python
import functools
import math

import jax
import jax.numpy as jnp
import numpy as np
from jax import lax
from jax.experimental import pallas as pl
from jax.experimental.pallas import tpu as pltpu
from jax.sharding import PartitionSpec as P

SPAN = 128
HD = 128
BF = jnp.bfloat16
F32 = jnp.float32
NX, NZ, NC = 4, 4, 2
HEADS, PSIZE, STATE = 32, 64, 256
CHAN = HEADS * PSIZE
TOK = 512
HB = 32
HBC = HB * PSIZE
CHUNK = 1024
VMEM_LIMIT = 58 << 20


def pairs_of(move):
    found = []
    for x in range(NX):
        for z in range(NZ):
            for c in range(NC):
                target = move(x, z, c)
                if target is not None:
                    tx, tz, tc = target
                    found.append(((x * NZ + z) * NC + c, (tx * NZ + tz) * NC + tc))
    return found


def send(value, move):
    return lax.ppermute(value, "ctx", pairs_of(move))


def swap_core(value):
    return send(value, lambda x, z, c: (x, z, 1 - c))


def along_z(value, steps):
    return send(value, lambda x, z, c: (x, (z + steps) % NZ, c))


def along_x(value, steps, wrap=False):
    def move(x, z, c):
        if wrap or 0 <= x + steps < NX:
            return ((x + steps) % NX, z, c)
        return None

    return send(value, move)


def shifted_rows(rows, tail, steps):
    if steps == 0:
        return rows
    rolled = pltpu.roll(rows, steps, 0)
    before = pltpu.roll(tail, steps, 0)
    at = lax.broadcasted_iota(jnp.int32, before.shape, 0)
    top = jnp.where(at < steps, before, rolled[:8])
    return jnp.concatenate([top, rolled[8:]], axis=0)


def conv_silu(rows, tail, taps):
    taps_count = taps.shape[0]
    total = None
    for k in range(taps_count):
        term = taps[k : k + 1] * shifted_rows(rows, tail, taps_count - 1 - k)
        total = term if total is None else total + term
    return (total * jax.nn.sigmoid(total)).astype(BF)


def two_parts(value):
    high = value.astype(BF).astype(F32)
    return [high, (value - high).astype(BF).astype(F32)]


def three_parts(value):
    high = value.astype(BF).astype(F32)
    return [high] + two_parts(value - high)


def conv_kernel(
    x_ref, before_ref, xtail_ref, pair_ref, pbefore_ref, ptail_ref, taps_ref, ptaps_ref, xin_ref, conv_ref
):
    first = pl.program_id(0) == 0
    before = jnp.where(first, ptail_ref[...], pbefore_ref[...]).astype(F32)[8:]
    conv_ref[...] = conv_silu(pair_ref[...].astype(F32), before, ptaps_ref[...])
    before = jnp.where(first, xtail_ref[...], before_ref[...]).astype(F32)[8:]
    xin_ref[...] = conv_silu(x_ref[...].astype(F32), before, taps_ref[...])


def convolved(ssm_in, tail, bc_in, conv_x, conv_bc):
    prior = lambda s: (jnp.maximum(s * (SPAN // 16) - 1, 0), 0)
    return pl.pallas_call(
        conv_kernel,
        grid=(TOK // SPAN,),
        in_specs=[
            pl.BlockSpec((SPAN, CHAN), lambda s: (s, 0)),
            pl.BlockSpec((16, CHAN), prior),
            pl.BlockSpec((16, CHAN), lambda s: (0, 0)),
            pl.BlockSpec((SPAN, 2 * STATE), lambda s: (s, 0)),
            pl.BlockSpec((16, 2 * STATE), prior),
            pl.BlockSpec((16, 2 * STATE), lambda s: (0, CHAN // (2 * STATE))),
            pl.BlockSpec((4, CHAN), lambda s: (0, 0)),
            pl.BlockSpec((4, 2 * STATE), lambda s: (0, 0)),
        ],
        out_specs=[
            pl.BlockSpec((SPAN, CHAN), lambda s: (s, 0)),
            pl.BlockSpec((SPAN, 2 * STATE), lambda s: (s, 0)),
        ],
        out_shape=[
            jax.ShapeDtypeStruct((TOK, CHAN), BF),
            jax.ShapeDtypeStruct((TOK, 2 * STATE), BF),
        ],
        compiler_params=pltpu.CompilerParams(vmem_limit_bytes=VMEM_LIMIT),
        cost_estimate=pl.CostEstimate(flops=1 << 20, bytes_accessed=1 << 16, transcendentals=0),
    )(ssm_in, ssm_in, tail, bc_in, bc_in, tail, conv_x, conv_bc)


def states_kernel(
    core_ref,
    xin_ref,
    pair_ref,
    steps_ref,
    drop_ref,
    spread_ref,
    rows_ref,
    cum_ref,
    log_ref,
    start_ref,
    mine_ref,
    give_ref,
    log_s,
    state_s,
):
    span = pl.program_id(0)

    @pl.when(span == 0)
    def _():
        log_s[...] = jnp.zeros_like(log_s)
        state_s[...] = jnp.zeros_like(state_s)

    at_i = lax.broadcasted_iota(jnp.int32, (SPAN, SPAN), 0)
    at_j = lax.broadcasted_iota(jnp.int32, (SPAN, SPAN), 1)
    upper = jnp.where(at_i <= at_j, 1.0, 0.0)
    cum = jnp.dot(
        drop_ref[...], upper, precision=lax.Precision.HIGHEST, preferred_element_type=F32
    )
    cum_ref[...] = cum
    last = cum[:, SPAN - 1 : SPAN]
    scales = jnp.concatenate(
        two_parts(jnp.exp(last - cum) * steps_ref[...]) + [jnp.zeros((2 * HEADS, SPAN), F32)], axis=0
    ).T.astype(BF)
    decays = jnp.broadcast_to(
        jnp.concatenate(two_parts(jnp.exp(last)), axis=0), (2 * HEADS, STATE)
    ).astype(BF)
    log_ref[...] = log_s[...] + cum
    log_s[...] = log_s[...] + last
    spread = spread_ref[...]
    weight = jnp.dot(
        scales, jnp.concatenate([spread, jnp.zeros_like(spread)], axis=0), preferred_element_type=F32
    )
    weighted = (xin_ref[...].astype(F32) * weight).astype(BF)
    gain = lax.dot_general(
        weighted, pair_ref[...], (((0,), (0,)), ((), ())), preferred_element_type=F32
    )
    decay = jnp.dot(rows_ref[...], decays, preferred_element_type=F32)
    state = state_s[...]
    start_ref[...] = state.astype(BF)
    state = state * decay + gain
    state_s[...] = state

    @pl.when(span == TOK // SPAN - 1)
    def _():
        low = state.astype(BF)
        first = core_ref[0] == 0
        mine_ref[...] = jnp.where(first, low[: CHAN // 2], low[CHAN // 2 :])
        give_ref[: CHAN // 2, :] = jnp.where(first, low[CHAN // 2 :], low[: CHAN // 2])
        parts = three_parts(log_s[...]) + [jnp.zeros((HEADS, SPAN), F32)]
        rows = jnp.concatenate(parts, axis=0).T[:16].astype(BF)
        give_ref[CHAN // 2 :, :] = jnp.concatenate([rows, jnp.zeros_like(rows)], axis=1)


def spread_rows():
    spread = np.zeros((2 * HEADS, CHAN), np.float32)
    for h in range(HEADS):
        for part in range(2):
            spread[part * HEADS + h, h * PSIZE : (h + 1) * PSIZE] = 1
    return spread


def own_states(core, xin, pair, steps, drop):
    spread = spread_rows()
    return pl.pallas_call(
        states_kernel,
        grid=(TOK // SPAN,),
        in_specs=[
            pl.BlockSpec(memory_space=pltpu.SMEM),
            pl.BlockSpec((SPAN, CHAN), lambda s: (s, 0)),
            pl.BlockSpec((SPAN, STATE), lambda s: (s, 0)),
            pl.BlockSpec((HEADS, SPAN), lambda s: (0, s)),
            pl.BlockSpec((HEADS, SPAN), lambda s: (0, s)),
            pl.BlockSpec((2 * HEADS, CHAN), lambda s: (0, 0)),
            pl.BlockSpec((CHAN, 2 * HEADS), lambda s: (0, 0)),
        ],
        out_specs=[
            pl.BlockSpec((HEADS, SPAN), lambda s: (0, s)),
            pl.BlockSpec((HEADS, SPAN), lambda s: (0, s)),
            pl.BlockSpec((CHAN, STATE), lambda s: (s, 0)),
            pl.BlockSpec((CHAN // 2, STATE), lambda s: (0, 0)),
            pl.BlockSpec((CHAN // 2 + 16, STATE), lambda s: (0, 0)),
        ],
        out_shape=[
            jax.ShapeDtypeStruct((HEADS, TOK), F32),
            jax.ShapeDtypeStruct((HEADS, TOK), F32),
            jax.ShapeDtypeStruct((TOK // SPAN * CHAN, STATE), BF),
            jax.ShapeDtypeStruct((CHAN // 2, STATE), BF),
            jax.ShapeDtypeStruct((CHAN // 2 + 16, STATE), BF),
        ],
        scratch_shapes=[
            pltpu.VMEM((HEADS, SPAN), F32),
            pltpu.VMEM((CHAN, STATE), F32),
        ],
        compiler_params=pltpu.CompilerParams(vmem_limit_bytes=VMEM_LIMIT),
        cost_estimate=pl.CostEstimate(flops=1 << 20, bytes_accessed=1 << 16, transcendentals=0),
    )(core, xin, pair, steps, drop, jnp.asarray(spread, BF), jnp.asarray(spread.T, BF))


def inside_kernel(
    xin_ref,
    pair_ref,
    cum_ref,
    steps_ref,
    start_ref,
    skip_ref,
    spread_ref,
    column_ref,
    y_ref,
    g_s,
    ci_s,
    ex_s,
):
    block = pl.program_id(1)
    cmat = pair_ref[:, STATE:]

    @pl.when(block == 0)
    def _():
        product = lax.dot_general(
            cmat, pair_ref[:, :STATE], (((1,), (1,)), ((), ())), preferred_element_type=F32
        )
        at_i = lax.broadcasted_iota(jnp.int32, (SPAN, SPAN), 0)
        at_j = lax.broadcasted_iota(jnp.int32, (SPAN, SPAN), 1)
        g_s[...] = jnp.where(at_j <= at_i, product, 0.0)
        cum = cum_ref[...]
        ci_s[...] = jnp.concatenate(three_parts(cum) + [jnp.zeros_like(cum)], axis=0).T.astype(BF)
        ex_s[...] = jnp.concatenate(
            two_parts(jnp.exp(cum)) + [jnp.zeros((2 * HEADS, SPAN), F32)], axis=0
        ).T.astype(BF)

    xf = xin_ref[...].astype(F32)
    spread = spread_ref[...]
    grown = jnp.dot(
        ex_s[...], jnp.concatenate([spread, jnp.zeros_like(spread)], axis=0), preferred_element_type=F32
    )
    rows_i = jnp.dot(ci_s[...], column_ref[...], preferred_element_type=F32)
    read = lax.dot_general(
        cmat, start_ref[...], (((1,), (1,)), ((), ())), preferred_element_type=F32
    )
    base = read * grown + skip_ref[...] * xf
    cum_rows = cum_ref[pl.ds(pl.multiple_of(block * HB, HB), HB), :]
    step_rows = steps_ref[pl.ds(pl.multiple_of(block * HB, HB), HB), :]
    masked = g_s[...]
    lane = lax.broadcasted_iota(jnp.int32, (SPAN, 2 * PSIZE), 1)
    for pair in range(HB // 2):
        mixes = []
        for h in (2 * pair, 2 * pair + 1):
            gap = rows_i[:, h * SPAN : (h + 1) * SPAN] - cum_rows[h : h + 1]
            mixes.append(
                (masked * jnp.exp(jnp.minimum(gap, 0.0)) * step_rows[h : h + 1]).astype(BF)
            )
        two = xf[:, pair * 128 : (pair + 1) * 128]
        left = jnp.where(lane < PSIZE, two, 0.0).astype(BF)
        right = jnp.where(lane < PSIZE, 0.0, two).astype(BF)
        intra = jnp.dot(
            jnp.concatenate(mixes, axis=1),
            jnp.concatenate([left, right], axis=0),
            preferred_element_type=F32,
        )
        y_ref[:, pair * 128 : (pair + 1) * 128] = (
            base[:, pair * 128 : (pair + 1) * 128] + intra
        ).astype(BF)


def inside_blocks(xin, pair, cum, steps, starts, skip):
    column = np.zeros((4 * HEADS, HEADS * SPAN), np.float32)
    for h in range(HEADS):
        for part in range(3):
            column[part * HEADS + h, h * SPAN : (h + 1) * SPAN] = 1
    blocks = HEADS // HB
    return pl.pallas_call(
        inside_kernel,
        grid=(TOK // SPAN, blocks),
        in_specs=[
            pl.BlockSpec((SPAN, HBC), lambda s, b: (s, b)),
            pl.BlockSpec((SPAN, 2 * STATE), lambda s, b: (s, 0)),
            pl.BlockSpec((HEADS, SPAN), lambda s, b: (0, s)),
            pl.BlockSpec((HEADS, SPAN), lambda s, b: (0, s)),
            pl.BlockSpec((HBC, STATE), lambda s, b: (s * blocks + b, 0)),
            pl.BlockSpec((1, HBC), lambda s, b: (0, b)),
            pl.BlockSpec((2 * HEADS, HBC), lambda s, b: (0, b)),
            pl.BlockSpec((4 * HEADS, HB * SPAN), lambda s, b: (0, b)),
        ],
        out_specs=pl.BlockSpec((SPAN, HBC), lambda s, b: (s, b)),
        out_shape=jax.ShapeDtypeStruct((TOK, CHAN), BF),
        scratch_shapes=[
            pltpu.VMEM((SPAN, SPAN), F32),
            pltpu.VMEM((SPAN, 4 * HEADS), BF),
            pltpu.VMEM((SPAN, 4 * HEADS), BF),
        ],
        compiler_params=pltpu.CompilerParams(vmem_limit_bytes=VMEM_LIMIT),
        cost_estimate=pl.CostEstimate(flops=1 << 34, bytes_accessed=1 << 16, transcendentals=0),
    )(xin, pair, cum, steps, starts, skip, jnp.asarray(spread_rows(), BF), jnp.asarray(column, BF))


CHIPS = NX * NZ
SAME_CORE = [[2 * chip + core for chip in range(CHIPS)] for core in range(NC)]


def chain_kernel(from_ref, into_ref):
    carried = jnp.zeros((PSIZE, STATE), F32)
    for chip in range(CHIPS):
        into_ref[chip] = carried.astype(BF)
        if chip < CHIPS - 1:
            parts = from_ref[chip, PSIZE:, :].astype(F32)
            decay = jnp.exp(parts[0:1] + parts[1:2] + parts[2:3])
            carried = decay * carried + from_ref[chip, :PSIZE, :].astype(F32)


def chain(states):
    return pl.pallas_call(
        chain_kernel,
        in_specs=[pl.BlockSpec(memory_space=pltpu.VMEM)],
        out_specs=pl.BlockSpec(memory_space=pltpu.VMEM),
        out_shape=jax.ShapeDtypeStruct((CHIPS, PSIZE, STATE), BF),
        cost_estimate=pl.CostEstimate(flops=1 << 20, bytes_accessed=1 << 16, transcendentals=0),
    )(states)


def with_logs(states, logs):
    parts = [part[:, None, None] for part in three_parts(logs)]
    row = lax.broadcasted_iota(jnp.int32, (16, 16, STATE), 1)
    extra = jnp.where(
        row == 0, parts[0], jnp.where(row == 1, parts[1], jnp.where(row == 2, parts[2], 0.0))
    )
    return jnp.concatenate([states, extra], axis=1).astype(BF)


def exchanged(value):
    return lax.all_to_all(value, "ctx", 0, 0, tiled=True, axis_index_groups=SAME_CORE)


def finish_kernel(
    core_ref, y_ref, c_ref, log_ref, in_ref, other_ref, gate_ref, gain_ref, spread_ref, out_ref
):
    grown = jnp.concatenate(
        two_parts(jnp.exp(log_ref[...])) + [jnp.zeros((2 * HEADS, SPAN), F32)], axis=0
    ).T.astype(BF)
    spread = spread_ref[...]
    scale = jnp.dot(
        grown, jnp.concatenate([spread, jnp.zeros_like(spread)], axis=0), preferred_element_type=F32
    )
    contract = (((1,), (1,)), ((), ()))
    kept = lax.dot_general(c_ref[...], in_ref[...], contract, preferred_element_type=F32)
    given = lax.dot_general(c_ref[...], other_ref[...], contract, preferred_element_type=F32)
    first = core_ref[0] == 0
    read = jnp.concatenate(
        [jnp.where(first, kept, given), jnp.where(first, given, kept)], axis=1
    )
    mixed = y_ref[...].astype(F32) + read * scale
    gate = gate_ref[...].astype(F32)
    gated = mixed * (gate * jax.nn.sigmoid(gate))
    mean = jnp.mean(gated * gated, axis=1, keepdims=True)
    out_ref[...] = (gated * lax.rsqrt(mean + 1e-05) * gain_ref[...]).astype(BF)


def finish(core, y, pair, logs, entering, other, gate, gain):
    return pl.pallas_call(
        finish_kernel,
        grid=(TOK // SPAN,),
        in_specs=[
            pl.BlockSpec(memory_space=pltpu.SMEM),
            pl.BlockSpec((SPAN, CHAN), lambda s: (s, 0)),
            pl.BlockSpec((SPAN, STATE), lambda s: (s, 1)),
            pl.BlockSpec((HEADS, SPAN), lambda s: (0, s)),
            pl.BlockSpec((CHAN // 2, STATE), lambda s: (0, 0)),
            pl.BlockSpec((CHAN // 2, STATE), lambda s: (0, 0)),
            pl.BlockSpec((SPAN, CHAN), lambda s: (s, 0)),
            pl.BlockSpec((1, CHAN), lambda s: (0, 0)),
            pl.BlockSpec((2 * HEADS, CHAN), lambda s: (0, 0)),
        ],
        out_specs=pl.BlockSpec((SPAN, CHAN), lambda s: (s, 0)),
        out_shape=jax.ShapeDtypeStruct((TOK, CHAN), BF),
        compiler_params=pltpu.CompilerParams(vmem_limit_bytes=VMEM_LIMIT),
        cost_estimate=pl.CostEstimate(flops=1 << 20, bytes_accessed=1 << 16, transcendentals=0),
    )(core, y, pair, logs, entering, other, gate, gain, jnp.asarray(spread_rows(), BF))


QHEADS = 4
SUB = 256


def attend_kernel(flag_ref, q_ref, *refs, planes, own, fresh):
    pieces, refs = refs[: 2 * planes], refs[2 * planes :]
    if not fresh:
        in_sums, in_top, *refs = refs
    if own:
        out_sums, out_top, *refs = refs
    else:
        part_ref, *refs = refs
    kv, sums, top, qq, sa, sb, ma, mb, key_sem, in_sem, out_sem = refs
    count = flag_ref[0]
    third = flag_ref[1]
    core = flag_ref[2]

    def carried(head):
        return (
            pltpu.make_async_copy(in_sums.at[head], sums.at[head], in_sem.at[0, head]),
            pltpu.make_async_copy(in_top.at[head], top.at[head], in_sem.at[1, head]),
        )

    def leaving(head):
        return (
            pltpu.make_async_copy(sums.at[head], out_sums.at[head], out_sem.at[0, head]),
            pltpu.make_async_copy(top.at[head], out_top.at[head], out_sem.at[1, head]),
        )

    def keys(p):
        slots = pl.ds(p * NZ, NZ)
        return (
            pltpu.make_async_copy(pieces[2 * p], kv.at[slots, 0], key_sem.at[p, 0]),
            pltpu.make_async_copy(pieces[2 * p + 1], kv.at[slots, 1], key_sem.at[p, 1]),
        )

    def score(head, at, s_ref, m_ref, masked=False):
        rows_in = kv[at, :, :, :HD].reshape(CHUNK, HD)
        twice = jnp.concatenate([rows_in, rows_in], axis=1)
        for r in range(TOK // SUB):
            rows = slice(r * SUB, (r + 1) * SUB)
            s = lax.dot_general(
                qq[head, rows, :], twice, (((1,), (1,)), ((), ())), preferred_element_type=F32
            )
            if masked:
                row = lax.broadcasted_iota(jnp.int32, s.shape, 0) + r * SUB
                key = lax.broadcasted_iota(jnp.int32, s.shape, 1)
                limit = jnp.where(core == 1, 2 * TOK, TOK)
                seen = ((key < TOK) & (key <= row)) | ((key >= TOK) & (key < limit))
                s = jnp.where(seen, s, -1e30)
            s_ref[rows, :] = s
            m_ref[rows, :] = jnp.broadcast_to(jnp.max(s, axis=1, keepdims=True), (SUB, HD))

    def gather(head, at, s_ref, m_ref):
        values = kv[at, :, :, HD:].reshape(CHUNK, HD)
        values = jnp.concatenate([values, jnp.ones((CHUNK, HD), BF)], axis=1)
        for r in range(TOK // SUB):
            rows = slice(r * SUB, (r + 1) * SUB)
            old = top[head, rows, :]
            new = jnp.maximum(old, m_ref[rows, :])
            weights = jnp.exp2(s_ref[rows, :] - new[:, :1]).astype(BF)
            factor = jnp.exp2(old - new)
            part = jnp.dot(weights, values, preferred_element_type=F32)
            sums[head, rows, :] = (
                sums[head, rows, :] * jnp.concatenate([factor, factor], axis=1) + part
            )
            top[head, rows, :] = new

    if not fresh:
        for head in range(QHEADS):
            for copy in carried(head):
                copy.start()

    @pl.when(count > 0)
    def _():
        for p in range(planes):

            @pl.when(own | (p < count))
            def _():
                for copy in keys(p):
                    copy.start()

        for head in range(QHEADS):
            scaled = q_ref[:, head * HD : (head + 1) * HD].astype(F32) * (HD**-0.5 * math.log2(math.e))
            high = scaled.astype(BF)
            low = (scaled - high.astype(F32)).astype(BF)
            qq[head] = jnp.concatenate([high, low], axis=1)
            if fresh:
                sums[head] = jnp.zeros((TOK, 2 * HD), F32)
                top[head] = jnp.full((TOK, HD), -1e30, F32)
        for p in range(planes):

            @pl.when(own | (p < count))
            def _():
                for copy in keys(p):
                    copy.wait()

        if own:
            def chunk(i):
                return jnp.where(i == 2, third, jnp.minimum(i, NZ - 1))

            def one_head(head, _):
                score(head, 0, sa, ma, masked=True)

                def body(j, _):
                    i = 2 * j
                    score(head, chunk(i + 1), sb, mb)
                    gather(head, chunk(i), sa, ma)
                    score(head, chunk(i + 2), sa, ma)
                    gather(head, chunk(i + 1), sb, mb)
                    return 0

                lax.fori_loop(0, count // 2, body, 0)

                @pl.when(count % 2 == 1)
                def _():
                    gather(head, chunk(count - 1), sa, ma)

                for copy in leaving(head):
                    copy.start()
                return 0

            def full_head(head, _):
                score(head, 1, sb, mb)
                gather(head, 0, sa, ma)
                score(head, 2, sa, ma)
                gather(head, 1, sb, mb)
                score(head, 3, sb, mb)
                gather(head, 2, sa, ma)
                score(jnp.minimum(head + 1, QHEADS - 1), 0, sa, ma, masked=True)
                gather(head, 3, sb, mb)
                for copy in leaving(head):
                    copy.start()
                return 0

            @pl.when(count == NZ)
            def _():
                score(0, 0, sa, ma, masked=True)
                lax.fori_loop(0, QHEADS, full_head, 0)

            @pl.when(count < NZ)
            def _():
                lax.fori_loop(0, QHEADS, one_head, 0)

            for head in range(QHEADS):
                for copy in leaving(head):
                    copy.wait()
        else:
            steps = 2 * count

            def where_at(step):
                head = step // steps
                return jnp.minimum(head, QHEADS - 1), 2 * (step - head * steps)

            score(0, 0, sa, ma)

            def body(step, _):
                head, at = where_at(step)
                if not fresh:

                    @pl.when(at == 0)
                    def _():
                        for copy in carried(head):
                            copy.wait()

                score(head, at + 1, sb, mb)
                gather(head, at, sa, ma)
                score(*where_at(step + 1), sa, ma)
                gather(head, at + 1, sb, mb)
                return 0

            lax.fori_loop(0, QHEADS * steps, body, 0)

    if not own:
        if not fresh:

            @pl.when(count == 0)
            def _():
                for head in range(QHEADS):
                    for copy in carried(head):
                        copy.wait()

        @pl.when(jnp.logical_or(count > 0, not fresh))
        def _():
            lane = lax.broadcasted_iota(jnp.int32, (TOK, HD), 1)
            log = jnp.zeros((TOK, HD), F32)
            for head in range(QHEADS):
                total = sums[head, :, HD:]
                part_ref[:, head * HD : (head + 1) * HD] = (sums[head, :, :HD] / total).astype(BF)
                for at, part in enumerate(three_parts(top[head] + jnp.log2(total))):
                    log = jnp.where(lane == 32 * head + at, part, log)
            part_ref[:, QHEADS * HD :] = log.astype(BF)


def attend(flags, query, *pieces, carry=None, own=False):
    fresh = carry is None
    planes = len(pieces) // 2
    vmem = pl.BlockSpec(memory_space=pltpu.VMEM)
    hbm = pl.BlockSpec(memory_space=pl.ANY)
    if own:
        out = [
            jax.ShapeDtypeStruct((QHEADS, TOK, 2 * HD), F32),
            jax.ShapeDtypeStruct((QHEADS, TOK, HD), F32),
        ]
        out_specs = [hbm, hbm]
    else:
        out, out_specs = jax.ShapeDtypeStruct((TOK, (QHEADS + 1) * HD), BF), vmem
    return pl.pallas_call(
        functools.partial(attend_kernel, planes=planes, own=own, fresh=fresh),
        in_specs=[pl.BlockSpec(memory_space=pltpu.SMEM), vmem]
        + [hbm] * len(pieces)
        + ([] if fresh else [hbm, hbm]),
        out_specs=out_specs,
        out_shape=out,
        scratch_shapes=[
            pltpu.VMEM((planes * NZ, NC, TOK, 2 * HD), BF),
            pltpu.VMEM((QHEADS, TOK, 2 * HD), F32),
            pltpu.VMEM((QHEADS, TOK, HD), F32),
            pltpu.VMEM((QHEADS, TOK, 2 * HD), BF),
            pltpu.VMEM((TOK, CHUNK), F32),
            pltpu.VMEM((TOK, CHUNK), F32),
            pltpu.VMEM((TOK, HD), F32),
            pltpu.VMEM((TOK, HD), F32),
            pltpu.SemaphoreType.DMA((planes, 2)),
            pltpu.SemaphoreType.DMA((2, QHEADS)),
            pltpu.SemaphoreType.DMA((2, QHEADS)),
        ],
        compiler_params=pltpu.CompilerParams(vmem_limit_bytes=VMEM_LIMIT),
        cost_estimate=pl.CostEstimate(
            flops=1 << 35 if fresh and not own else 1 << 20, bytes_accessed=1 << 16, transcendentals=0
        ),
    )(flags, query, *pieces, *([] if fresh else carry))


def merge_kernel(flag_ref, mine_ref, other_ref, out_ref):
    row = lax.broadcasted_iota(jnp.int32, (HD, HD), 0)
    with_other = flag_ref[0] > 0
    logs = [ref[:, QHEADS * HD :] for ref in (mine_ref, other_ref)]
    for head in range(QHEADS):
        pick = jnp.where((row >= 32 * head) & (row < 32 * head + 3), 1.0, 0.0).astype(BF)
        mine, other = [jnp.dot(log, pick, preferred_element_type=F32) for log in logs]
        other = jnp.where(with_other, other, -1e30)
        new = jnp.maximum(mine, other)
        mine, other = jnp.exp2(mine - new), jnp.exp2(other - new)
        columns = slice(head * HD, (head + 1) * HD)
        joint = mine_ref[:, columns].astype(F32) * mine + other_ref[:, columns].astype(F32) * other
        out_ref[:, columns] = (joint / (mine + other)).astype(BF)


def merge(flags, part, other):
    rows = TOK // 2
    wide = pl.BlockSpec((rows, (QHEADS + 1) * HD), lambda r: (r, 0))
    return pl.pallas_call(
        merge_kernel,
        grid=(TOK // rows,),
        in_specs=[pl.BlockSpec(memory_space=pltpu.SMEM), wide, wide],
        out_specs=pl.BlockSpec((rows, QHEADS * HD), lambda r: (r, 0)),
        out_shape=jax.ShapeDtypeStruct((TOK, QHEADS * HD), BF),
        compiler_params=pltpu.CompilerParams(vmem_limit_bytes=VMEM_LIMIT),
        cost_estimate=pl.CostEstimate(flops=1 << 20, bytes_accessed=1 << 16, transcendentals=0),
    )(flags, part, other)


def local(
    hidden,
    dt_weight,
    dt_bias,
    decay_rate,
    skip_gain,
    ssm_in,
    bc_in,
    conv_x,
    conv_bc,
    gate_in,
    norm_gain,
    query_heads,
    key_heads,
    value_heads,
):
    mine = lax.axis_index("ctx")
    x, z, c = mine // (NZ * NC), (mine // NC) % NZ, mine % NC
    core = c.astype(jnp.int32)[None]

    def flags(count):
        return jnp.stack([count, jnp.where(z == NZ - 1, 2, 3), c]).astype(jnp.int32)

    bc = bc_in.reshape(TOK, 2 * STATE)
    ends = jnp.concatenate([ssm_in[TOK - 16 :], bc[TOK - 16 :]], axis=1)
    tail = lax.ppermute(ends, "ctx", [(i, i + 1) for i in range(31)])
    partial = lax.dot_general(
        dt_weight, hidden, (((0,), (1,)), ((), ())), preferred_element_type=F32
    )
    partial, tail, keys, query = lax.optimization_barrier((partial, tail, key_heads, query_heads))
    parts = lax.all_to_all(partial.reshape(8, HEADS, TOK), "head", 0, 0, tiled=True)
    xin, pair = convolved(ssm_in, tail, bc, conv_x, conv_bc.reshape(4, 2 * STATE))
    rows = jnp.concatenate([keys, value_heads], axis=1)
    up, down = along_z(rows, 1), along_z(rows, -1)
    visitor = send(query, lambda x, z, c: (x - 1, z, c) if x >= 2 else None)
    parts, xin, pair = lax.optimization_barrier((parts, xin, pair))
    steps = jax.nn.softplus(jnp.sum(parts, axis=0) + dt_bias[:, None])
    drop = -steps * decay_rate[:, None]
    total = jnp.sum(drop, axis=1)
    cum, logs, starts, keep, give = own_states(core, xin, pair, steps, drop)

    keep, give, up, down, visitor = lax.optimization_barrier((keep, give, up, down, visitor))
    other = swap_core(give)
    partner = jnp.sum(other[CHAN // 2, : 3 * HEADS].astype(F32).reshape(3, HEADS), axis=0)
    other = other[: CHAN // 2]
    by_half = lambda value: lax.dynamic_index_in_dim(value.reshape(2, 16), c, 0, False)
    shape = (16, PSIZE, STATE)
    log_first = by_half(jnp.where(c == 0, total, partner))
    log_second = by_half(jnp.where(c == 0, partner, total))
    early = jnp.where(c == 0, keep, other).reshape(shape).astype(F32)
    late = jnp.where(c == 0, other, keep).reshape(shape).astype(F32)
    both = with_logs(
        late + jnp.exp(log_second)[:, None, None] * early, log_first + log_second
    )
    collected = exchanged(both)
    both, xin, rows, up, down, visitor = lax.optimization_barrier(
        (both, xin, rows, up, down, visitor)
    )
    middle = TOK // 2
    two = [along_z(up[:middle], 1), along_z(down[middle:], -1)]
    visitor = send(visitor, lambda x, z, c: (x - 1, z, c) if x in (1, 2) else None)
    y = inside_blocks(xin, pair, cum, steps, starts, jnp.repeat(skip_gain, PSIZE)[None])
    plane = jnp.stack([rows, up, down, jnp.concatenate(two, axis=0)])
    plane_pair = swap_core(plane)
    left = along_x(plane, 1)
    right = send(plane, lambda x, z, c: (NX - 1, z, c) if x == 0 else None)
    seen = attend(flags(z + 1), query, plane, plane_pair, own=True)
    collected, y, seen = lax.optimization_barrier((collected, y, seen))
    carried = chain(collected)
    chip_in = exchanged(carried)
    planes_seen = jnp.where(x == 0, 0, jnp.where(x == NX - 1, 2, 1))
    carried, to_visit, to_see, visitor, left, right = lax.optimization_barrier(
        (carried, flags(jnp.where(x <= 1, 1, 0)), flags(planes_seen), visitor, left, right)
    )
    left_pair = swap_core(left)
    right_pair = swap_core(right)
    part = attend(to_visit, visitor, plane, plane_pair)
    part, to_see = lax.optimization_barrier((part, to_see))
    part = send(part, lambda x, z, c: (x + 2, z, c) if x <= 1 else None)
    seen = attend(to_see, query, left, left_pair, right, right_pair, carry=seen)
    chip_in, seen = lax.optimization_barrier((chip_in, seen))
    after = (early + jnp.exp(log_first)[:, None, None] * chip_in.astype(F32)).astype(BF)
    entering = jnp.where(c == 0, chip_in, after).reshape(CHAN // 2, STATE)
    sent = jnp.where(c == 0, after, chip_in).reshape(CHAN // 2, STATE)
    received = swap_core(sent)
    sent, seen = lax.optimization_barrier((sent, seen))
    attn_out = merge(flags(jnp.where(x >= 2, 1, 0)), seen, part)
    received, attn_out = lax.optimization_barrier((received, attn_out))
    mamba_out = finish(core, y, pair, logs, entering, received, gate_in, norm_gain[None])
    return (mamba_out, attn_out)


def solution(mesh):
    in_specs = (
        P("ctx", "head"),
        P("head", None),
        P("head"),
        P("head"),
        P("head"),
        P("ctx", "head"),
        P("ctx", "head", None),
        P(None, "head"),
        P(None, "head", None),
        P("ctx", "head"),
        P("head"),
        P("ctx", "head"),
        P("ctx", "head"),
        P("ctx", "head"),
    )
    out_specs = (P("ctx", "head"), P("ctx", "head"))
    return jax.shard_map(local, mesh=mesh, in_specs=in_specs, out_specs=out_specs, check_vma=False)
```

```python
import functools
import math

import jax
import jax.numpy as jnp
from jax import lax
from jax.experimental import pallas as pl
from jax.experimental.pallas import tpu as pltpu
from jax.sharding import PartitionSpec as P

SPAN = 128
HD = 128
BF = jnp.bfloat16
F32 = jnp.float32
NX, NZ, NC = 4, 4, 2
HEADS, PSIZE, STATE = 32, 64, 256
CHAN = HEADS * PSIZE
TOK = 512
HB = 32
HBC = HB * PSIZE
CHUNK = 1024
VMEM_LIMIT = 58 << 20
ATTEND_LIMIT = 28 << 20
CONV_ROWS = 256
END_ROWS = 256


def pairs_of(move):
    found = []
    for x in range(NX):
        for z in range(NZ):
            for c in range(NC):
                target = move(x, z, c)
                if target is not None:
                    tx, tz, tc = target
                    found.append(((x * NZ + z) * NC + c, (tx * NZ + tz) * NC + tc))
    return found


def send(value, move):
    return lax.ppermute(value, "ctx", pairs_of(move))


def swap_core(value):
    return send(value, lambda x, z, c: (x, z, 1 - c))


def along_z(value, steps):
    return send(value, lambda x, z, c: (x, (z + steps) % NZ, c))


def along_x(value, steps, wrap=False):
    def move(x, z, c):
        if wrap or 0 <= x + steps < NX:
            return ((x + steps) % NX, z, c)
        return None

    return send(value, move)


def shifted_rows(rows, tail, steps):
    if steps == 0:
        return rows
    rolled = pltpu.roll(rows, steps, 0)
    before = pltpu.roll(tail, steps, 0)
    at = lax.broadcasted_iota(jnp.int32, before.shape, 0)
    top = jnp.where(at < steps, before, rolled[:8])
    return jnp.concatenate([top, rolled[8:]], axis=0)


def conv_silu(rows, tail, taps):
    taps_count = taps.shape[0]
    total = None
    for k in range(taps_count):
        term = taps[k : k + 1] * shifted_rows(rows, tail, taps_count - 1 - k)
        total = term if total is None else total + term
    return (total * jax.nn.sigmoid(total)).astype(BF)


def two_parts(value):
    high = value.astype(BF).astype(F32)
    return [high, (value - high).astype(BF).astype(F32)]


def three_parts(value):
    high = value.astype(BF).astype(F32)
    return [high] + two_parts(value - high)


def conv_kernel(
    x_ref, before_ref, xtail_ref, pair_ref, pbefore_ref, ptail_ref, taps_ref, ptaps_ref, xin_ref, conv_ref
):
    first = pl.program_id(0) == 0
    before = jnp.where(first, ptail_ref[...], pbefore_ref[...]).astype(F32)[8:]
    conv_ref[...] = conv_silu(pair_ref[...].astype(F32), before, ptaps_ref[...])
    before = jnp.where(first, xtail_ref[...], before_ref[...]).astype(F32)[8:]
    xin_ref[...] = conv_silu(x_ref[...].astype(F32), before, taps_ref[...])


def convolved(ssm_in, tail, bc_in, conv_x, conv_bc):
    prior = lambda s: (jnp.maximum(s * (CONV_ROWS // 16) - 1, 0), 0)
    return pl.pallas_call(
        conv_kernel,
        grid=(TOK // CONV_ROWS,),
        in_specs=[
            pl.BlockSpec((CONV_ROWS, CHAN), lambda s: (s, 0)),
            pl.BlockSpec((16, CHAN), prior),
            pl.BlockSpec((16, CHAN), lambda s: (0, 0)),
            pl.BlockSpec((CONV_ROWS, 2 * STATE), lambda s: (s, 0)),
            pl.BlockSpec((16, 2 * STATE), prior),
            pl.BlockSpec((16, 2 * STATE), lambda s: (0, CHAN // (2 * STATE))),
            pl.BlockSpec((4, CHAN), lambda s: (0, 0)),
            pl.BlockSpec((4, 2 * STATE), lambda s: (0, 0)),
        ],
        out_specs=[
            pl.BlockSpec((CONV_ROWS, CHAN), lambda s: (s, 0)),
            pl.BlockSpec((CONV_ROWS, 2 * STATE), lambda s: (s, 0)),
        ],
        out_shape=[
            jax.ShapeDtypeStruct((TOK, CHAN), BF),
            jax.ShapeDtypeStruct((TOK, 2 * STATE), BF),
        ],
        compiler_params=pltpu.CompilerParams(vmem_limit_bytes=VMEM_LIMIT),
        cost_estimate=pl.CostEstimate(flops=1 << 20, bytes_accessed=1 << 16, transcendentals=0),
    )(ssm_in, ssm_in, tail, bc_in, bc_in, tail, conv_x, conv_bc)


def states_kernel(
    core_ref,
    xin_ref,
    pair_ref,
    steps_ref,
    drop_ref,
    cum_ref,
    log_ref,
    read_ref,
    mine_ref,
    give_ref,
    log_s,
    state_s,
    spread_s,
    rows_s,
):
    span = pl.program_id(0)

    @pl.when(span == 0)
    def _():
        log_s[...] = jnp.zeros_like(log_s)
        state_s[...] = jnp.zeros_like(state_s)
        spread_s[...] = spread_heads()
        channel = lax.broadcasted_iota(jnp.int32, (CHAN, 4 * HEADS), 0)
        column = lax.broadcasted_iota(jnp.int32, (CHAN, 4 * HEADS), 1)
        hit = (column < 2 * HEADS) & (column % HEADS == channel // PSIZE)
        rows_s[...] = jnp.where(hit, 1.0, 0.0).astype(BF)

    at_i = lax.broadcasted_iota(jnp.int32, (SPAN, SPAN), 0)
    at_j = lax.broadcasted_iota(jnp.int32, (SPAN, SPAN), 1)
    upper = jnp.where(at_i <= at_j, 1.0, 0.0)
    cum = jnp.dot(
        drop_ref[...], upper, precision=lax.Precision.HIGHEST, preferred_element_type=F32
    )
    cum_ref[...] = cum
    last = cum[:, SPAN - 1 : SPAN]
    scales = jnp.concatenate(
        two_parts(jnp.exp(last - cum) * steps_ref[...]) + [jnp.zeros((2 * HEADS, SPAN), F32)], axis=0
    ).T.astype(BF)
    decays = jnp.broadcast_to(
        jnp.concatenate(two_parts(jnp.exp(last)) + [jnp.zeros((2 * HEADS, 1), F32)], axis=0),
        (4 * HEADS, STATE),
    ).astype(BF)
    log_ref[...] = log_s[...] + cum
    log_s[...] = log_s[...] + last
    weight = jnp.dot(scales, spread_s[...], preferred_element_type=F32)
    weighted = (xin_ref[...].astype(F32) * weight).astype(BF)
    gain = lax.dot_general(
        weighted, pair_ref[:, :STATE], (((0,), (0,)), ((), ())), preferred_element_type=F32
    )
    decay = jnp.dot(rows_s[...], decays, preferred_element_type=F32)
    state = state_s[...]
    read_ref[...] = lax.dot_general(
        pair_ref[:, STATE:], state.astype(BF), (((1,), (1,)), ((), ())), preferred_element_type=F32
    ).astype(BF)
    state = state * decay + gain
    state_s[...] = state

    @pl.when(span == TOK // SPAN - 1)
    def _():
        low = state.astype(BF)
        first = core_ref[0] == 0
        mine_ref[...] = jnp.where(first, low[: CHAN // 2], low[CHAN // 2 :])
        give_ref[: CHAN // 2, :] = jnp.where(first, low[CHAN // 2 :], low[: CHAN // 2])
        parts = three_parts(log_s[...]) + [jnp.zeros((HEADS, SPAN), F32)]
        rows = jnp.concatenate(parts, axis=0).T[:16].astype(BF)
        give_ref[CHAN // 2 :, :] = jnp.concatenate([rows, jnp.zeros_like(rows)], axis=1)


def spread_heads():
    row = lax.broadcasted_iota(jnp.int32, (4 * HEADS, CHAN), 0)
    channel = lax.broadcasted_iota(jnp.int32, (4 * HEADS, CHAN), 1)
    hit = (row < 2 * HEADS) & (row % HEADS == channel // PSIZE)
    return jnp.where(hit, 1.0, 0.0).astype(BF)


def spread_columns():
    row = lax.broadcasted_iota(jnp.int32, (4 * HEADS, HEADS * SPAN), 0)
    column = lax.broadcasted_iota(jnp.int32, (4 * HEADS, HEADS * SPAN), 1)
    hit = (row < 3 * HEADS) & (row % HEADS == column // SPAN)
    return jnp.where(hit, 1.0, 0.0).astype(BF)


def own_states(core, xin, pair, steps, drop):
    return pl.pallas_call(
        states_kernel,
        grid=(TOK // SPAN,),
        in_specs=[
            pl.BlockSpec(memory_space=pltpu.SMEM),
            pl.BlockSpec((SPAN, CHAN), lambda s: (s, 0)),
            pl.BlockSpec((SPAN, 2 * STATE), lambda s: (s, 0)),
            pl.BlockSpec((HEADS, SPAN), lambda s: (0, s)),
            pl.BlockSpec((HEADS, SPAN), lambda s: (0, s)),
        ],
        out_specs=[
            pl.BlockSpec((HEADS, SPAN), lambda s: (0, s)),
            pl.BlockSpec((HEADS, SPAN), lambda s: (0, s)),
            pl.BlockSpec((SPAN, CHAN), lambda s: (s, 0)),
            pl.BlockSpec((CHAN // 2, STATE), lambda s: (0, 0)),
            pl.BlockSpec((CHAN // 2 + 16, STATE), lambda s: (0, 0)),
        ],
        out_shape=[
            jax.ShapeDtypeStruct((HEADS, TOK), F32),
            jax.ShapeDtypeStruct((HEADS, TOK), F32),
            jax.ShapeDtypeStruct((TOK, CHAN), BF),
            jax.ShapeDtypeStruct((CHAN // 2, STATE), BF),
            jax.ShapeDtypeStruct((CHAN // 2 + 16, STATE), BF),
        ],
        scratch_shapes=[
            pltpu.VMEM((HEADS, SPAN), F32),
            pltpu.VMEM((CHAN, STATE), F32),
            pltpu.VMEM((4 * HEADS, CHAN), BF),
            pltpu.VMEM((CHAN, 4 * HEADS), BF),
        ],
        compiler_params=pltpu.CompilerParams(vmem_limit_bytes=VMEM_LIMIT),
        cost_estimate=pl.CostEstimate(flops=1 << 20, bytes_accessed=1 << 16, transcendentals=0),
    )(core, xin, pair, steps, drop)


def inside_kernel(
    xin_ref,
    pair_ref,
    cum_ref,
    steps_ref,
    read_ref,
    skip_ref,
    y_ref,
    g_s,
    ci_s,
    ex_s,
    log_s,
    spread_s,
    column_s,
):
    block = pl.program_id(1)
    cmat = pair_ref[:, STATE:]

    @pl.when((block == 0) & (pl.program_id(0) == 0))
    def _():
        spread_s[...] = spread_heads()
        column_s[...] = spread_columns()

    @pl.when(block == 0)
    def _():
        product = lax.dot_general(
            cmat, pair_ref[:, :STATE], (((1,), (1,)), ((), ())), preferred_element_type=F32
        )
        at_i = lax.broadcasted_iota(jnp.int32, (SPAN, SPAN), 0)
        at_j = lax.broadcasted_iota(jnp.int32, (SPAN, SPAN), 1)
        g_s[...] = jnp.where(at_j <= at_i, product, 0.0)
        cum = cum_ref[...]
        log_s[...] = jnp.log(steps_ref[...])
        ci_s[...] = jnp.concatenate(three_parts(cum) + [jnp.zeros_like(cum)], axis=0).T.astype(BF)
        ex_s[...] = jnp.concatenate(
            two_parts(jnp.exp(cum)) + [jnp.zeros((2 * HEADS, SPAN), F32)], axis=0
        ).T.astype(BF)

    xf = xin_ref[...].astype(F32)
    grown = jnp.dot(ex_s[...], spread_s[...], preferred_element_type=F32)
    rows_i = jnp.dot(ci_s[...], column_s[...], preferred_element_type=F32)
    base = read_ref[...].astype(F32) * grown + skip_ref[...] * xf
    cum_rows = cum_ref[pl.ds(pl.multiple_of(block * HB, HB), HB), :]
    log_rows = log_s[pl.ds(pl.multiple_of(block * HB, HB), HB), :]
    cum_rows = cum_rows - log_rows
    masked = g_s[...]
    lane = lax.broadcasted_iota(jnp.int32, (SPAN, 2 * PSIZE), 1)
    for pair in range(HB // 2):
        mixes = []
        for h in (2 * pair, 2 * pair + 1):
            gap = rows_i[:, h * SPAN : (h + 1) * SPAN] - cum_rows[h : h + 1]
            mixes.append((masked * jnp.exp(jnp.minimum(gap, log_rows[h : h + 1]))).astype(BF))
        two = xf[:, pair * 128 : (pair + 1) * 128]
        left = jnp.where(lane < PSIZE, two, 0.0).astype(BF)
        right = jnp.where(lane < PSIZE, 0.0, two).astype(BF)
        intra = jnp.dot(
            jnp.concatenate(mixes, axis=1),
            jnp.concatenate([left, right], axis=0),
            preferred_element_type=F32,
        )
        y_ref[:, pair * 128 : (pair + 1) * 128] = (
            base[:, pair * 128 : (pair + 1) * 128] + intra
        ).astype(BF)


def inside_blocks(xin, pair, cum, steps, read, skip):
    blocks = HEADS // HB
    return pl.pallas_call(
        inside_kernel,
        grid=(TOK // SPAN, blocks),
        in_specs=[
            pl.BlockSpec((SPAN, HBC), lambda s, b: (s, b)),
            pl.BlockSpec((SPAN, 2 * STATE), lambda s, b: (s, 0)),
            pl.BlockSpec((HEADS, SPAN), lambda s, b: (0, s)),
            pl.BlockSpec((HEADS, SPAN), lambda s, b: (0, s)),
            pl.BlockSpec((SPAN, HBC), lambda s, b: (s, b)),
            pl.BlockSpec((1, HBC), lambda s, b: (0, b)),
        ],
        out_specs=pl.BlockSpec((SPAN, HBC), lambda s, b: (s, b)),
        out_shape=jax.ShapeDtypeStruct((TOK, CHAN), BF),
        scratch_shapes=[
            pltpu.VMEM((SPAN, SPAN), F32),
            pltpu.VMEM((SPAN, 4 * HEADS), BF),
            pltpu.VMEM((SPAN, 4 * HEADS), BF),
            pltpu.VMEM((HEADS, SPAN), F32),
            pltpu.VMEM((4 * HEADS, CHAN), BF),
            pltpu.VMEM((4 * HEADS, HEADS * SPAN), BF),
        ],
        compiler_params=pltpu.CompilerParams(vmem_limit_bytes=VMEM_LIMIT),
        cost_estimate=pl.CostEstimate(flops=1 << 34, bytes_accessed=1 << 16, transcendentals=0),
    )(xin, pair, cum, steps, read, skip)


CHIPS = NX * NZ
SAME_CORE = [[2 * chip + core for chip in range(CHIPS)] for core in range(NC)]


def chain_kernel(from_ref, into_ref):
    carried = jnp.zeros((PSIZE, STATE), F32)
    for chip in range(CHIPS):
        into_ref[chip] = carried.astype(BF)
        if chip < CHIPS - 1:
            parts = from_ref[chip, PSIZE:, :].astype(F32)
            decay = jnp.exp(parts[0:1] + parts[1:2] + parts[2:3])
            carried = decay * carried + from_ref[chip, :PSIZE, :].astype(F32)


def chain(states):
    return pl.pallas_call(
        chain_kernel,
        in_specs=[pl.BlockSpec(memory_space=pltpu.VMEM)],
        out_specs=pl.BlockSpec(memory_space=pltpu.VMEM),
        out_shape=jax.ShapeDtypeStruct((CHIPS, PSIZE, STATE), BF),
        cost_estimate=pl.CostEstimate(flops=1 << 20, bytes_accessed=1 << 16, transcendentals=0),
    )(states)


def with_logs(states, logs):
    parts = [part[:, None, None] for part in three_parts(logs)]
    row = lax.broadcasted_iota(jnp.int32, (16, 16, STATE), 1)
    extra = jnp.where(
        row == 0, parts[0], jnp.where(row == 1, parts[1], jnp.where(row == 2, parts[2], 0.0))
    )
    return jnp.concatenate([states, extra], axis=1).astype(BF)


def exchanged(value):
    return lax.all_to_all(value, "ctx", 0, 0, tiled=True, axis_index_groups=SAME_CORE)


def finish_kernel(
    core_ref, y_ref, c_ref, log_ref, in_ref, other_ref, gate_ref, gain_ref, out_ref, spread_s
):
    grown = jnp.concatenate(
        two_parts(jnp.exp(log_ref[...])) + [jnp.zeros((2 * HEADS, END_ROWS), F32)], axis=0
    ).T.astype(BF)

    @pl.when(pl.program_id(0) == 0)
    def _():
        spread_s[...] = spread_heads()

    scale = jnp.dot(grown, spread_s[...], preferred_element_type=F32)
    contract = (((1,), (1,)), ((), ()))
    kept = lax.dot_general(c_ref[...], in_ref[...], contract, preferred_element_type=F32)
    given = lax.dot_general(c_ref[...], other_ref[...], contract, preferred_element_type=F32)
    first = core_ref[0] == 0
    read = jnp.concatenate(
        [jnp.where(first, kept, given), jnp.where(first, given, kept)], axis=1
    )
    mixed = y_ref[...].astype(F32) + read * scale
    gate = gate_ref[...].astype(F32)
    gated = mixed * (gate * jax.nn.sigmoid(gate))
    mean = jnp.mean(gated * gated, axis=1, keepdims=True)
    out_ref[...] = (gated * lax.rsqrt(mean + 1e-05) * gain_ref[...]).astype(BF)


def finish(core, y, pair, logs, entering, other, gate, gain):
    return pl.pallas_call(
        finish_kernel,
        grid=(TOK // END_ROWS,),
        in_specs=[
            pl.BlockSpec(memory_space=pltpu.SMEM),
            pl.BlockSpec((END_ROWS, CHAN), lambda s: (s, 0)),
            pl.BlockSpec((END_ROWS, STATE), lambda s: (s, 1)),
            pl.BlockSpec((HEADS, END_ROWS), lambda s: (0, s)),
            pl.BlockSpec((CHAN // 2, STATE), lambda s: (0, 0)),
            pl.BlockSpec((CHAN // 2, STATE), lambda s: (0, 0)),
            pl.BlockSpec((END_ROWS, CHAN), lambda s: (s, 0)),
            pl.BlockSpec((1, CHAN), lambda s: (0, 0)),
        ],
        out_specs=pl.BlockSpec((END_ROWS, CHAN), lambda s: (s, 0)),
        out_shape=jax.ShapeDtypeStruct((TOK, CHAN), BF),
        scratch_shapes=[pltpu.VMEM((4 * HEADS, CHAN), BF)],
        compiler_params=pltpu.CompilerParams(vmem_limit_bytes=VMEM_LIMIT),
        cost_estimate=pl.CostEstimate(flops=1 << 20, bytes_accessed=1 << 16, transcendentals=0),
    )(core, y, pair, logs, entering, other, gate, gain)


QHEADS = 4
SUB = 256


def attend_kernel(flag_ref, q_ref, *refs, planes, own, fresh):
    pieces, refs = refs[: 2 * planes], refs[2 * planes :]
    if not fresh:
        in_sums, in_top, *refs = refs
    if own:
        out_sums, out_top, *refs = refs
    else:
        part_ref, *refs = refs
    kv, sums, top, qq, sa, sb, ma, mb, key_sem, in_sem, out_sem = refs
    count = flag_ref[0]
    third = flag_ref[1]
    core = flag_ref[2]

    def carried(head):
        return (
            pltpu.make_async_copy(in_sums.at[head], sums.at[head], in_sem.at[0, head]),
            pltpu.make_async_copy(in_top.at[head], top.at[head], in_sem.at[1, head]),
        )

    def leaving(head):
        return (
            pltpu.make_async_copy(sums.at[head], out_sums.at[head], out_sem.at[0, head]),
            pltpu.make_async_copy(top.at[head], out_top.at[head], out_sem.at[1, head]),
        )

    def keys(p):
        slots = pl.ds(p * NZ, NZ)
        return (
            pltpu.make_async_copy(pieces[2 * p], kv.at[slots, 0], key_sem.at[p, 0]),
            pltpu.make_async_copy(pieces[2 * p + 1], kv.at[slots, 1], key_sem.at[p, 1]),
        )

    def score(head, at, s_ref, m_ref, masked=False):
        rows_in = kv[at, :, :, :HD].reshape(CHUNK, HD)
        twice = jnp.concatenate([rows_in, rows_in], axis=1)
        for r in range(TOK // SUB):
            rows = slice(r * SUB, (r + 1) * SUB)
            s = lax.dot_general(
                qq[head, rows, :], twice, (((1,), (1,)), ((), ())), preferred_element_type=F32
            )
            if masked:
                row = lax.broadcasted_iota(jnp.int32, s.shape, 0) + r * SUB
                key = lax.broadcasted_iota(jnp.int32, s.shape, 1)
                limit = jnp.where(core == 1, 2 * TOK, TOK)
                seen = ((key < TOK) & (key <= row)) | ((key >= TOK) & (key < limit))
                s = jnp.where(seen, s, -1e30)
            s_ref[rows, :] = s
            m_ref[rows, :] = jnp.broadcast_to(jnp.max(s, axis=1, keepdims=True), (SUB, HD))

    def gather(head, at, s_ref, m_ref):
        values = kv[at, :, :, HD:].reshape(CHUNK, HD)
        values = jnp.concatenate([values, jnp.ones((CHUNK, HD), BF)], axis=1)
        for r in range(TOK // SUB):
            rows = slice(r * SUB, (r + 1) * SUB)
            old = top[head, rows, :]
            new = jnp.maximum(old, m_ref[rows, :])
            weights = jnp.exp2(s_ref[rows, :] - new[:, :1]).astype(BF)
            factor = jnp.exp2(old - new)
            part = jnp.dot(weights, values, preferred_element_type=F32)
            sums[head, rows, :] = (
                sums[head, rows, :] * jnp.concatenate([factor, factor], axis=1) + part
            )
            top[head, rows, :] = new

    if not fresh:
        for head in range(QHEADS):
            for copy in carried(head):
                copy.start()

    @pl.when(count > 0)
    def _():
        for p in range(planes):

            @pl.when(own | (p < count))
            def _():
                for copy in keys(p):
                    copy.start()

        for head in range(QHEADS):
            scaled = q_ref[:, head * HD : (head + 1) * HD].astype(F32) * (HD**-0.5 * math.log2(math.e))
            high = scaled.astype(BF)
            low = (scaled - high.astype(F32)).astype(BF)
            qq[head] = jnp.concatenate([high, low], axis=1)
            if fresh:
                sums[head] = jnp.zeros((TOK, 2 * HD), F32)
                top[head] = jnp.full((TOK, HD), -1e30, F32)
        for p in range(planes):

            @pl.when(own | (p < count))
            def _():
                for copy in keys(p):
                    copy.wait()

        if own:
            def chunk(i):
                return jnp.where(i == 2, third, jnp.minimum(i, NZ - 1))

            def one_head(head, _):
                score(head, 0, sa, ma, masked=True)

                def body(j, _):
                    i = 2 * j
                    score(head, chunk(i + 1), sb, mb)
                    gather(head, chunk(i), sa, ma)
                    score(head, chunk(i + 2), sa, ma)
                    gather(head, chunk(i + 1), sb, mb)
                    return 0

                lax.fori_loop(0, count // 2, body, 0)

                @pl.when(count % 2 == 1)
                def _():
                    gather(head, chunk(count - 1), sa, ma)

                for copy in leaving(head):
                    copy.start()
                return 0

            def full_head(head, _):
                score(head, 1, sb, mb)
                gather(head, 0, sa, ma)
                score(head, 2, sa, ma)
                gather(head, 1, sb, mb)
                score(head, 3, sb, mb)
                gather(head, 2, sa, ma)
                score(jnp.minimum(head + 1, QHEADS - 1), 0, sa, ma, masked=True)
                gather(head, 3, sb, mb)
                for copy in leaving(head):
                    copy.start()
                return 0

            @pl.when(count == NZ)
            def _():
                score(0, 0, sa, ma, masked=True)
                lax.fori_loop(0, QHEADS, full_head, 0)

            @pl.when(count < NZ)
            def _():
                lax.fori_loop(0, QHEADS, one_head, 0)

            for head in range(QHEADS):
                for copy in leaving(head):
                    copy.wait()
        else:
            steps = 2 * count

            def where_at(step):
                head = step // steps
                return jnp.minimum(head, QHEADS - 1), 2 * (step - head * steps)

            score(0, 0, sa, ma)

            def body(step, _):
                head, at = where_at(step)
                if not fresh:

                    @pl.when(at == 0)
                    def _():
                        for copy in carried(head):
                            copy.wait()

                score(head, at + 1, sb, mb)
                gather(head, at, sa, ma)
                score(*where_at(step + 1), sa, ma)
                gather(head, at + 1, sb, mb)
                return 0

            lax.fori_loop(0, QHEADS * steps, body, 0)

    if not own:
        if not fresh:

            @pl.when(count == 0)
            def _():
                for head in range(QHEADS):
                    for copy in carried(head):
                        copy.wait()

        @pl.when(jnp.logical_or(count > 0, not fresh))
        def _():
            lane = lax.broadcasted_iota(jnp.int32, (TOK, HD), 1)
            log = jnp.zeros((TOK, HD), F32)
            for head in range(QHEADS):
                total = sums[head, :, HD:]
                part_ref[:, head * HD : (head + 1) * HD] = (sums[head, :, :HD] / total).astype(BF)
                for at, part in enumerate(three_parts(top[head] + jnp.log2(total))):
                    log = jnp.where(lane == 32 * head + at, part, log)
            part_ref[:, QHEADS * HD :] = log.astype(BF)


def attend(flags, query, *pieces, carry=None, own=False):
    fresh = carry is None
    planes = len(pieces) // 2
    vmem = pl.BlockSpec(memory_space=pltpu.VMEM)
    hbm = pl.BlockSpec(memory_space=pl.ANY)
    if own:
        out = [
            jax.ShapeDtypeStruct((QHEADS, TOK, 2 * HD), F32),
            jax.ShapeDtypeStruct((QHEADS, TOK, HD), F32),
        ]
        out_specs = [hbm, hbm]
    else:
        out, out_specs = jax.ShapeDtypeStruct((TOK, (QHEADS + 1) * HD), BF), vmem
    return pl.pallas_call(
        functools.partial(attend_kernel, planes=planes, own=own, fresh=fresh),
        in_specs=[pl.BlockSpec(memory_space=pltpu.SMEM), vmem]
        + [hbm] * len(pieces)
        + ([] if fresh else [hbm, hbm]),
        out_specs=out_specs,
        out_shape=out,
        scratch_shapes=[
            pltpu.VMEM((planes * NZ, NC, TOK, 2 * HD), BF),
            pltpu.VMEM((QHEADS, TOK, 2 * HD), F32),
            pltpu.VMEM((QHEADS, TOK, HD), F32),
            pltpu.VMEM((QHEADS, TOK, 2 * HD), BF),
            pltpu.VMEM((TOK, CHUNK), F32),
            pltpu.VMEM((TOK, CHUNK), F32),
            pltpu.VMEM((TOK, HD), F32),
            pltpu.VMEM((TOK, HD), F32),
            pltpu.SemaphoreType.DMA((planes, 2)),
            pltpu.SemaphoreType.DMA((2, QHEADS)),
            pltpu.SemaphoreType.DMA((2, QHEADS)),
        ],
        compiler_params=pltpu.CompilerParams(vmem_limit_bytes=ATTEND_LIMIT),
        cost_estimate=pl.CostEstimate(
            flops=1 << 35 if fresh and not own else 1 << 20, bytes_accessed=1 << 16, transcendentals=0
        ),
    )(flags, query, *pieces, *([] if fresh else carry))


def merge_kernel(flag_ref, mine_ref, other_ref, out_ref):
    row = lax.broadcasted_iota(jnp.int32, (HD, HD), 0)
    with_other = flag_ref[0] > 0
    logs = [ref[:, QHEADS * HD :] for ref in (mine_ref, other_ref)]
    for head in range(QHEADS):
        pick = jnp.where((row >= 32 * head) & (row < 32 * head + 3), 1.0, 0.0).astype(BF)
        mine, other = [jnp.dot(log, pick, preferred_element_type=F32) for log in logs]
        other = jnp.where(with_other, other, -1e30)
        new = jnp.maximum(mine, other)
        mine, other = jnp.exp2(mine - new), jnp.exp2(other - new)
        columns = slice(head * HD, (head + 1) * HD)
        joint = mine_ref[:, columns].astype(F32) * mine + other_ref[:, columns].astype(F32) * other
        out_ref[:, columns] = (joint / (mine + other)).astype(BF)


def merge(flags, part, other):
    rows = TOK // 2
    wide = pl.BlockSpec((rows, (QHEADS + 1) * HD), lambda r: (r, 0))
    return pl.pallas_call(
        merge_kernel,
        grid=(TOK // rows,),
        in_specs=[pl.BlockSpec(memory_space=pltpu.SMEM), wide, wide],
        out_specs=pl.BlockSpec((rows, QHEADS * HD), lambda r: (r, 0)),
        out_shape=jax.ShapeDtypeStruct((TOK, QHEADS * HD), BF),
        compiler_params=pltpu.CompilerParams(vmem_limit_bytes=VMEM_LIMIT),
        cost_estimate=pl.CostEstimate(flops=1 << 20, bytes_accessed=1 << 16, transcendentals=0),
    )(flags, part, other)


def local(
    hidden,
    dt_weight,
    dt_bias,
    decay_rate,
    skip_gain,
    ssm_in,
    bc_in,
    conv_x,
    conv_bc,
    gate_in,
    norm_gain,
    query_heads,
    key_heads,
    value_heads,
):
    mine = lax.axis_index("ctx")
    x, z, c = mine // (NZ * NC), (mine // NC) % NZ, mine % NC
    core = c.astype(jnp.int32)[None]

    def flags(count):
        return jnp.stack([count, jnp.where(z == NZ - 1, 2, 3), c]).astype(jnp.int32)

    bc = bc_in.reshape(TOK, 2 * STATE)
    partial = lax.dot_general(
        dt_weight, hidden, (((0,), (1,)), ((), ())), preferred_element_type=F32
    )
    partial, keys, ends_x, ends_bc = lax.optimization_barrier(
        (partial, key_heads, ssm_in[TOK - 16 :], bc[TOK - 16 :])
    )
    ends = jnp.concatenate([ends_x, ends_bc], axis=1)
    tail = lax.ppermute(ends, "ctx", [(i, i + 1) for i in range(31)])
    parts = lax.all_to_all(partial.reshape(8, HEADS, TOK), "head", 0, 0, tiled=True)
    xin, pair = convolved(ssm_in, tail, bc, conv_x, conv_bc.reshape(4, 2 * STATE))
    rows = jnp.concatenate([keys, value_heads], axis=1)
    up, down, two = along_z(rows, 1), along_z(rows, -1), along_z(rows, 2)
    parts, xin, pair = lax.optimization_barrier((parts, xin, pair))
    steps = jax.nn.softplus(jnp.sum(parts, axis=0) + dt_bias[:, None])
    drop = -steps * decay_rate[:, None]
    total = jnp.sum(drop, axis=1)
    cum, logs, read, keep, give = own_states(core, xin, pair, steps, drop)

    keep, give, up, down = lax.optimization_barrier((keep, give, up, down))
    other = swap_core(give)
    partner = jnp.sum(other[CHAN // 2, : 3 * HEADS].astype(F32).reshape(3, HEADS), axis=0)
    other = other[: CHAN // 2]
    by_half = lambda value: lax.dynamic_index_in_dim(value.reshape(2, 16), c, 0, False)
    shape = (16, PSIZE, STATE)
    log_first = by_half(jnp.where(c == 0, total, partner))
    log_second = by_half(jnp.where(c == 0, partner, total))
    early = jnp.where(c == 0, keep, other).reshape(shape).astype(F32)
    late = jnp.where(c == 0, other, keep).reshape(shape).astype(F32)
    both = with_logs(
        late + jnp.exp(log_second)[:, None, None] * early, log_first + log_second
    )
    collected = exchanged(both)
    both, xin, rows, up, down, two, query = lax.optimization_barrier(
        (both, xin, rows, up, down, two, query_heads)
    )
    visitor = send(query, lambda x, z, c: (x - 2, z, c) if x >= 2 else None)
    y = inside_blocks(xin, pair, cum, steps, read, jnp.repeat(skip_gain, PSIZE)[None])
    plane = jnp.stack([rows, up, down, two])
    plane_pair = swap_core(plane)
    left = along_x(plane, 1)
    right = send(plane, lambda x, z, c: (NX - 1, z, c) if x == 0 else None)
    seen = attend(flags(z + 1), query, plane, plane_pair, own=True)
    collected, y, seen = lax.optimization_barrier((collected, y, seen))
    carried = chain(collected)
    chip_in = exchanged(carried)
    planes_seen = jnp.where(x == 0, 0, jnp.where(x == NX - 1, 2, 1))
    carried, to_visit, to_see, visitor, left, right = lax.optimization_barrier(
        (carried, flags(jnp.where(x <= 1, 1, 0)), flags(planes_seen), visitor, left, right)
    )
    left_pair = swap_core(left)
    right_pair = swap_core(right)
    part = attend(to_visit, visitor, plane, plane_pair)
    part, to_see = lax.optimization_barrier((part, to_see))
    part = send(part, lambda x, z, c: (x + 2, z, c) if x <= 1 else None)
    seen = attend(to_see, query, left, left_pair, right, right_pair, carry=seen)
    chip_in, seen = lax.optimization_barrier((chip_in, seen))
    after = (early + jnp.exp(log_first)[:, None, None] * chip_in.astype(F32)).astype(BF)
    entering = jnp.where(c == 0, chip_in, after).reshape(CHAN // 2, STATE)
    sent = jnp.where(c == 0, after, chip_in).reshape(CHAN // 2, STATE)
    received = swap_core(sent)
    sent, seen = lax.optimization_barrier((sent, seen))
    attn_out = merge(flags(jnp.where(x >= 2, 1, 0)), seen, part)
    received, attn_out = lax.optimization_barrier((received, attn_out))
    mamba_out = finish(core, y, pair, logs, entering, received, gate_in, norm_gain[None])
    return (mamba_out, attn_out)


def solution(mesh):
    in_specs = (
        P("ctx", "head"),
        P("head", None),
        P("head"),
        P("head"),
        P("head"),
        P("ctx", "head"),
        P("ctx", "head", None),
        P(None, "head"),
        P(None, "head", None),
        P("ctx", "head"),
        P("head"),
        P("ctx", "head"),
        P("ctx", "head"),
        P("ctx", "head"),
    )
    out_specs = (P("ctx", "head"), P("ctx", "head"))
    return jax.shard_map(local, mesh=mesh, in_specs=in_specs, out_specs=out_specs, check_vma=False)
```

```python
import functools
import math

import jax
import jax.numpy as jnp
from jax import lax
from jax.experimental import pallas as pl
from jax.experimental.pallas import tpu as pltpu
from jax.sharding import PartitionSpec as P

SPAN = 128
HD = 128
BF = jnp.bfloat16
F32 = jnp.float32
NX, NZ, NC = 4, 4, 2
HEADS, PSIZE, STATE = 32, 64, 256
CHAN = HEADS * PSIZE
TOK = 512
HB = 32
HBC = HB * PSIZE
CHUNK = 1024
VMEM_LIMIT = 58 << 20
ATTEND_LIMIT = 22 << 20
CONV_ROWS = 256
END_ROWS = 256


def pairs_of(move):
    found = []
    for x in range(NX):
        for z in range(NZ):
            for c in range(NC):
                target = move(x, z, c)
                if target is not None:
                    tx, tz, tc = target
                    found.append(((x * NZ + z) * NC + c, (tx * NZ + tz) * NC + tc))
    return found


def send(value, move):
    return lax.ppermute(value, "ctx", pairs_of(move))


def swap_core(value):
    return send(value, lambda x, z, c: (x, z, 1 - c))


def along_z(value, steps):
    return send(value, lambda x, z, c: (x, (z + steps) % NZ, c))


def along_x(value, steps, wrap=False):
    def move(x, z, c):
        if wrap or 0 <= x + steps < NX:
            return ((x + steps) % NX, z, c)
        return None

    return send(value, move)


def shifted_rows(rows, tail, steps):
    if steps == 0:
        return rows
    rolled = pltpu.roll(rows, steps, 0)
    before = pltpu.roll(tail, steps, 0)
    at = lax.broadcasted_iota(jnp.int32, before.shape, 0)
    top = jnp.where(at < steps, before, rolled[:8])
    return jnp.concatenate([top, rolled[8:]], axis=0)


def conv_silu(rows, tail, taps):
    taps_count = taps.shape[0]
    total = None
    for k in range(taps_count):
        term = taps[k : k + 1] * shifted_rows(rows, tail, taps_count - 1 - k)
        total = term if total is None else total + term
    return (total * jax.nn.sigmoid(total)).astype(BF)


def two_parts(value):
    high = value.astype(BF).astype(F32)
    return [high, (value - high).astype(BF).astype(F32)]


def three_parts(value):
    high = value.astype(BF).astype(F32)
    return [high] + two_parts(value - high)


def conv_kernel(
    x_ref, before_ref, xtail_ref, pair_ref, pbefore_ref, ptail_ref, taps_ref, ptaps_ref, xin_ref, conv_ref
):
    first = pl.program_id(0) == 0
    before = jnp.where(first, ptail_ref[...], pbefore_ref[...]).astype(F32)[8:]
    conv_ref[...] = conv_silu(pair_ref[...].astype(F32), before, ptaps_ref[...])
    before = jnp.where(first, xtail_ref[...], before_ref[...]).astype(F32)[8:]
    xin_ref[...] = conv_silu(x_ref[...].astype(F32), before, taps_ref[...])


def convolved(ssm_in, tail, bc_in, conv_x, conv_bc):
    prior = lambda s: (jnp.maximum(s * (CONV_ROWS // 16) - 1, 0), 0)
    return pl.pallas_call(
        conv_kernel,
        grid=(TOK // CONV_ROWS,),
        in_specs=[
            pl.BlockSpec((CONV_ROWS, CHAN), lambda s: (s, 0)),
            pl.BlockSpec((16, CHAN), prior),
            pl.BlockSpec((16, CHAN), lambda s: (0, 0)),
            pl.BlockSpec((CONV_ROWS, 2 * STATE), lambda s: (s, 0)),
            pl.BlockSpec((16, 2 * STATE), prior),
            pl.BlockSpec((16, 2 * STATE), lambda s: (0, CHAN // (2 * STATE))),
            pl.BlockSpec((4, CHAN), lambda s: (0, 0)),
            pl.BlockSpec((4, 2 * STATE), lambda s: (0, 0)),
        ],
        out_specs=[
            pl.BlockSpec((CONV_ROWS, CHAN), lambda s: (s, 0)),
            pl.BlockSpec((CONV_ROWS, 2 * STATE), lambda s: (s, 0)),
        ],
        out_shape=[
            jax.ShapeDtypeStruct((TOK, CHAN), BF),
            jax.ShapeDtypeStruct((TOK, 2 * STATE), BF),
        ],
        compiler_params=pltpu.CompilerParams(vmem_limit_bytes=VMEM_LIMIT),
        cost_estimate=pl.CostEstimate(flops=1 << 20, bytes_accessed=1 << 16, transcendentals=0),
    )(ssm_in, ssm_in, tail, bc_in, bc_in, tail, conv_x, conv_bc)


def states_kernel(
    core_ref,
    xin_ref,
    pair_ref,
    steps_ref,
    drop_ref,
    cum_ref,
    log_ref,
    read_ref,
    mine_ref,
    give_ref,
    log_s,
    state_s,
    spread_s,
    rows_s,
):
    span = pl.program_id(0)

    @pl.when(span == 0)
    def _():
        log_s[...] = jnp.zeros_like(log_s)
        state_s[...] = jnp.zeros_like(state_s)
        spread_s[...] = spread_heads()
        channel = lax.broadcasted_iota(jnp.int32, (CHAN, 4 * HEADS), 0)
        column = lax.broadcasted_iota(jnp.int32, (CHAN, 4 * HEADS), 1)
        hit = (column < 2 * HEADS) & (column % HEADS == channel // PSIZE)
        rows_s[...] = jnp.where(hit, 1.0, 0.0).astype(BF)

    at_i = lax.broadcasted_iota(jnp.int32, (SPAN, SPAN), 0)
    at_j = lax.broadcasted_iota(jnp.int32, (SPAN, SPAN), 1)
    upper = jnp.where(at_i <= at_j, 1.0, 0.0)
    cum = jnp.dot(
        drop_ref[...], upper, precision=lax.Precision.HIGHEST, preferred_element_type=F32
    )
    cum_ref[...] = cum
    last = cum[:, SPAN - 1 : SPAN]
    scales = jnp.concatenate(
        two_parts(jnp.exp(last - cum) * steps_ref[...]) + [jnp.zeros((2 * HEADS, SPAN), F32)], axis=0
    ).T.astype(BF)
    decays = jnp.broadcast_to(
        jnp.concatenate(two_parts(jnp.exp(last)) + [jnp.zeros((2 * HEADS, 1), F32)], axis=0),
        (4 * HEADS, STATE),
    ).astype(BF)
    log_ref[...] = log_s[...] + cum
    log_s[...] = log_s[...] + last
    weight = jnp.dot(scales, spread_s[...], preferred_element_type=F32)
    weighted = (xin_ref[...].astype(F32) * weight).astype(BF)
    gain = lax.dot_general(
        weighted, pair_ref[:, :STATE], (((0,), (0,)), ((), ())), preferred_element_type=F32
    )
    decay = jnp.dot(rows_s[...], decays, preferred_element_type=F32)
    state = state_s[...]
    read_ref[...] = lax.dot_general(
        pair_ref[:, STATE:], state.astype(BF), (((1,), (1,)), ((), ())), preferred_element_type=F32
    ).astype(BF)
    state = state * decay + gain
    state_s[...] = state

    @pl.when(span == TOK // SPAN - 1)
    def _():
        low = state.astype(BF)
        first = core_ref[0] == 0
        mine_ref[...] = jnp.where(first, low[: CHAN // 2], low[CHAN // 2 :])
        give_ref[: CHAN // 2, :] = jnp.where(first, low[CHAN // 2 :], low[: CHAN // 2])
        parts = three_parts(log_s[...]) + [jnp.zeros((HEADS, SPAN), F32)]
        rows = jnp.concatenate(parts, axis=0).T[:16].astype(BF)
        give_ref[CHAN // 2 :, :] = jnp.concatenate([rows, jnp.zeros_like(rows)], axis=1)


def spread_heads():
    row = lax.broadcasted_iota(jnp.int32, (4 * HEADS, CHAN), 0)
    channel = lax.broadcasted_iota(jnp.int32, (4 * HEADS, CHAN), 1)
    hit = (row < 2 * HEADS) & (row % HEADS == channel // PSIZE)
    return jnp.where(hit, 1.0, 0.0).astype(BF)


def spread_columns():
    row = lax.broadcasted_iota(jnp.int32, (4 * HEADS, HEADS * SPAN), 0)
    column = lax.broadcasted_iota(jnp.int32, (4 * HEADS, HEADS * SPAN), 1)
    hit = (row < 3 * HEADS) & (row % HEADS == column // SPAN)
    return jnp.where(hit, 1.0, 0.0).astype(BF)


def own_states(core, xin, pair, steps, drop):
    return pl.pallas_call(
        states_kernel,
        grid=(TOK // SPAN,),
        in_specs=[
            pl.BlockSpec(memory_space=pltpu.SMEM),
            pl.BlockSpec((SPAN, CHAN), lambda s: (s, 0)),
            pl.BlockSpec((SPAN, 2 * STATE), lambda s: (s, 0)),
            pl.BlockSpec((HEADS, SPAN), lambda s: (0, s)),
            pl.BlockSpec((HEADS, SPAN), lambda s: (0, s)),
        ],
        out_specs=[
            pl.BlockSpec((HEADS, SPAN), lambda s: (0, s)),
            pl.BlockSpec((HEADS, SPAN), lambda s: (0, s)),
            pl.BlockSpec((SPAN, CHAN), lambda s: (s, 0)),
            pl.BlockSpec((CHAN // 2, STATE), lambda s: (0, 0)),
            pl.BlockSpec((CHAN // 2 + 16, STATE), lambda s: (0, 0)),
        ],
        out_shape=[
            jax.ShapeDtypeStruct((HEADS, TOK), F32),
            jax.ShapeDtypeStruct((HEADS, TOK), F32),
            jax.ShapeDtypeStruct((TOK, CHAN), BF),
            jax.ShapeDtypeStruct((CHAN // 2, STATE), BF),
            jax.ShapeDtypeStruct((CHAN // 2 + 16, STATE), BF),
        ],
        scratch_shapes=[
            pltpu.VMEM((HEADS, SPAN), F32),
            pltpu.VMEM((CHAN, STATE), F32),
            pltpu.VMEM((4 * HEADS, CHAN), BF),
            pltpu.VMEM((CHAN, 4 * HEADS), BF),
        ],
        compiler_params=pltpu.CompilerParams(vmem_limit_bytes=VMEM_LIMIT),
        cost_estimate=pl.CostEstimate(flops=1 << 20, bytes_accessed=1 << 16, transcendentals=0),
    )(core, xin, pair, steps, drop)


def inside_kernel(
    xin_ref,
    pair_ref,
    cum_ref,
    steps_ref,
    read_ref,
    skip_ref,
    y_ref,
    g_s,
    ci_s,
    ex_s,
    log_s,
    spread_s,
    column_s,
):
    block = pl.program_id(1)
    cmat = pair_ref[:, STATE:]

    @pl.when((block == 0) & (pl.program_id(0) == 0))
    def _():
        spread_s[...] = spread_heads()
        column_s[...] = spread_columns()

    @pl.when(block == 0)
    def _():
        product = lax.dot_general(
            cmat, pair_ref[:, :STATE], (((1,), (1,)), ((), ())), preferred_element_type=F32
        )
        at_i = lax.broadcasted_iota(jnp.int32, (SPAN, SPAN), 0)
        at_j = lax.broadcasted_iota(jnp.int32, (SPAN, SPAN), 1)
        g_s[...] = jnp.where(at_j <= at_i, product, 0.0)
        cum = cum_ref[...]
        log_s[...] = jnp.log(steps_ref[...])
        ci_s[...] = jnp.concatenate(three_parts(cum) + [jnp.zeros_like(cum)], axis=0).T.astype(BF)
        ex_s[...] = jnp.concatenate(
            two_parts(jnp.exp(cum)) + [jnp.zeros((2 * HEADS, SPAN), F32)], axis=0
        ).T.astype(BF)

    xf = xin_ref[...].astype(F32)
    grown = jnp.dot(ex_s[...], spread_s[...], preferred_element_type=F32)
    rows_i = jnp.dot(ci_s[...], column_s[...], preferred_element_type=F32)
    base = read_ref[...].astype(F32) * grown + skip_ref[...] * xf
    cum_rows = cum_ref[pl.ds(pl.multiple_of(block * HB, HB), HB), :]
    log_rows = log_s[pl.ds(pl.multiple_of(block * HB, HB), HB), :]
    cum_rows = cum_rows - log_rows
    masked = g_s[...]
    lane = lax.broadcasted_iota(jnp.int32, (SPAN, 2 * PSIZE), 1)
    for pair in range(HB // 2):
        mixes = []
        for h in (2 * pair, 2 * pair + 1):
            gap = rows_i[:, h * SPAN : (h + 1) * SPAN] - cum_rows[h : h + 1]
            mixes.append((masked * jnp.exp(jnp.minimum(gap, log_rows[h : h + 1]))).astype(BF))
        two = xf[:, pair * 128 : (pair + 1) * 128]
        left = jnp.where(lane < PSIZE, two, 0.0).astype(BF)
        right = jnp.where(lane < PSIZE, 0.0, two).astype(BF)
        intra = jnp.dot(
            jnp.concatenate(mixes, axis=1),
            jnp.concatenate([left, right], axis=0),
            preferred_element_type=F32,
        )
        y_ref[:, pair * 128 : (pair + 1) * 128] = (
            base[:, pair * 128 : (pair + 1) * 128] + intra
        ).astype(BF)


def inside_blocks(xin, pair, cum, steps, read, skip):
    blocks = HEADS // HB
    return pl.pallas_call(
        inside_kernel,
        grid=(TOK // SPAN, blocks),
        in_specs=[
            pl.BlockSpec((SPAN, HBC), lambda s, b: (s, b)),
            pl.BlockSpec((SPAN, 2 * STATE), lambda s, b: (s, 0)),
            pl.BlockSpec((HEADS, SPAN), lambda s, b: (0, s)),
            pl.BlockSpec((HEADS, SPAN), lambda s, b: (0, s)),
            pl.BlockSpec((SPAN, HBC), lambda s, b: (s, b)),
            pl.BlockSpec((1, HBC), lambda s, b: (0, b)),
        ],
        out_specs=pl.BlockSpec((SPAN, HBC), lambda s, b: (s, b)),
        out_shape=jax.ShapeDtypeStruct((TOK, CHAN), BF),
        scratch_shapes=[
            pltpu.VMEM((SPAN, SPAN), F32),
            pltpu.VMEM((SPAN, 4 * HEADS), BF),
            pltpu.VMEM((SPAN, 4 * HEADS), BF),
            pltpu.VMEM((HEADS, SPAN), F32),
            pltpu.VMEM((4 * HEADS, CHAN), BF),
            pltpu.VMEM((4 * HEADS, HEADS * SPAN), BF),
        ],
        compiler_params=pltpu.CompilerParams(vmem_limit_bytes=VMEM_LIMIT),
        cost_estimate=pl.CostEstimate(flops=1 << 34, bytes_accessed=1 << 16, transcendentals=0),
    )(xin, pair, cum, steps, read, skip)


CHIPS = NX * NZ
SAME_CORE = [[2 * chip + core for chip in range(CHIPS)] for core in range(NC)]


def chain_kernel(from_ref, into_ref):
    carried = jnp.zeros((PSIZE, STATE), F32)
    for chip in range(CHIPS):
        into_ref[chip] = carried.astype(BF)
        if chip < CHIPS - 1:
            parts = from_ref[chip, PSIZE:, :].astype(F32)
            decay = jnp.exp(parts[0:1] + parts[1:2] + parts[2:3])
            carried = decay * carried + from_ref[chip, :PSIZE, :].astype(F32)


def chain(states):
    return pl.pallas_call(
        chain_kernel,
        in_specs=[pl.BlockSpec(memory_space=pltpu.VMEM)],
        out_specs=pl.BlockSpec(memory_space=pltpu.VMEM),
        out_shape=jax.ShapeDtypeStruct((CHIPS, PSIZE, STATE), BF),
        cost_estimate=pl.CostEstimate(flops=1 << 20, bytes_accessed=1 << 16, transcendentals=0),
    )(states)


def with_logs(states, logs):
    parts = [part[:, None, None] for part in three_parts(logs)]
    row = lax.broadcasted_iota(jnp.int32, (16, 16, STATE), 1)
    extra = jnp.where(
        row == 0, parts[0], jnp.where(row == 1, parts[1], jnp.where(row == 2, parts[2], 0.0))
    )
    return jnp.concatenate([states, extra], axis=1).astype(BF)


def exchanged(value):
    return lax.all_to_all(value, "ctx", 0, 0, tiled=True, axis_index_groups=SAME_CORE)


def finish_kernel(
    core_ref, y_ref, c_ref, log_ref, in_ref, other_ref, gate_ref, gain_ref, out_ref, spread_s
):
    grown = jnp.concatenate(
        two_parts(jnp.exp(log_ref[...])) + [jnp.zeros((2 * HEADS, END_ROWS), F32)], axis=0
    ).T.astype(BF)

    @pl.when(pl.program_id(0) == 0)
    def _():
        spread_s[...] = spread_heads()

    scale = jnp.dot(grown, spread_s[...], preferred_element_type=F32)
    contract = (((1,), (1,)), ((), ()))
    kept = lax.dot_general(c_ref[...], in_ref[...], contract, preferred_element_type=F32)
    given = lax.dot_general(c_ref[...], other_ref[...], contract, preferred_element_type=F32)
    first = core_ref[0] == 0
    read = jnp.concatenate(
        [jnp.where(first, kept, given), jnp.where(first, given, kept)], axis=1
    )
    mixed = y_ref[...].astype(F32) + read * scale
    gate = gate_ref[...].astype(F32)
    gated = mixed * (gate * jax.nn.sigmoid(gate))
    mean = jnp.mean(gated * gated, axis=1, keepdims=True)
    out_ref[...] = (gated * lax.rsqrt(mean + 1e-05) * gain_ref[...]).astype(BF)


def finish(core, y, pair, logs, entering, other, gate, gain):
    return pl.pallas_call(
        finish_kernel,
        grid=(TOK // END_ROWS,),
        in_specs=[
            pl.BlockSpec(memory_space=pltpu.SMEM),
            pl.BlockSpec((END_ROWS, CHAN), lambda s: (s, 0)),
            pl.BlockSpec((END_ROWS, STATE), lambda s: (s, 1)),
            pl.BlockSpec((HEADS, END_ROWS), lambda s: (0, s)),
            pl.BlockSpec((CHAN // 2, STATE), lambda s: (0, 0)),
            pl.BlockSpec((CHAN // 2, STATE), lambda s: (0, 0)),
            pl.BlockSpec((END_ROWS, CHAN), lambda s: (s, 0)),
            pl.BlockSpec((1, CHAN), lambda s: (0, 0)),
        ],
        out_specs=pl.BlockSpec((END_ROWS, CHAN), lambda s: (s, 0)),
        out_shape=jax.ShapeDtypeStruct((TOK, CHAN), BF),
        scratch_shapes=[pltpu.VMEM((4 * HEADS, CHAN), BF)],
        compiler_params=pltpu.CompilerParams(vmem_limit_bytes=VMEM_LIMIT),
        cost_estimate=pl.CostEstimate(flops=1 << 20, bytes_accessed=1 << 16, transcendentals=0),
    )(core, y, pair, logs, entering, other, gate, gain)


QHEADS = 4
SUB = 256


def attend_kernel(flag_ref, q_ref, *refs, planes, own, fresh):
    pieces, refs = refs[: 2 * planes], refs[2 * planes :]
    if not fresh:
        in_sums, in_top, *refs = refs
    if own:
        out_sums, out_top, *refs = refs
    else:
        part_ref, *refs = refs
    kv, sums, top, qq, sa, sb, ma, mb, key_sem, in_sem, out_sem = refs
    count = flag_ref[0]
    third = flag_ref[1]
    core = flag_ref[2]

    def carried(head):
        return (
            pltpu.make_async_copy(in_sums.at[head], sums.at[head], in_sem.at[0, head]),
            pltpu.make_async_copy(in_top.at[head], top.at[head], in_sem.at[1, head]),
        )

    def leaving(head):
        return (
            pltpu.make_async_copy(sums.at[head], out_sums.at[head], out_sem.at[0, head]),
            pltpu.make_async_copy(top.at[head], out_top.at[head], out_sem.at[1, head]),
        )

    def keys(p):
        slots = pl.ds(p * NZ, NZ)
        return (
            pltpu.make_async_copy(pieces[2 * p], kv.at[slots, 0], key_sem.at[p, 0]),
            pltpu.make_async_copy(pieces[2 * p + 1], kv.at[slots, 1], key_sem.at[p, 1]),
        )

    def score(head, at, s_ref, m_ref, masked=False):
        rows_in = kv[at, :, :, :HD].reshape(CHUNK, HD)
        twice = jnp.concatenate([rows_in, rows_in], axis=1)
        for r in range(TOK // SUB):
            rows = slice(r * SUB, (r + 1) * SUB)
            s = lax.dot_general(
                qq[head, rows, :], twice, (((1,), (1,)), ((), ())), preferred_element_type=F32
            )
            if masked:
                row = lax.broadcasted_iota(jnp.int32, s.shape, 0) + r * SUB
                key = lax.broadcasted_iota(jnp.int32, s.shape, 1)
                limit = jnp.where(core == 1, 2 * TOK, TOK)
                seen = ((key < TOK) & (key <= row)) | ((key >= TOK) & (key < limit))
                s = jnp.where(seen, s, -1e30)
            s_ref[rows, :] = s
            m_ref[rows, :] = jnp.broadcast_to(jnp.max(s, axis=1, keepdims=True), (SUB, HD))

    def gather(head, at, s_ref, m_ref):
        values = kv[at, :, :, HD:].reshape(CHUNK, HD)
        values = jnp.concatenate([values, jnp.ones((CHUNK, HD), BF)], axis=1)
        for r in range(TOK // SUB):
            rows = slice(r * SUB, (r + 1) * SUB)
            old = top[head, rows, :]
            new = jnp.maximum(old, m_ref[rows, :])
            weights = jnp.exp2(s_ref[rows, :] - new[:, :1]).astype(BF)
            factor = jnp.exp2(old - new)
            part = jnp.dot(weights, values, preferred_element_type=F32)
            sums[head, rows, :] = (
                sums[head, rows, :] * jnp.concatenate([factor, factor], axis=1) + part
            )
            top[head, rows, :] = new

    if not fresh:
        for head in range(QHEADS):
            for copy in carried(head):
                copy.start()

    @pl.when(count > 0)
    def _():
        for p in range(planes):

            @pl.when(own | (p < count))
            def _():
                for copy in keys(p):
                    copy.start()

        for head in range(QHEADS):
            scaled = q_ref[:, head * HD : (head + 1) * HD].astype(F32) * (HD**-0.5 * math.log2(math.e))
            high = scaled.astype(BF)
            low = (scaled - high.astype(F32)).astype(BF)
            qq[head] = jnp.concatenate([high, low], axis=1)
            if fresh:
                sums[head] = jnp.zeros((TOK, 2 * HD), F32)
                top[head] = jnp.full((TOK, HD), -1e30, F32)
        for p in range(planes):

            @pl.when(own | (p < count))
            def _():
                for copy in keys(p):
                    copy.wait()

        if own:
            def chunk(i):
                return jnp.where(i == 2, third, jnp.minimum(i, NZ - 1))

            def one_head(head, _):
                score(head, 0, sa, ma, masked=True)

                def body(j, _):
                    i = 2 * j
                    score(head, chunk(i + 1), sb, mb)
                    gather(head, chunk(i), sa, ma)
                    score(head, chunk(i + 2), sa, ma)
                    gather(head, chunk(i + 1), sb, mb)
                    return 0

                lax.fori_loop(0, count // 2, body, 0)

                @pl.when(count % 2 == 1)
                def _():
                    gather(head, chunk(count - 1), sa, ma)

                for copy in leaving(head):
                    copy.start()
                return 0

            def full_head(head, _):
                score(head, 1, sb, mb)
                gather(head, 0, sa, ma)
                score(head, 2, sa, ma)
                gather(head, 1, sb, mb)
                score(head, 3, sb, mb)
                gather(head, 2, sa, ma)
                score(jnp.minimum(head + 1, QHEADS - 1), 0, sa, ma, masked=True)
                gather(head, 3, sb, mb)
                for copy in leaving(head):
                    copy.start()
                return 0

            @pl.when(count == NZ)
            def _():
                score(0, 0, sa, ma, masked=True)
                lax.fori_loop(0, QHEADS, full_head, 0)

            @pl.when(count < NZ)
            def _():
                lax.fori_loop(0, QHEADS, one_head, 0)

            for head in range(QHEADS):
                for copy in leaving(head):
                    copy.wait()
        else:
            steps = 2 * count

            def where_at(step):
                head = step // steps
                return jnp.minimum(head, QHEADS - 1), 2 * (step - head * steps)

            score(0, 0, sa, ma)

            def body(step, _):
                head, at = where_at(step)
                if not fresh:

                    @pl.when(at == 0)
                    def _():
                        for copy in carried(head):
                            copy.wait()

                score(head, at + 1, sb, mb)
                gather(head, at, sa, ma)
                score(*where_at(step + 1), sa, ma)
                gather(head, at + 1, sb, mb)
                return 0

            lax.fori_loop(0, QHEADS * steps, body, 0)

    if not own:
        if not fresh:

            @pl.when(count == 0)
            def _():
                for head in range(QHEADS):
                    for copy in carried(head):
                        copy.wait()

        @pl.when(jnp.logical_or(count > 0, not fresh))
        def _():
            lane = lax.broadcasted_iota(jnp.int32, (TOK, HD), 1)
            log = jnp.zeros((TOK, HD), F32)
            for head in range(QHEADS):
                total = sums[head, :, HD:]
                part_ref[:, head * HD : (head + 1) * HD] = (sums[head, :, :HD] / total).astype(BF)
                for at, part in enumerate(three_parts(top[head] + jnp.log2(total))):
                    log = jnp.where(lane == 32 * head + at, part, log)
            part_ref[:, QHEADS * HD :] = log.astype(BF)


def attend(flags, query, *pieces, carry=None, own=False):
    fresh = carry is None
    planes = len(pieces) // 2
    vmem = pl.BlockSpec(memory_space=pltpu.VMEM)
    hbm = pl.BlockSpec(memory_space=pl.ANY)
    if own:
        out = [
            jax.ShapeDtypeStruct((QHEADS, TOK, 2 * HD), F32),
            jax.ShapeDtypeStruct((QHEADS, TOK, HD), F32),
        ]
        out_specs = [hbm, hbm]
    else:
        out, out_specs = jax.ShapeDtypeStruct((TOK, (QHEADS + 1) * HD), BF), vmem
    return pl.pallas_call(
        functools.partial(attend_kernel, planes=planes, own=own, fresh=fresh),
        in_specs=[pl.BlockSpec(memory_space=pltpu.SMEM), vmem]
        + [hbm] * len(pieces)
        + ([] if fresh else [hbm, hbm]),
        out_specs=out_specs,
        out_shape=out,
        scratch_shapes=[
            pltpu.VMEM((planes * NZ, NC, TOK, 2 * HD), BF),
            pltpu.VMEM((QHEADS, TOK, 2 * HD), F32),
            pltpu.VMEM((QHEADS, TOK, HD), F32),
            pltpu.VMEM((QHEADS, TOK, 2 * HD), BF),
            pltpu.VMEM((TOK, CHUNK), F32),
            pltpu.VMEM((TOK, CHUNK), F32),
            pltpu.VMEM((TOK, HD), F32),
            pltpu.VMEM((TOK, HD), F32),
            pltpu.SemaphoreType.DMA((planes, 2)),
            pltpu.SemaphoreType.DMA((2, QHEADS)),
            pltpu.SemaphoreType.DMA((2, QHEADS)),
        ],
        compiler_params=pltpu.CompilerParams(vmem_limit_bytes=ATTEND_LIMIT),
        cost_estimate=pl.CostEstimate(
            flops=1 << 35 if fresh and not own else 1 << 20, bytes_accessed=1 << 16, transcendentals=0
        ),
    )(flags, query, *pieces, *([] if fresh else carry))


def merge_kernel(flag_ref, mine_ref, other_ref, out_ref):
    with_other = flag_ref[0] > 0

    @pl.when(jnp.logical_not(with_other))
    def _():
        out_ref[...] = mine_ref[:, : QHEADS * HD]

    @pl.when(with_other)
    def _():
        row = lax.broadcasted_iota(jnp.int32, (HD, HD), 0)
        logs = [ref[:, QHEADS * HD :] for ref in (mine_ref, other_ref)]
        for head in range(QHEADS):
            pick = jnp.where((row >= 32 * head) & (row < 32 * head + 3), 1.0, 0.0).astype(BF)
            mine, other = [jnp.dot(log, pick, preferred_element_type=F32) for log in logs]
            new = jnp.maximum(mine, other)
            mine, other = jnp.exp2(mine - new), jnp.exp2(other - new)
            columns = slice(head * HD, (head + 1) * HD)
            joint = mine_ref[:, columns].astype(F32) * mine + other_ref[:, columns].astype(F32) * other
            out_ref[:, columns] = (joint / (mine + other)).astype(BF)


def merge(flags, part, other):
    rows = TOK // 2
    wide = pl.BlockSpec((rows, (QHEADS + 1) * HD), lambda r: (r, 0))
    return pl.pallas_call(
        merge_kernel,
        grid=(TOK // rows,),
        in_specs=[pl.BlockSpec(memory_space=pltpu.SMEM), wide, wide],
        out_specs=pl.BlockSpec((rows, QHEADS * HD), lambda r: (r, 0)),
        out_shape=jax.ShapeDtypeStruct((TOK, QHEADS * HD), BF),
        compiler_params=pltpu.CompilerParams(vmem_limit_bytes=ATTEND_LIMIT),
        cost_estimate=pl.CostEstimate(flops=1 << 20, bytes_accessed=1 << 16, transcendentals=0),
    )(flags, part, other)


def local(
    hidden,
    dt_weight,
    dt_bias,
    decay_rate,
    skip_gain,
    ssm_in,
    bc_in,
    conv_x,
    conv_bc,
    gate_in,
    norm_gain,
    query_heads,
    key_heads,
    value_heads,
):
    mine = lax.axis_index("ctx")
    x, z, c = mine // (NZ * NC), (mine // NC) % NZ, mine % NC
    core = c.astype(jnp.int32)[None]

    def flags(count):
        return jnp.stack([count, jnp.where(z == NZ - 1, 2, 3), c]).astype(jnp.int32)

    bc = bc_in.reshape(TOK, 2 * STATE)
    partial = lax.dot_general(
        dt_weight, hidden, (((0,), (1,)), ((), ())), preferred_element_type=F32
    )
    partial, keys, ends_x, ends_bc = lax.optimization_barrier(
        (partial, key_heads, ssm_in[TOK - 16 :], bc[TOK - 16 :])
    )
    ends = jnp.concatenate([ends_x, ends_bc], axis=1)
    tail = lax.ppermute(ends, "ctx", [(i, i + 1) for i in range(31)])
    parts = lax.all_to_all(partial.reshape(8, HEADS, TOK), "head", 0, 0, tiled=True)
    xin, pair = convolved(ssm_in, tail, bc, conv_x, conv_bc.reshape(4, 2 * STATE))
    rows = jnp.concatenate([keys, value_heads], axis=1)
    up, down, two = along_z(rows, 1), along_z(rows, -1), along_z(rows, 2)
    parts, xin, pair = lax.optimization_barrier((parts, xin, pair))
    steps = jax.nn.softplus(jnp.sum(parts, axis=0) + dt_bias[:, None])
    drop = -steps * decay_rate[:, None]
    total = jnp.sum(drop, axis=1)
    cum, logs, read, keep, give = own_states(core, xin, pair, steps, drop)

    keep, give, up, down = lax.optimization_barrier((keep, give, up, down))
    other = swap_core(give)
    partner = jnp.sum(other[CHAN // 2, : 3 * HEADS].astype(F32).reshape(3, HEADS), axis=0)
    other = other[: CHAN // 2]
    by_half = lambda value: lax.dynamic_index_in_dim(value.reshape(2, 16), c, 0, False)
    shape = (16, PSIZE, STATE)
    log_first = by_half(jnp.where(c == 0, total, partner))
    log_second = by_half(jnp.where(c == 0, partner, total))
    early = jnp.where(c == 0, keep, other).reshape(shape).astype(F32)
    late = jnp.where(c == 0, other, keep).reshape(shape).astype(F32)
    both = with_logs(
        late + jnp.exp(log_second)[:, None, None] * early, log_first + log_second
    )
    collected = exchanged(both)
    both, xin, rows, up, down, two, query = lax.optimization_barrier(
        (both, xin, rows, up, down, two, query_heads)
    )
    visitor = send(query, lambda x, z, c: (x - 2, z, c) if x >= 2 else None)
    y = inside_blocks(xin, pair, cum, steps, read, jnp.repeat(skip_gain, PSIZE)[None])
    plane = jnp.stack([rows, up, down, two])
    plane_pair = swap_core(plane)
    left = along_x(plane, 1)
    right = send(plane, lambda x, z, c: (NX - 1, z, c) if x == 0 else None)
    seen = attend(flags(z + 1), query, plane, plane_pair, own=True)
    collected, y, seen = lax.optimization_barrier((collected, y, seen))
    carried = chain(collected)
    chip_in = exchanged(carried)
    planes_seen = jnp.where(x == 0, 0, jnp.where(x == NX - 1, 2, 1))
    carried, to_visit, to_see, visitor, left, right = lax.optimization_barrier(
        (carried, flags(jnp.where(x <= 1, 1, 0)), flags(planes_seen), visitor, left, right)
    )
    left_pair = swap_core(left)
    right_pair = swap_core(right)
    part = attend(to_visit, visitor, plane, plane_pair)
    part, to_see = lax.optimization_barrier((part, to_see))
    part = send(part, lambda x, z, c: (x + 2, z, c) if x <= 1 else None)
    seen = attend(to_see, query, left, left_pair, right, right_pair, carry=seen)
    chip_in, seen = lax.optimization_barrier((chip_in, seen))
    after = (early + jnp.exp(log_first)[:, None, None] * chip_in.astype(F32)).astype(BF)
    entering = jnp.where(c == 0, chip_in, after).reshape(CHAN // 2, STATE)
    sent = jnp.where(c == 0, after, chip_in).reshape(CHAN // 2, STATE)
    received = swap_core(sent)
    sent, seen = lax.optimization_barrier((sent, seen))
    attn_out = merge(flags(jnp.where(x >= 2, 1, 0)), seen, part)
    received, attn_out = lax.optimization_barrier((received, attn_out))
    mamba_out = finish(core, y, pair, logs, entering, received, gate_in, norm_gain[None])
    return (mamba_out, attn_out)


def solution(mesh):
    in_specs = (
        P("ctx", "head"),
        P("head", None),
        P("head"),
        P("head"),
        P("head"),
        P("ctx", "head"),
        P("ctx", "head", None),
        P(None, "head"),
        P(None, "head", None),
        P("ctx", "head"),
        P("head"),
        P("ctx", "head"),
        P("ctx", "head"),
        P("ctx", "head"),
    )
    out_specs = (P("ctx", "head"), P("ctx", "head"))
    return jax.shard_map(local, mesh=mesh, in_specs=in_specs, out_specs=out_specs, check_vma=False)
```

```python
import functools
import math

import jax
import jax.numpy as jnp
from jax import lax
from jax.experimental import pallas as pl
from jax.experimental.pallas import tpu as pltpu
from jax.sharding import PartitionSpec as P

SPAN = 128
HD = 128
BF = jnp.bfloat16
F32 = jnp.float32
NX, NZ, NC = 4, 4, 2
HEADS, PSIZE, STATE = 32, 64, 256
CHAN = HEADS * PSIZE
TOK = 512
HB = 32
HBC = HB * PSIZE
CHUNK = 1024
VMEM_LIMIT = 58 << 20
ATTEND_LIMIT = 22 << 20
CONV_ROWS = 256
END_ROWS = 256


def pairs_of(move):
    found = []
    for x in range(NX):
        for z in range(NZ):
            for c in range(NC):
                target = move(x, z, c)
                if target is not None:
                    tx, tz, tc = target
                    found.append(((x * NZ + z) * NC + c, (tx * NZ + tz) * NC + tc))
    return found


def send(value, move):
    return lax.ppermute(value, "ctx", pairs_of(move))


def swap_core(value):
    return send(value, lambda x, z, c: (x, z, 1 - c))


def along_z(value, steps):
    return send(value, lambda x, z, c: (x, (z + steps) % NZ, c))


def along_x(value, steps, wrap=False):
    def move(x, z, c):
        if wrap or 0 <= x + steps < NX:
            return ((x + steps) % NX, z, c)
        return None

    return send(value, move)


def shifted_rows(rows, tail, steps):
    if steps == 0:
        return rows
    rolled = pltpu.roll(rows, steps, 0)
    before = pltpu.roll(tail, steps, 0)
    at = lax.broadcasted_iota(jnp.int32, before.shape, 0)
    top = jnp.where(at < steps, before, rolled[:8])
    return jnp.concatenate([top, rolled[8:]], axis=0)


def conv_silu(rows, tail, taps):
    taps_count = taps.shape[0]
    total = None
    for k in range(taps_count):
        term = taps[k : k + 1] * shifted_rows(rows, tail, taps_count - 1 - k)
        total = term if total is None else total + term
    return (total * jax.nn.sigmoid(total)).astype(BF)


def two_parts(value):
    high = value.astype(BF).astype(F32)
    return [high, (value - high).astype(BF).astype(F32)]


def three_parts(value):
    high = value.astype(BF).astype(F32)
    return [high] + two_parts(value - high)


def conv_kernel(
    x_ref, before_ref, xtail_ref, pair_ref, pbefore_ref, ptail_ref, taps_ref, ptaps_ref, xin_ref, conv_ref
):
    first = pl.program_id(0) == 0
    before = jnp.where(first, ptail_ref[...], pbefore_ref[...]).astype(F32)[8:]
    conv_ref[...] = conv_silu(pair_ref[...].astype(F32), before, ptaps_ref[...])
    before = jnp.where(first, xtail_ref[...], before_ref[...]).astype(F32)[8:]
    xin_ref[...] = conv_silu(x_ref[...].astype(F32), before, taps_ref[...])


def convolved(ssm_in, tail, bc_in, conv_x, conv_bc):
    prior = lambda s: (jnp.maximum(s * (CONV_ROWS // 16) - 1, 0), 0)
    return pl.pallas_call(
        conv_kernel,
        grid=(TOK // CONV_ROWS,),
        in_specs=[
            pl.BlockSpec((CONV_ROWS, CHAN), lambda s: (s, 0)),
            pl.BlockSpec((16, CHAN), prior),
            pl.BlockSpec((16, CHAN), lambda s: (0, 0)),
            pl.BlockSpec((CONV_ROWS, 2 * STATE), lambda s: (s, 0)),
            pl.BlockSpec((16, 2 * STATE), prior),
            pl.BlockSpec((16, 2 * STATE), lambda s: (0, CHAN // (2 * STATE))),
            pl.BlockSpec((4, CHAN), lambda s: (0, 0)),
            pl.BlockSpec((4, 2 * STATE), lambda s: (0, 0)),
        ],
        out_specs=[
            pl.BlockSpec((CONV_ROWS, CHAN), lambda s: (s, 0)),
            pl.BlockSpec((CONV_ROWS, 2 * STATE), lambda s: (s, 0)),
        ],
        out_shape=[
            jax.ShapeDtypeStruct((TOK, CHAN), BF),
            jax.ShapeDtypeStruct((TOK, 2 * STATE), BF),
        ],
        compiler_params=pltpu.CompilerParams(vmem_limit_bytes=VMEM_LIMIT),
        cost_estimate=pl.CostEstimate(flops=1 << 20, bytes_accessed=1 << 16, transcendentals=0),
    )(ssm_in, ssm_in, tail, bc_in, bc_in, tail, conv_x, conv_bc)


def states_kernel(
    core_ref,
    xin_ref,
    pair_ref,
    steps_ref,
    drop_ref,
    cum_ref,
    log_ref,
    read_ref,
    mine_ref,
    give_ref,
    log_s,
    state_s,
    spread_s,
    rows_s,
):
    span = pl.program_id(0)

    @pl.when(span == 0)
    def _():
        log_s[...] = jnp.zeros_like(log_s)
        state_s[...] = jnp.zeros_like(state_s)
        spread_s[...] = spread_heads()
        channel = lax.broadcasted_iota(jnp.int32, (CHAN, 4 * HEADS), 0)
        column = lax.broadcasted_iota(jnp.int32, (CHAN, 4 * HEADS), 1)
        hit = (column < 2 * HEADS) & (column % HEADS == channel // PSIZE)
        rows_s[...] = jnp.where(hit, 1.0, 0.0).astype(BF)

    at_i = lax.broadcasted_iota(jnp.int32, (SPAN, SPAN), 0)
    at_j = lax.broadcasted_iota(jnp.int32, (SPAN, SPAN), 1)
    upper = jnp.where(at_i <= at_j, 1.0, 0.0)
    cum = jnp.dot(
        drop_ref[...], upper, precision=lax.Precision.HIGHEST, preferred_element_type=F32
    )
    cum_ref[...] = cum
    last = cum[:, SPAN - 1 : SPAN]
    scales = jnp.concatenate(
        two_parts(jnp.exp(last - cum) * steps_ref[...]) + [jnp.zeros((2 * HEADS, SPAN), F32)], axis=0
    ).T.astype(BF)
    decays = jnp.broadcast_to(
        jnp.concatenate(two_parts(jnp.exp(last)) + [jnp.zeros((2 * HEADS, 1), F32)], axis=0),
        (4 * HEADS, STATE),
    ).astype(BF)
    log_ref[...] = log_s[...] + cum
    log_s[...] = log_s[...] + last
    weight = jnp.dot(scales, spread_s[...], preferred_element_type=F32)
    weighted = (xin_ref[...].astype(F32) * weight).astype(BF)
    gain = lax.dot_general(
        weighted, pair_ref[:, :STATE], (((0,), (0,)), ((), ())), preferred_element_type=F32
    )
    decay = jnp.dot(rows_s[...], decays, preferred_element_type=F32)
    state = state_s[...]
    read_ref[...] = lax.dot_general(
        pair_ref[:, STATE:], state.astype(BF), (((1,), (1,)), ((), ())), preferred_element_type=F32
    ).astype(BF)
    state = state * decay + gain
    state_s[...] = state

    @pl.when(span == TOK // SPAN - 1)
    def _():
        low = state.astype(BF)
        first = core_ref[0] == 0
        mine_ref[...] = jnp.where(first, low[: CHAN // 2], low[CHAN // 2 :])
        give_ref[: CHAN // 2, :] = jnp.where(first, low[CHAN // 2 :], low[: CHAN // 2])
        parts = three_parts(log_s[...]) + [jnp.zeros((HEADS, SPAN), F32)]
        rows = jnp.concatenate(parts, axis=0).T[:16].astype(BF)
        give_ref[CHAN // 2 :, :] = jnp.concatenate([rows, jnp.zeros_like(rows)], axis=1)


def spread_heads():
    row = lax.broadcasted_iota(jnp.int32, (4 * HEADS, CHAN), 0)
    channel = lax.broadcasted_iota(jnp.int32, (4 * HEADS, CHAN), 1)
    hit = (row < 2 * HEADS) & (row % HEADS == channel // PSIZE)
    return jnp.where(hit, 1.0, 0.0).astype(BF)


def spread_columns():
    row = lax.broadcasted_iota(jnp.int32, (4 * HEADS, HEADS * SPAN), 0)
    column = lax.broadcasted_iota(jnp.int32, (4 * HEADS, HEADS * SPAN), 1)
    hit = (row < 3 * HEADS) & (row % HEADS == column // SPAN)
    return jnp.where(hit, 1.0, 0.0).astype(BF)


def own_states(core, xin, pair, steps, drop):
    return pl.pallas_call(
        states_kernel,
        grid=(TOK // SPAN,),
        in_specs=[
            pl.BlockSpec(memory_space=pltpu.SMEM),
            pl.BlockSpec((SPAN, CHAN), lambda s: (s, 0)),
            pl.BlockSpec((SPAN, 2 * STATE), lambda s: (s, 0)),
            pl.BlockSpec((HEADS, SPAN), lambda s: (0, s)),
            pl.BlockSpec((HEADS, SPAN), lambda s: (0, s)),
        ],
        out_specs=[
            pl.BlockSpec((HEADS, SPAN), lambda s: (0, s)),
            pl.BlockSpec((HEADS, SPAN), lambda s: (0, s)),
            pl.BlockSpec((SPAN, CHAN), lambda s: (s, 0)),
            pl.BlockSpec((CHAN // 2, STATE), lambda s: (0, 0)),
            pl.BlockSpec((CHAN // 2 + 16, STATE), lambda s: (0, 0)),
        ],
        out_shape=[
            jax.ShapeDtypeStruct((HEADS, TOK), F32),
            jax.ShapeDtypeStruct((HEADS, TOK), F32),
            jax.ShapeDtypeStruct((TOK, CHAN), BF),
            jax.ShapeDtypeStruct((CHAN // 2, STATE), BF),
            jax.ShapeDtypeStruct((CHAN // 2 + 16, STATE), BF),
        ],
        scratch_shapes=[
            pltpu.VMEM((HEADS, SPAN), F32),
            pltpu.VMEM((CHAN, STATE), F32),
            pltpu.VMEM((4 * HEADS, CHAN), BF),
            pltpu.VMEM((CHAN, 4 * HEADS), BF),
        ],
        compiler_params=pltpu.CompilerParams(vmem_limit_bytes=VMEM_LIMIT),
        cost_estimate=pl.CostEstimate(flops=1 << 20, bytes_accessed=1 << 16, transcendentals=0),
    )(core, xin, pair, steps, drop)


def inside_span(
    part,
    xin_ref,
    pair_ref,
    cum_ref,
    steps_ref,
    read_ref,
    skip_ref,
    y_ref,
    g_s,
    ci_s,
    ex_s,
    log_s,
    spread_s,
    column_s,
):
    block = pl.program_id(1)
    cmat = pair_ref[:, STATE:]

    @pl.when((block == 0) & (pl.program_id(0) == 0) & (part == 0))
    def _():
        spread_s[...] = spread_heads()
        column_s[...] = spread_columns()

    @pl.when(block == 0)
    def _():
        product = lax.dot_general(
            cmat, pair_ref[:, :STATE], (((1,), (1,)), ((), ())), preferred_element_type=F32
        )
        at_i = lax.broadcasted_iota(jnp.int32, (SPAN, SPAN), 0)
        at_j = lax.broadcasted_iota(jnp.int32, (SPAN, SPAN), 1)
        g_s[...] = jnp.where(at_j <= at_i, product, 0.0)
        cum = cum_ref[...]
        log_s[...] = jnp.log(steps_ref[...])
        ci_s[...] = jnp.concatenate(three_parts(cum) + [jnp.zeros_like(cum)], axis=0).T.astype(BF)
        ex_s[...] = jnp.concatenate(
            two_parts(jnp.exp(cum)) + [jnp.zeros((2 * HEADS, SPAN), F32)], axis=0
        ).T.astype(BF)

    xf = xin_ref[...].astype(F32)
    grown = jnp.dot(ex_s[...], spread_s[...], preferred_element_type=F32)
    rows_i = jnp.dot(ci_s[...], column_s[...], preferred_element_type=F32)
    base = read_ref[...].astype(F32) * grown + skip_ref[...] * xf
    cum_rows = cum_ref[pl.ds(pl.multiple_of(block * HB, HB), HB), :]
    log_rows = log_s[pl.ds(pl.multiple_of(block * HB, HB), HB), :]
    cum_rows = cum_rows - log_rows
    masked = g_s[...]
    lane = lax.broadcasted_iota(jnp.int32, (SPAN, 2 * PSIZE), 1)
    for pair in range(HB // 2):
        mixes = []
        for h in (2 * pair, 2 * pair + 1):
            gap = rows_i[:, h * SPAN : (h + 1) * SPAN] - cum_rows[h : h + 1]
            mixes.append((masked * jnp.exp(jnp.minimum(gap, log_rows[h : h + 1]))).astype(BF))
        two = xf[:, pair * 128 : (pair + 1) * 128]
        left = jnp.where(lane < PSIZE, two, 0.0).astype(BF)
        right = jnp.where(lane < PSIZE, 0.0, two).astype(BF)
        intra = jnp.dot(
            jnp.concatenate(mixes, axis=1),
            jnp.concatenate([left, right], axis=0),
            preferred_element_type=F32,
        )
        y_ref[:, pair * 128 : (pair + 1) * 128] = (
            base[:, pair * 128 : (pair + 1) * 128] + intra
        ).astype(BF)


def inside_kernel(xin_ref, pair_ref, cum_ref, steps_ref, read_ref, skip_ref, y_ref, *scratch):
    for part in range(2):
        at = pl.ds(part * SPAN, SPAN)
        inside_span(
            part,
            xin_ref.at[at, :],
            pair_ref.at[at, :],
            cum_ref.at[:, at],
            steps_ref.at[:, at],
            read_ref.at[at, :],
            skip_ref,
            y_ref.at[at, :],
            *scratch,
        )


def inside_blocks(xin, pair, cum, steps, read, skip):
    blocks = HEADS // HB
    return pl.pallas_call(
        inside_kernel,
        grid=(TOK // (2 * SPAN), blocks),
        in_specs=[
            pl.BlockSpec((2 * SPAN, HBC), lambda s, b: (s, b)),
            pl.BlockSpec((2 * SPAN, 2 * STATE), lambda s, b: (s, 0)),
            pl.BlockSpec((HEADS, 2 * SPAN), lambda s, b: (0, s)),
            pl.BlockSpec((HEADS, 2 * SPAN), lambda s, b: (0, s)),
            pl.BlockSpec((2 * SPAN, HBC), lambda s, b: (s, b)),
            pl.BlockSpec((1, HBC), lambda s, b: (0, b)),
        ],
        out_specs=pl.BlockSpec((2 * SPAN, HBC), lambda s, b: (s, b)),
        out_shape=jax.ShapeDtypeStruct((TOK, CHAN), BF),
        scratch_shapes=[
            pltpu.VMEM((SPAN, SPAN), F32),
            pltpu.VMEM((SPAN, 4 * HEADS), BF),
            pltpu.VMEM((SPAN, 4 * HEADS), BF),
            pltpu.VMEM((HEADS, SPAN), F32),
            pltpu.VMEM((4 * HEADS, CHAN), BF),
            pltpu.VMEM((4 * HEADS, HEADS * SPAN), BF),
        ],
        compiler_params=pltpu.CompilerParams(vmem_limit_bytes=VMEM_LIMIT),
        cost_estimate=pl.CostEstimate(flops=1 << 34, bytes_accessed=1 << 16, transcendentals=0),
    )(xin, pair, cum, steps, read, skip)


CHIPS = NX * NZ
SAME_CORE = [[2 * chip + core for chip in range(CHIPS)] for core in range(NC)]


def chain_kernel(from_ref, into_ref):
    carried = jnp.zeros((PSIZE, STATE), F32)
    for chip in range(CHIPS):
        into_ref[chip] = carried.astype(BF)
        if chip < CHIPS - 1:
            parts = from_ref[chip, PSIZE:, :].astype(F32)
            decay = jnp.exp(parts[0:1] + parts[1:2] + parts[2:3])
            carried = decay * carried + from_ref[chip, :PSIZE, :].astype(F32)


def chain(states):
    return pl.pallas_call(
        chain_kernel,
        in_specs=[pl.BlockSpec(memory_space=pltpu.VMEM)],
        out_specs=pl.BlockSpec(memory_space=pltpu.VMEM),
        out_shape=jax.ShapeDtypeStruct((CHIPS, PSIZE, STATE), BF),
        cost_estimate=pl.CostEstimate(flops=1 << 20, bytes_accessed=1 << 16, transcendentals=0),
    )(states)


def with_logs(states, logs):
    parts = [part[:, None, None] for part in three_parts(logs)]
    row = lax.broadcasted_iota(jnp.int32, (16, 16, STATE), 1)
    extra = jnp.where(
        row == 0, parts[0], jnp.where(row == 1, parts[1], jnp.where(row == 2, parts[2], 0.0))
    )
    return jnp.concatenate([states, extra], axis=1).astype(BF)


def exchanged(value):
    return lax.all_to_all(value, "ctx", 0, 0, tiled=True, axis_index_groups=SAME_CORE)


def finish_kernel(
    core_ref, y_ref, c_ref, log_ref, in_ref, other_ref, gate_ref, gain_ref, out_ref, spread_s
):
    grown = jnp.concatenate(
        two_parts(jnp.exp(log_ref[...])) + [jnp.zeros((2 * HEADS, END_ROWS), F32)], axis=0
    ).T.astype(BF)

    @pl.when(pl.program_id(0) == 0)
    def _():
        spread_s[...] = spread_heads()

    scale = jnp.dot(grown, spread_s[...], preferred_element_type=F32)
    contract = (((1,), (1,)), ((), ()))
    kept = lax.dot_general(c_ref[...], in_ref[...], contract, preferred_element_type=F32)
    given = lax.dot_general(c_ref[...], other_ref[...], contract, preferred_element_type=F32)
    first = core_ref[0] == 0
    read = jnp.concatenate(
        [jnp.where(first, kept, given), jnp.where(first, given, kept)], axis=1
    )
    mixed = y_ref[...].astype(F32) + read * scale
    gate = gate_ref[...].astype(F32)
    gated = mixed * (gate * jax.nn.sigmoid(gate))
    mean = jnp.mean(gated * gated, axis=1, keepdims=True)
    out_ref[...] = (gated * lax.rsqrt(mean + 1e-05) * gain_ref[...]).astype(BF)


def finish(core, y, pair, logs, entering, other, gate, gain):
    return pl.pallas_call(
        finish_kernel,
        grid=(TOK // END_ROWS,),
        in_specs=[
            pl.BlockSpec(memory_space=pltpu.SMEM),
            pl.BlockSpec((END_ROWS, CHAN), lambda s: (s, 0)),
            pl.BlockSpec((END_ROWS, STATE), lambda s: (s, 1)),
            pl.BlockSpec((HEADS, END_ROWS), lambda s: (0, s)),
            pl.BlockSpec((CHAN // 2, STATE), lambda s: (0, 0)),
            pl.BlockSpec((CHAN // 2, STATE), lambda s: (0, 0)),
            pl.BlockSpec((END_ROWS, CHAN), lambda s: (s, 0)),
            pl.BlockSpec((1, CHAN), lambda s: (0, 0)),
        ],
        out_specs=pl.BlockSpec((END_ROWS, CHAN), lambda s: (s, 0)),
        out_shape=jax.ShapeDtypeStruct((TOK, CHAN), BF),
        scratch_shapes=[pltpu.VMEM((4 * HEADS, CHAN), BF)],
        compiler_params=pltpu.CompilerParams(vmem_limit_bytes=VMEM_LIMIT),
        cost_estimate=pl.CostEstimate(flops=1 << 20, bytes_accessed=1 << 16, transcendentals=0),
    )(core, y, pair, logs, entering, other, gate, gain)


QHEADS = 4
SUB = 256


def attend_kernel(flag_ref, q_ref, *refs, planes, own, fresh):
    pieces, refs = refs[: 2 * planes], refs[2 * planes :]
    if not fresh:
        in_sums, in_top, *refs = refs
    if own:
        out_sums, out_top, *refs = refs
    else:
        part_ref, *refs = refs
    kv, sums, top, qq, sa, sb, ma, mb, key_sem, in_sem, out_sem = refs
    count = flag_ref[0]
    third = flag_ref[1]
    core = flag_ref[2]

    def carried(head):
        return (
            pltpu.make_async_copy(in_sums.at[head], sums.at[head], in_sem.at[0, head]),
            pltpu.make_async_copy(in_top.at[head], top.at[head], in_sem.at[1, head]),
        )

    def leaving(head):
        return (
            pltpu.make_async_copy(sums.at[head], out_sums.at[head], out_sem.at[0, head]),
            pltpu.make_async_copy(top.at[head], out_top.at[head], out_sem.at[1, head]),
        )

    def keys(p):
        slots = pl.ds(p * NZ, NZ)
        return (
            pltpu.make_async_copy(pieces[2 * p], kv.at[slots, 0], key_sem.at[p, 0]),
            pltpu.make_async_copy(pieces[2 * p + 1], kv.at[slots, 1], key_sem.at[p, 1]),
        )

    def score(head, at, s_ref, m_ref, masked=False):
        rows_in = kv[at, :, :, :HD].reshape(CHUNK, HD)
        twice = jnp.concatenate([rows_in, rows_in], axis=1)
        for r in range(TOK // SUB):
            rows = slice(r * SUB, (r + 1) * SUB)
            s = lax.dot_general(
                qq[head, rows, :], twice, (((1,), (1,)), ((), ())), preferred_element_type=F32
            )
            if masked:
                row = lax.broadcasted_iota(jnp.int32, s.shape, 0) + r * SUB
                key = lax.broadcasted_iota(jnp.int32, s.shape, 1)
                limit = jnp.where(core == 1, 2 * TOK, TOK)
                seen = ((key < TOK) & (key <= row)) | ((key >= TOK) & (key < limit))
                s = jnp.where(seen, s, -1e30)
            s_ref[rows, :] = s
            m_ref[rows, :] = jnp.broadcast_to(jnp.max(s, axis=1, keepdims=True), (SUB, HD))

    def gather(head, at, s_ref, m_ref):
        values = kv[at, :, :, HD:].reshape(CHUNK, HD)
        values = jnp.concatenate([values, jnp.ones((CHUNK, HD), BF)], axis=1)
        for r in range(TOK // SUB):
            rows = slice(r * SUB, (r + 1) * SUB)
            old = top[head, rows, :]
            new = jnp.maximum(old, m_ref[rows, :])
            weights = jnp.exp2(s_ref[rows, :] - new[:, :1]).astype(BF)
            factor = jnp.exp2(old - new)
            part = jnp.dot(weights, values, preferred_element_type=F32)
            sums[head, rows, :] = (
                sums[head, rows, :] * jnp.concatenate([factor, factor], axis=1) + part
            )
            top[head, rows, :] = new

    if not fresh:
        for head in range(QHEADS):
            for copy in carried(head):
                copy.start()

    @pl.when(count > 0)
    def _():
        for p in range(planes):

            @pl.when(own | (p < count))
            def _():
                for copy in keys(p):
                    copy.start()

        for head in range(QHEADS):
            scaled = q_ref[:, head * HD : (head + 1) * HD].astype(F32) * (HD**-0.5 * math.log2(math.e))
            high = scaled.astype(BF)
            low = (scaled - high.astype(F32)).astype(BF)
            qq[head] = jnp.concatenate([high, low], axis=1)
            if fresh:
                sums[head] = jnp.zeros((TOK, 2 * HD), F32)
                top[head] = jnp.full((TOK, HD), -1e30, F32)
        for p in range(planes):

            @pl.when(own | (p < count))
            def _():
                for copy in keys(p):
                    copy.wait()

        if own:
            def chunk(i):
                return jnp.where(i == 2, third, jnp.minimum(i, NZ - 1))

            def one_head(head, _):
                score(head, 0, sa, ma, masked=True)

                def body(j, _):
                    i = 2 * j
                    score(head, chunk(i + 1), sb, mb)
                    gather(head, chunk(i), sa, ma)
                    score(head, chunk(i + 2), sa, ma)
                    gather(head, chunk(i + 1), sb, mb)
                    return 0

                lax.fori_loop(0, count // 2, body, 0)

                @pl.when(count % 2 == 1)
                def _():
                    gather(head, chunk(count - 1), sa, ma)

                for copy in leaving(head):
                    copy.start()
                return 0

            def full_head(head, _):
                score(head, 1, sb, mb)
                gather(head, 0, sa, ma)
                score(head, 2, sa, ma)
                gather(head, 1, sb, mb)
                score(head, 3, sb, mb)
                gather(head, 2, sa, ma)
                score(jnp.minimum(head + 1, QHEADS - 1), 0, sa, ma, masked=True)
                gather(head, 3, sb, mb)
                for copy in leaving(head):
                    copy.start()
                return 0

            @pl.when(count == NZ)
            def _():
                score(0, 0, sa, ma, masked=True)
                lax.fori_loop(0, QHEADS, full_head, 0)

            @pl.when(count < NZ)
            def _():
                lax.fori_loop(0, QHEADS, one_head, 0)

            for head in range(QHEADS):
                for copy in leaving(head):
                    copy.wait()
        else:
            steps = 2 * count

            def where_at(step):
                head = step // steps
                return jnp.minimum(head, QHEADS - 1), 2 * (step - head * steps)

            score(0, 0, sa, ma)

            def body(step, _):
                head, at = where_at(step)
                if not fresh:

                    @pl.when(at == 0)
                    def _():
                        for copy in carried(head):
                            copy.wait()

                score(head, at + 1, sb, mb)
                gather(head, at, sa, ma)
                score(*where_at(step + 1), sa, ma)
                gather(head, at + 1, sb, mb)
                return 0

            lax.fori_loop(0, QHEADS * steps, body, 0)

    if not own:
        if not fresh:

            @pl.when(count == 0)
            def _():
                for head in range(QHEADS):
                    for copy in carried(head):
                        copy.wait()

        @pl.when(jnp.logical_or(count > 0, not fresh))
        def _():
            lane = lax.broadcasted_iota(jnp.int32, (TOK, HD), 1)
            log = jnp.zeros((TOK, HD), F32)
            for head in range(QHEADS):
                total = sums[head, :, HD:]
                part_ref[:, head * HD : (head + 1) * HD] = (sums[head, :, :HD] / total).astype(BF)
                for at, part in enumerate(three_parts(top[head] + jnp.log2(total))):
                    log = jnp.where(lane == 32 * head + at, part, log)
            part_ref[:, QHEADS * HD :] = log.astype(BF)


def attend(flags, query, *pieces, carry=None, own=False):
    fresh = carry is None
    planes = len(pieces) // 2
    vmem = pl.BlockSpec(memory_space=pltpu.VMEM)
    hbm = pl.BlockSpec(memory_space=pl.ANY)
    if own:
        out = [
            jax.ShapeDtypeStruct((QHEADS, TOK, 2 * HD), F32),
            jax.ShapeDtypeStruct((QHEADS, TOK, HD), F32),
        ]
        out_specs = [hbm, hbm]
    else:
        out, out_specs = jax.ShapeDtypeStruct((TOK, (QHEADS + 1) * HD), BF), vmem
    return pl.pallas_call(
        functools.partial(attend_kernel, planes=planes, own=own, fresh=fresh),
        in_specs=[pl.BlockSpec(memory_space=pltpu.SMEM), vmem]
        + [hbm] * len(pieces)
        + ([] if fresh else [hbm, hbm]),
        out_specs=out_specs,
        out_shape=out,
        scratch_shapes=[
            pltpu.VMEM((planes * NZ, NC, TOK, 2 * HD), BF),
            pltpu.VMEM((QHEADS, TOK, 2 * HD), F32),
            pltpu.VMEM((QHEADS, TOK, HD), F32),
            pltpu.VMEM((QHEADS, TOK, 2 * HD), BF),
            pltpu.VMEM((TOK, CHUNK), F32),
            pltpu.VMEM((TOK, CHUNK), F32),
            pltpu.VMEM((TOK, HD), F32),
            pltpu.VMEM((TOK, HD), F32),
            pltpu.SemaphoreType.DMA((planes, 2)),
            pltpu.SemaphoreType.DMA((2, QHEADS)),
            pltpu.SemaphoreType.DMA((2, QHEADS)),
        ],
        compiler_params=pltpu.CompilerParams(vmem_limit_bytes=ATTEND_LIMIT),
        cost_estimate=pl.CostEstimate(
            flops=1 << 35 if fresh and not own else 1 << 20, bytes_accessed=1 << 16, transcendentals=0
        ),
    )(flags, query, *pieces, *([] if fresh else carry))


def merge_kernel(flag_ref, mine_ref, other_ref, out_ref):
    with_other = flag_ref[0] > 0

    @pl.when(jnp.logical_not(with_other))
    def _():
        out_ref[...] = mine_ref[:, : QHEADS * HD]

    @pl.when(with_other)
    def _():
        row = lax.broadcasted_iota(jnp.int32, (HD, HD), 0)
        logs = [ref[:, QHEADS * HD :] for ref in (mine_ref, other_ref)]
        for head in range(QHEADS):
            pick = jnp.where((row >= 32 * head) & (row < 32 * head + 3), 1.0, 0.0).astype(BF)
            mine, other = [jnp.dot(log, pick, preferred_element_type=F32) for log in logs]
            new = jnp.maximum(mine, other)
            mine, other = jnp.exp2(mine - new), jnp.exp2(other - new)
            columns = slice(head * HD, (head + 1) * HD)
            joint = mine_ref[:, columns].astype(F32) * mine + other_ref[:, columns].astype(F32) * other
            out_ref[:, columns] = (joint / (mine + other)).astype(BF)


def merge(flags, part, other):
    rows = TOK // 2
    wide = pl.BlockSpec((rows, (QHEADS + 1) * HD), lambda r: (r, 0))
    return pl.pallas_call(
        merge_kernel,
        grid=(TOK // rows,),
        in_specs=[pl.BlockSpec(memory_space=pltpu.SMEM), wide, wide],
        out_specs=pl.BlockSpec((rows, QHEADS * HD), lambda r: (r, 0)),
        out_shape=jax.ShapeDtypeStruct((TOK, QHEADS * HD), BF),
        compiler_params=pltpu.CompilerParams(vmem_limit_bytes=ATTEND_LIMIT),
        cost_estimate=pl.CostEstimate(flops=1 << 20, bytes_accessed=1 << 16, transcendentals=0),
    )(flags, part, other)


def local(
    hidden,
    dt_weight,
    dt_bias,
    decay_rate,
    skip_gain,
    ssm_in,
    bc_in,
    conv_x,
    conv_bc,
    gate_in,
    norm_gain,
    query_heads,
    key_heads,
    value_heads,
):
    mine = lax.axis_index("ctx")
    x, z, c = mine // (NZ * NC), (mine // NC) % NZ, mine % NC
    core = c.astype(jnp.int32)[None]

    def flags(count):
        return jnp.stack([count, jnp.where(z == NZ - 1, 2, 3), c]).astype(jnp.int32)

    bc = bc_in.reshape(TOK, 2 * STATE)
    partial = lax.dot_general(
        dt_weight, hidden, (((0,), (1,)), ((), ())), preferred_element_type=F32
    )
    partial, keys, ends_x, ends_bc = lax.optimization_barrier(
        (partial, key_heads, ssm_in[TOK - 16 :], bc[TOK - 16 :])
    )
    ends = jnp.concatenate([ends_x, ends_bc], axis=1)
    tail = lax.ppermute(ends, "ctx", [(i, i + 1) for i in range(31)])
    parts = lax.all_to_all(partial.reshape(8, HEADS, TOK), "head", 0, 0, tiled=True)
    xin, pair = convolved(ssm_in, tail, bc, conv_x, conv_bc.reshape(4, 2 * STATE))
    rows = jnp.concatenate([keys, value_heads], axis=1)
    up, down, two = along_z(rows, 1), along_z(rows, -1), along_z(rows, 2)
    parts, xin, pair = lax.optimization_barrier((parts, xin, pair))
    steps = jax.nn.softplus(jnp.sum(parts, axis=0) + dt_bias[:, None])
    drop = -steps * decay_rate[:, None]
    total = jnp.sum(drop, axis=1)
    cum, logs, read, keep, give = own_states(core, xin, pair, steps, drop)

    keep, give, up, down = lax.optimization_barrier((keep, give, up, down))
    other = swap_core(give)
    partner = jnp.sum(other[CHAN // 2, : 3 * HEADS].astype(F32).reshape(3, HEADS), axis=0)
    other = other[: CHAN // 2]
    by_half = lambda value: lax.dynamic_index_in_dim(value.reshape(2, 16), c, 0, False)
    shape = (16, PSIZE, STATE)
    log_first = by_half(jnp.where(c == 0, total, partner))
    log_second = by_half(jnp.where(c == 0, partner, total))
    early = jnp.where(c == 0, keep, other).reshape(shape).astype(F32)
    late = jnp.where(c == 0, other, keep).reshape(shape).astype(F32)
    both = with_logs(
        late + jnp.exp(log_second)[:, None, None] * early, log_first + log_second
    )
    collected = exchanged(both)
    both, xin, rows, up, down, two, query = lax.optimization_barrier(
        (both, xin, rows, up, down, two, query_heads)
    )
    visitor = send(query, lambda x, z, c: (x - 2, z, c) if x >= 2 else None)
    y = inside_blocks(xin, pair, cum, steps, read, jnp.repeat(skip_gain, PSIZE)[None])
    plane = jnp.stack([rows, up, down, two])
    plane_pair = swap_core(plane)
    left = along_x(plane, 1)
    right = send(plane, lambda x, z, c: (NX - 1, z, c) if x == 0 else None)
    seen = attend(flags(z + 1), query, plane, plane_pair, own=True)
    collected, y, seen = lax.optimization_barrier((collected, y, seen))
    carried = chain(collected)
    chip_in = exchanged(carried)
    planes_seen = jnp.where(x == 0, 0, jnp.where(x == NX - 1, 2, 1))
    carried, to_visit, to_see, visitor, left, right = lax.optimization_barrier(
        (carried, flags(jnp.where(x <= 1, 1, 0)), flags(planes_seen), visitor, left, right)
    )
    left_pair = swap_core(left)
    right_pair = swap_core(right)
    part = attend(to_visit, visitor, plane, plane_pair)
    part, to_see = lax.optimization_barrier((part, to_see))
    part = send(part, lambda x, z, c: (x + 2, z, c) if x <= 1 else None)
    seen = attend(to_see, query, left, left_pair, right, right_pair, carry=seen)
    chip_in, seen = lax.optimization_barrier((chip_in, seen))
    after = (early + jnp.exp(log_first)[:, None, None] * chip_in.astype(F32)).astype(BF)
    entering = jnp.where(c == 0, chip_in, after).reshape(CHAN // 2, STATE)
    sent = jnp.where(c == 0, after, chip_in).reshape(CHAN // 2, STATE)
    received = swap_core(sent)
    sent, seen = lax.optimization_barrier((sent, seen))
    attn_out = merge(flags(jnp.where(x >= 2, 1, 0)), seen, part)
    received, attn_out = lax.optimization_barrier((received, attn_out))
    mamba_out = finish(core, y, pair, logs, entering, received, gate_in, norm_gain[None])
    return (mamba_out, attn_out)


def solution(mesh):
    in_specs = (
        P("ctx", "head"),
        P("head", None),
        P("head"),
        P("head"),
        P("head"),
        P("ctx", "head"),
        P("ctx", "head", None),
        P(None, "head"),
        P(None, "head", None),
        P("ctx", "head"),
        P("head"),
        P("ctx", "head"),
        P("ctx", "head"),
        P("ctx", "head"),
    )
    out_specs = (P("ctx", "head"), P("ctx", "head"))
    return jax.shard_map(local, mesh=mesh, in_specs=in_specs, out_specs=out_specs, check_vma=False)
```
